32 devices in a mesh: pipe: 2 (over core), dp: 4 (over z), group: 4 (over y, x).
Axes of the slice: x: 2, y: 2, z: 4, core: 2. Of those that a mesh axis runs over, the one named last changes fastest.
Arguments:
- section_inputs: bfloat16 [2, 2, 16, 256, 768], P('pipe', None, ('dp', 'group')), may hold values from -6 to 6
- cotangent: bfloat16 [2, 16, 256, 768], P(None, ('dp', 'group')), may hold values from -6 to 6
- encoder_segments: int32 [2, 16, 256], P(None, ('dp', 'group')), may hold values from 0 to 3, never falling along the last dimension, each value on 1 to 160 neighbouring positions
- decoder_segments: int32 [2, 16, 256], P(None, ('dp', 'group')), may hold values from 0 to 3, never falling along the last dimension, each value on 1 to 160 neighbouring positions
- encoder_valid: int32 [2, 16, 256], P(None, ('dp', 'group')), may hold values 0 or 1
- decoder_valid: int32 [2, 16, 256], P(None, ('dp', 'group')), may hold values 0 or 1
- position_buckets: int32 [512], replicated, may hold values from 0 to 319
- encoder_gains: bfloat16 [2, 768], replicated, may hold values from 0.5 to 1.5
- encoder_shifts: bfloat16 [2, 768], replicated, may hold values from -1.25 to 1.25
- encoder_qkv: bfloat16 [768, 2304], replicated, may hold values from -0.21875 to 0.21875
- encoder_out: bfloat16 [768, 768], replicated, may hold values from -0.625 to 0.625
- encoder_up: bfloat16 [768, 3072], replicated, may hold values from -0.21875 to 0.21875
- encoder_down: bfloat16 [3072, 768], replicated, may hold values from -0.109375 to 0.109375
- position_table: bfloat16 [320, 12], replicated, may hold values from -6 to 6
- decoder_gains: bfloat16 [3, 768], replicated, may hold values from 0.5 to 1.5
- decoder_shifts: bfloat16 [3, 768], replicated, may hold values from -1.25 to 1.25
- decoder_qkv: bfloat16 [768, 2304], replicated, may hold values from -0.21875 to 0.21875
- decoder_out: bfloat16 [768, 768], replicated, may hold values from -0.625 to 0.625
- cross_query: bfloat16 [768, 768], replicated, may hold values from -0.21875 to 0.21875
- cross_keyvalue: bfloat16 [768, 1536], replicated, may hold values from -0.21875 to 0.21875
- cross_out: bfloat16 [768, 768], replicated, may hold values from -0.625 to 0.625
- decoder_up: bfloat16 [768, 3072], replicated, may hold values from -0.21875 to 0.21875
- decoder_down: bfloat16 [3072, 768], replicated, may hold values from -0.109375 to 0.109375
Outputs:
- section_outputs: bfloat16 [2, 2, 16, 256, 768], P('pipe', None, ('dp', 'group'))
- section_grads: bfloat16 [2, 2, 16, 256, 768], P('pipe', None, ('dp', 'group'))
- encoder_gains_grad: float32 [2, 768], P(None, ('pipe', 'dp'))
- encoder_shifts_grad: float32 [2, 768], P(None, ('pipe', 'dp'))
- encoder_qkv_grad: float32 [768, 2304], P(('pipe', 'dp'))
- encoder_out_grad: float32 [768, 768], P(('pipe', 'dp'))
- encoder_up_grad: float32 [768, 3072], P(('pipe', 'dp'))
- encoder_down_grad: float32 [3072, 768], P(('pipe', 'dp'))
- position_table_grad: float32 [320, 12], P(('pipe', 'dp'))
- decoder_gains_grad: float32 [3, 768], P(None, ('pipe', 'dp'))
- decoder_shifts_grad: float32 [3, 768], P(None, ('pipe', 'dp'))
- decoder_qkv_grad: float32 [768, 2304], P(('pipe', 'dp'))
- decoder_out_grad: float32 [768, 768], P(('pipe', 'dp'))
- cross_query_grad: float32 [768, 768], P(('pipe', 'dp'))
- cross_keyvalue_grad: float32 [768, 1536], P(('pipe', 'dp'))
- cross_out_grad: float32 [768, 768], P(('pipe', 'dp'))
- decoder_up_grad: float32 [768, 3072], P(('pipe', 'dp'))
- decoder_down_grad: float32 [3072, 768], P(('pipe', 'dp'))
The draws below stay inside these ranges and needn't reach their ends.
All inputs are finite; a program needn't handle non-finite values. No bound on the sum of `encoder_valid` or of `decoder_valid` on one device may be relied on, other than what follows from the above.
Results may differ from the reference program's by a relative error of at most 0.03.
Values may be sent and summed in bfloat16 or wider, within the bound.
A program may use at most 448 MiB of HBM per device.

```python
import math
import jax
import jax.numpy as jnp
import numpy as np
from jax import lax

HEADS = 12
FF = 3072
BUCKETS = 320
SEQ = 256
SEGS = 4
MICRO = 2
D = 768
ROWS_ALL = 16


def plant(drawn, key, low, top_value):
    spot = [jax.random.randint(jax.random.fold_in(key, axis), (), 0, length) for axis, length in enumerate(drawn.shape)]
    widest = drawn.shape.index(max(drawn.shape))
    neighbour = spot[:widest] + [(spot[widest] + 1) % drawn.shape[widest]] + spot[widest + 1:]
    return drawn.at[tuple(spot)].set(low).at[tuple(neighbour)].set(top_value)


def level_of(stream_key, dims, split, low, high):
    def one(position, parts):
        steps = jax.random.uniform(jax.random.fold_in(jax.random.fold_in(stream_key, 6), position), (parts,), jnp.float32, low / len(split), high / len(split))
        return jnp.repeat(jnp.exp(steps), dims[position] // parts).reshape((-1,) + (1,) * (len(dims) - position - 1))

    factor_of = one(*split[0])
    for cut in split[1:]:
        factor_of = factor_of * one(*cut)
    return factor_of


def split_up(count, total, reach, skew):
    loads = [(1 << 20) // math.isqrt(rank ** skew) + 1 for rank in range(2, count + 1)]
    rest, counts = total - reach - (count - 1), [1] * (count - 1)
    while rest > 0:
        movable = [i for i in range(count - 1) if counts[i] < reach]
        whole, budget = sum([loads[i] for i in movable]), rest
        for i in movable:
            more = min(reach - counts[i], max(1, budget * loads[i] // whole), rest)
            counts[i] = counts[i] + more
            rest = rest - more
    return np.array([reach] + counts)


def ragged(key, amount, total, most, skew):
    if amount == 2:
        one = jax.random.randint(key, (), max(1, total - most), min(most, total - 1) + 1)
        return jnp.stack([one, total - one])
    tallies = jnp.asarray(split_up(amount, total, most, skew), jnp.int32)
    couples = (amount - 1) // 2
    giver, taker = tallies[1:1 + 2 * couples:2], tallies[2:2 + 2 * couples:2]
    margin = jnp.minimum(giver - 1, most - taker)
    moved = jax.random.randint(jax.random.fold_in(key, 1), (couples,), 0, 1 << 20) % (margin + 1)
    tallies = tallies.at[1:1 + 2 * couples:2].set(giver - moved).at[2:2 + 2 * couples:2].set(taker + moved)
    return tallies[jax.random.permutation(jax.random.fold_in(key, 2), amount)]


def normal_values(own_key, shape, scale, most, split=(), dtype=jnp.bfloat16):
    level = level_of(own_key, shape, split, -0.22, 0.18) if split else 1.0
    entries = jax.random.normal(own_key, shape, jnp.float32) * scale * level
    return jnp.minimum(jnp.maximum(entries, -most), most).astype(dtype)


def setup_inputs(seed: int = 0) -> dict:
    keys = jax.random.split(jax.random.key(seed), 24)
    return {
        "section_inputs": normal_values(keys[0], (2, MICRO, ROWS_ALL, SEQ, D), 1.0, 6.0, ((0, 2), (2, 16))),
        "cotangent": normal_values(keys[1], (MICRO, ROWS_ALL, SEQ, D), 1.0, 6.0, ((1, 16),)),
        "encoder_segments": jax.vmap(lambda own: jnp.searchsorted(jnp.cumsum(ragged(own, SEGS, SEQ, SEQ // 2 + SEQ // 8, 0)), jnp.arange(SEQ), side="right"))(jax.random.split(keys[2], MICRO * ROWS_ALL)).reshape((MICRO, ROWS_ALL, SEQ)).astype(jnp.int32),
        "decoder_segments": jax.vmap(lambda own: jnp.searchsorted(jnp.cumsum(ragged(own, SEGS, SEQ, SEQ // 2 + SEQ // 8, 0)), jnp.arange(SEQ), side="right"))(jax.random.split(keys[3], MICRO * ROWS_ALL)).reshape((MICRO, ROWS_ALL, SEQ)).astype(jnp.int32),
        "encoder_valid": plant((jax.random.randint(keys[4], (MICRO, ROWS_ALL, SEQ), 0, 8) < 7).astype(jnp.int32), jax.random.fold_in(keys[4], 1), 0, 1),
        "decoder_valid": plant((jax.random.randint(keys[5], (MICRO, ROWS_ALL, SEQ), 0, 8) < 7).astype(jnp.int32), jax.random.fold_in(keys[5], 1), 0, 1),
        "position_buckets": plant(jax.random.randint(keys[6], (2 * SEQ,), 0, BUCKETS), jax.random.fold_in(keys[6], 1), 0, BUCKETS - 1).astype(jnp.int32),
        "encoder_gains": jnp.clip(1.0 + 0.1 * jax.random.normal(keys[7], (2, D), jnp.float32), 0.5, 1.5).astype(jnp.bfloat16),
        "encoder_shifts": normal_values(keys[8], (2, D), 0.2, 1.25),
        "encoder_qkv": normal_values(keys[9], (D, 3 * D), D ** -0.5, 0.21875),
        "encoder_out": normal_values(keys[10], (D, D), (D // 8) ** -0.5, 0.625),
        "encoder_up": normal_values(keys[11], (D, FF), D ** -0.5, 0.21875),
        "encoder_down": normal_values(keys[12], (FF, D), FF ** -0.5, 0.109375),
        "position_table": normal_values(keys[13], (BUCKETS, HEADS), 1.0, 6.0),
        "decoder_gains": jnp.clip(1.0 + 0.1 * jax.random.normal(keys[14], (3, D), jnp.float32), 0.5, 1.5).astype(jnp.bfloat16),
        "decoder_shifts": normal_values(keys[15], (3, D), 0.2, 1.25),
        "decoder_qkv": normal_values(keys[16], (D, 3 * D), D ** -0.5, 0.21875),
        "decoder_out": normal_values(keys[17], (D, D), (D // 8) ** -0.5, 0.625),
        "cross_query": normal_values(keys[18], (D, D), D ** -0.5, 0.21875),
        "cross_keyvalue": normal_values(keys[19], (D, 2 * D), D ** -0.5, 0.21875),
        "cross_out": normal_values(keys[20], (D, D), (D // 8) ** -0.5, 0.625),
        "decoder_up": normal_values(keys[21], (D, FF), D ** -0.5, 0.21875),
        "decoder_down": normal_values(keys[22], (FF, D), FF ** -0.5, 0.109375),
    }


NEGATIVE = -1e+30
HIGHEST = lax.Precision.HIGHEST

@jax.custom_vjp
def low(v):
    return lax.optimization_barrier(v.astype(jnp.bfloat16)).astype(jnp.float32)

@jax.custom_vjp
def low_back(v):
    return v

def low_keep(v):
    return (low(v), None)

def low_pass(kept, grad):
    return (grad,)

def back_keep(v):
    return (v, None)

def back_low(kept, grad):
    return (low(grad),)
low.defvjp(low_keep, low_pass)
low_back.defvjp(back_keep, back_low)

def layer_norm(values, gain_row, shift_row):
    centre = values - lax.optimization_barrier(jnp.mean(values, axis=-1, keepdims=True))
    spread = lax.optimization_barrier(jnp.mean(centre * centre, axis=-1, keepdims=True))
    return centre * lax.rsqrt(spread + 1e-05) * gain_row + shift_row

def product(left_side, right_side):
    return jnp.dot(left_side, right_side, precision=HIGHEST)

def split_heads(joined_part):
    return joined_part.reshape(joined_part.shape[0], joined_part.shape[1], HEADS, -1)

def self_allowed(segments, validity, causal):
    length = segments.shape[-1]
    query_pos = lax.broadcasted_iota(jnp.int32, (length, length), 0)
    key_pos = lax.broadcasted_iota(jnp.int32, (length, length), 1)
    same_segment = segments[:, :, None] == segments[:, None, :]
    allowed = same_segment & ((validity[:, None, :] == 1) | (query_pos == key_pos)[None])
    if causal:
        allowed = allowed & (key_pos <= query_pos)[None]
    return allowed

def cross_allowed(query_segments, key_segments, key_validity):
    first_frame = jnp.concatenate([jnp.ones((key_segments.shape[0], 1), jnp.bool_), key_segments[:, 1:] != key_segments[:, :-1]], axis=1)
    usable = (key_validity == 1) | first_frame
    return (query_segments[:, :, None] == key_segments[:, None, :]) & usable[:, None, :]

def expand_bias(bias_table, buckets, length):
    per_offset = jnp.take(bias_table, buckets, axis=0)
    offsets = lax.broadcasted_iota(jnp.int32, (length, length), 1) - lax.broadcasted_iota(jnp.int32, (length, length), 0) + length
    return jnp.transpose(jnp.take(per_offset, offsets, axis=0), (2, 0, 1))

def attention(queries, key_heads, value_heads, allowed, score_bias):
    score_scale = queries.shape[-1] ** (-0.5)
    scores = jnp.einsum('bqhe,bkhe->bhqk', queries, key_heads, precision=HIGHEST) * score_scale + score_bias
    scores = low_back(scores)
    scores = jnp.where(allowed[:, None], scores, NEGATIVE)
    largest = lax.optimization_barrier(jnp.max(scores, axis=-1, keepdims=True))
    log_total = largest + jnp.log(lax.optimization_barrier(jnp.sum(jnp.exp(scores - largest), axis=-1, keepdims=True)))
    weights = low(jnp.exp(scores - log_total))
    attended = jnp.einsum('bhqk,bkhe->bqhe', weights, value_heads, precision=HIGHEST)
    return attended.reshape(attended.shape[0], attended.shape[1], -1)

def self_branch(resid_in, gain_row, shift_row, w_qkv, w_out, allowed, score_bias):
    model_width = resid_in.shape[-1]
    normed = low(layer_norm(resid_in, gain_row, shift_row))
    joined = low_back(low(product(normed, w_qkv)))
    attended = attention(split_heads(joined[..., :model_width]), split_heads(joined[..., model_width:2 * model_width]), split_heads(joined[..., 2 * model_width:]), allowed, score_bias)
    attended = low_back(low(attended))
    return resid_in + low_back(product(attended, w_out))

def feed_forward(resid_in, gain_row, shift_row, w_up, w_down):
    normed = low(layer_norm(resid_in, gain_row, shift_row))
    hidden = low_back(product(normed, w_up))
    active = low(jax.nn.gelu(hidden, approximate=False))
    return resid_in + low_back(product(active, w_down))

def block(weight_set, buckets, encoder_rows, decoder_rows, encoder_segs, encoder_validity, decoder_segs, decoder_validity):
    enc_gain_rows, enc_shift_rows, enc_qkv, enc_out, enc_up, enc_down, bias_table, dec_gain_rows, dec_shift_rows, dec_qkv, dec_out, cross_q, cross_kv, cross_o, dec_up, dec_down = weight_set
    model_width = encoder_rows.shape[-1]
    length = encoder_rows.shape[1]
    score_bias = expand_bias(bias_table, buckets, length)
    after_attn = self_branch(encoder_rows, enc_gain_rows[0], enc_shift_rows[0], enc_qkv, enc_out, self_allowed(encoder_segs, encoder_validity, False), score_bias)
    encoded = feed_forward(after_attn, enc_gain_rows[1], enc_shift_rows[1], enc_up, enc_down)
    memory = low_back(low(encoded))
    after_self = self_branch(decoder_rows, dec_gain_rows[0], dec_shift_rows[0], dec_qkv, dec_out, self_allowed(decoder_segs, decoder_validity, True), 0.0)
    normed_cross = low(layer_norm(after_self, dec_gain_rows[1], dec_shift_rows[1]))
    cross_queries = low_back(low(product(normed_cross, cross_q)))
    cross_pairs = low_back(low(product(memory, cross_kv)))
    cross_att = attention(split_heads(cross_queries), split_heads(cross_pairs[..., :model_width]), split_heads(cross_pairs[..., model_width:]), cross_allowed(decoder_segs, encoder_segs, encoder_validity), 0.0)
    cross_att = low_back(low(cross_att))
    after_cross = after_self + low_back(product(cross_att, cross_o))
    decoded = feed_forward(after_cross, dec_gain_rows[2], dec_shift_rows[2], dec_up, dec_down)
    return (decoded, memory)

def reference(section_inputs, cotangent, encoder_segments, decoder_segments, encoder_valid, decoder_valid, position_buckets, encoder_gains, encoder_shifts, encoder_qkv, encoder_out, encoder_up, encoder_down, position_table, decoder_gains, decoder_shifts, decoder_qkv, decoder_out, cross_query, cross_keyvalue, cross_out, decoder_up, decoder_down):
    weight_set = tuple((weight.astype(jnp.float32) for weight in (encoder_gains, encoder_shifts, encoder_qkv, encoder_out, encoder_up, encoder_down, position_table, decoder_gains, decoder_shifts, decoder_qkv, decoder_out, cross_query, cross_keyvalue, cross_out, decoder_up, decoder_down)))
    micro_count, row_total, length, model_width = cotangent.shape
    block_rows = math.gcd(micro_count * row_total, 16)
    block_count = micro_count * row_total // block_rows

    def regroup(array):
        return array.reshape((block_count, block_rows) + array.shape[2:])
    masks = (regroup(encoder_segments), regroup(encoder_valid), regroup(decoder_segments), regroup(decoder_valid))

    def whole(encoder_all, decoder_all, weight_tuple):

        def one_block(carried, pieces):
            return (carried, jax.checkpoint(block)(weight_tuple, position_buckets, *pieces))
        unused, outputs = lax.scan(one_block, None, (encoder_all, decoder_all) + masks)
        return (outputs[0], outputs[1])
    encoder_all = regroup(section_inputs[0].astype(jnp.float32))
    decoder_all = regroup(section_inputs[1].astype(jnp.float32))
    decoded, back_fn, memory = jax.vjp(whole, encoder_all, decoder_all, weight_set, has_aux=True)
    encoder_grad, decoder_grad, weight_grads = back_fn(regroup(cotangent.astype(jnp.float32)))
    full_shape = (micro_count, row_total, length, model_width)
    section_outputs = jnp.stack([memory.reshape(full_shape), decoded.reshape(full_shape)]).astype(jnp.bfloat16)
    section_grads = jnp.stack([encoder_grad.reshape(full_shape), decoder_grad.reshape(full_shape)]).astype(jnp.bfloat16)
    return (section_outputs, section_grads, weight_grads[0], weight_grads[1], weight_grads[2], weight_grads[3], weight_grads[4], weight_grads[5], weight_grads[6], weight_grads[7], weight_grads[8], weight_grads[9], weight_grads[10], weight_grads[11], weight_grads[12], weight_grads[13], weight_grads[14], weight_grads[15])
```

```python
import functools
from types import SimpleNamespace

import jax
import jax.numpy as jnp
from jax import lax
from jax.experimental import pallas as pl
from jax.experimental.pallas import tpu as pltpu
from jax.sharding import PartitionSpec as P

HEADS = 12
NEGATIVE = -1e30
BF, F32 = jnp.bfloat16, jnp.float32
GAIN_ROWS = 16


def dot(a, b):
    return jnp.dot(a, b, preferred_element_type=F32)


def dot_nt(a, b):
    return lax.dot_general(a, b, (((1,), (1,)), ((), ())), preferred_element_type=F32)


def dot_tn(a, b):
    return lax.dot_general(a, b, (((0,), (0,)), ((), ())), preferred_element_type=F32)


def row_loop(rows, chunk, body):
    def step(i, carry):
        body(pl.ds(pl.multiple_of(i * chunk, chunk), chunk))
        return carry

    lax.fori_loop(0, rows // chunk, step, 0)


def norm_stats(x):
    centre = x - jnp.mean(x, axis=-1, keepdims=True)
    spread = jnp.mean(centre * centre, axis=-1, keepdims=True)
    return centre, lax.rsqrt(spread + 1e-05)


def norm_forward(x_ref, gain, shift, n_ref):
    def body(rows):
        centre, inv = norm_stats(x_ref[rows, :].astype(F32))
        n_ref[rows, :] = (centre * inv * gain + shift).astype(BF)

    row_loop(x_ref.shape[0], 64, body)


def norm_backward(x_ref, gain, dn_ref, stream_ref, sums_ref, gain_at, shift_at):
    width = x_ref.shape[1]

    def step(i, carry):
        dgain, dshift = carry
        rows = pl.ds(pl.multiple_of(i * 64, 64), 64)
        centre, inv = norm_stats(x_ref[rows, :].astype(F32))
        hat = centre * inv
        dn = dn_ref[rows, :]
        dhat = dn * gain
        mean_one = jnp.mean(dhat, axis=-1, keepdims=True)
        mean_two = jnp.mean(dhat * hat, axis=-1, keepdims=True)
        stream_ref[rows, :] += inv * (dhat - mean_one - hat * mean_two)
        return (
            dgain + jnp.sum(dn * hat, axis=0, keepdims=True),
            dshift + jnp.sum(dn, axis=0, keepdims=True),
        )

    zero = jnp.zeros((1, width), F32)
    dgain, dshift = lax.fori_loop(0, x_ref.shape[0] // 64, step, (zero, zero))
    sums_ref[gain_at : gain_at + 1, :] = dgain
    sums_ref[shift_at : shift_at + 1, :] = dshift


def project(a_ref, w_ref, out_ref, tile=256):
    for start in range(0, w_ref.shape[1], tile):
        cols = slice(start, start + tile)
        out_ref[:, cols] = dot(a_ref[...], w_ref[:, cols]).astype(out_ref.dtype)


def project_add(a_ref, w_ref, resid_ref, out_ref, tile=256):
    for start in range(0, w_ref.shape[1], tile):
        cols = slice(start, start + tile)
        out_ref[:, cols] = (
            resid_ref[:, cols].astype(F32) + dot(a_ref[...], w_ref[:, cols])
        ).astype(out_ref.dtype)


def project_back(g_ref, w_ref, out_ref, tile=256):
    for start in range(0, w_ref.shape[0], tile):
        cols = slice(start, start + tile)
        out_ref[:, cols] = dot_nt(g_ref[...], w_ref[cols, :]).astype(out_ref.dtype)


def feed_up(n_ref, w_ref, z_ref, slope_ref, tile=512):
    for start in range(0, w_ref.shape[1], tile):
        cols = slice(start, start + tile)
        u = dot(n_ref[...], w_ref[:, cols])
        cdf = 0.5 * (1.0 + lax.erf(u * 0.7071067811865476))
        z_ref[:, cols] = (u * cdf).astype(BF)
        slope_ref[:, cols] = (cdf + u * (0.3989422804014327 * jnp.exp(-0.5 * u * u))).astype(BF)


def feed_down_back(g_ref, w_ref, slope_ref, tile=512):
    for start in range(0, w_ref.shape[0], tile):
        cols = slice(start, start + tile)
        grad = dot_nt(g_ref[...], w_ref[cols, :])
        slope_ref[:, cols] = (grad * slope_ref[:, cols].astype(F32)).astype(BF)


def attend(q_ref, q_at, k_ref, k_at, v_ref, v_at, mask_ref, p_ref, o_ref, bias_ref=None):
    length = q_ref.shape[0]
    head = o_ref.shape[1] // HEADS
    pair = 2 * head
    scale = head**-0.5

    def step(i, carry):
        def cols(at):
            return pl.ds(pl.multiple_of(at + i * pair, pair), pair)

        low_half = lax.broadcasted_iota(jnp.int32, (length, pair), 1) < head
        q = q_ref[:, cols(q_at)] * jnp.asarray(scale, BF)
        k = k_ref[:, cols(k_at)]
        v = v_ref[:, cols(v_at)]
        outs = []
        for half in range(2):
            own = low_half if half == 0 else jnp.logical_not(low_half)
            s = dot_nt(jnp.where(own, q, jnp.zeros_like(q)), k) + mask_ref[...]
            if bias_ref is not None:
                wide = jnp.broadcast_to(
                    bias_ref[pl.ds(2 * i + half, 1), :], (length, 2 * length)
                )
                s = s + pltpu.roll(wide, length, 1, stride=1, stride_axis=0)[:, :length]
            e = jnp.exp(s - jnp.max(s, axis=-1, keepdims=True))
            p = (e * (1.0 / jnp.sum(e, axis=-1, keepdims=True))).astype(BF)
            p_ref[2 * i + half] = p
            outs.append(dot(p, v))
        o_ref[:, cols(0)] = jnp.where(low_half, outs[0], outs[1]).astype(BF)
        return carry

    lax.fori_loop(0, HEADS // 2, step, 0)


def attend_back(q_ref, q_at, k_ref, k_at, v_ref, v_at, p_ref, do_ref, diag_ref=None, flip_ref=None):
    length = q_ref.shape[0]
    head = do_ref.shape[1] // HEADS
    pair = 2 * head
    scale = head**-0.5

    def step(i, carry):
        def cols(at):
            return pl.ds(pl.multiple_of(at + i * pair, pair), pair)

        low_half = lax.broadcasted_iota(jnp.int32, (length, pair), 1) < head
        q = q_ref[:, cols(q_at)]
        k = k_ref[:, cols(k_at)]
        v = v_ref[:, cols(v_at)]
        do = do_ref[:, cols(0)]
        dqs, dks, dvs = [], [], []
        for half in range(2):
            own = low_half if half == 0 else jnp.logical_not(low_half)
            p = p_ref[2 * i + half]
            dp = dot_nt(jnp.where(own, do, jnp.zeros_like(do)), v)
            wide_p = p.astype(F32)
            row = jnp.sum(wide_p * dp, axis=-1, keepdims=True)
            ds = (wide_p * (dp - row)).astype(BF)
            dvs.append(dot_tn(p, do))
            dqs.append(dot(ds, k))
            dks.append(dot_tn(ds, q))
            if diag_ref is not None:
                flipped = dot(flip_ref[...], ds)
                wide = jnp.concatenate([flipped, jnp.zeros_like(flipped)], axis=1)
                rolled = pltpu.roll(wide, 1, 1, stride=1, stride_axis=0)
                diag_ref[pl.ds(2 * i + half, 1), :] = jnp.sum(rolled, axis=0, keepdims=True)
        q_ref[:, cols(q_at)] = (jnp.where(low_half, dqs[0], dqs[1]) * scale).astype(BF)
        k_ref[:, cols(k_at)] = (jnp.where(low_half, dks[0], dks[1]) * scale).astype(BF)
        v_ref[:, cols(v_at)] = jnp.where(low_half, dvs[0], dvs[1]).astype(BF)
        return carry

    lax.fori_loop(0, HEADS // 2, step, 0)


def build_masks(eseg, dseg, evalid, dvalid, enc_ref, dec_ref, cross_ref):
    length = enc_ref.shape[0]
    shape = (length, length)
    key = lax.broadcasted_iota(jnp.int32, shape, 1)
    query = lax.broadcasted_iota(jnp.int32, shape, 0)
    eseg_key = jnp.broadcast_to(eseg.astype(F32), shape)
    dseg_key = jnp.broadcast_to(dseg.astype(F32), shape)
    eseg_query, dseg_query = eseg_key.T, dseg_key.T
    evalid_key = jnp.broadcast_to(evalid, shape) == 1
    dvalid_key = jnp.broadcast_to(dvalid, shape) == 1
    before = pltpu.roll(eseg_key, 1, 1)
    first = (key == 0) | (eseg_key != before)
    enc = (eseg_query == eseg_key) & (evalid_key | (key == query))
    dec = (dseg_query == dseg_key) & (dvalid_key | (key == query)) & (key <= query)
    cross = (dseg_query == eseg_key) & (evalid_key | first)
    enc_ref[...] = jnp.where(enc, 0.0, NEGATIVE)
    dec_ref[...] = jnp.where(dec, 0.0, NEGATIVE)
    cross_ref[...] = jnp.where(cross, 0.0, NEGATIVE)


def bucket_onehot(buckets, bucket_count):
    shape = (bucket_count, buckets.shape[1])
    return jnp.broadcast_to(buckets, shape) == lax.broadcasted_iota(jnp.int32, shape, 0)


def layers_kernel(blocks, groups, *refs):
    spaces = []
    for names in groups:
        spaces.append(SimpleNamespace(**dict(zip(names, refs))))
        refs = refs[len(names) :]
    hbm, small_in, out, v, s = spaces
    pipe = lax.axis_index("pipe")
    length, width = hbm.x_enc.shape
    started, pending = [], []

    def load(source, target):
        copy = pltpu.make_async_copy(source, target, s.sem_in.at[len(started)])
        copy.start()
        started.append(copy)
        return copy

    def store(source, target):
        copy = pltpu.make_async_copy(source, target, s.sem_out.at[len(pending)])
        copy.start()
        pending.append(copy)

    get_x_enc = load(hbm.x_enc, v.x_enc)
    get_e_qkv = load(hbm.e_qkv, s.e_qkv)
    get_e_out = load(hbm.e_out, s.e_out)
    get_e_up = load(hbm.e_up, s.up)
    get_e_down = load(hbm.e_down, s.down)
    get_x_dec = load(hbm.x_dec, v.x_dec)
    get_d_qkv = load(hbm.d_qkv, s.d_qkv)
    get_d_out = load(hbm.d_out, s.d_out)
    get_c_query = load(hbm.c_query, s.c_query)
    get_c_kv = load(hbm.c_kv, s.c_kv)
    get_c_out = load(hbm.c_out, s.c_out)
    get_cot = load(hbm.cot.at[pipe, 0], v.cot)

    own = pl.ds(pipe, 1)
    build_masks(
        small_in.enc_seg[own, :], small_in.dec_seg[own, :], small_in.enc_valid[own, :],
        small_in.dec_valid[own, :], s.mask_enc, s.mask_dec, s.mask_cross,
    )
    buckets = small_in.buckets[...]
    bucket_count = small_in.table.shape[0]
    s.bias[0:HEADS, :] = dot_tn(small_in.table[...], bucket_onehot(buckets, bucket_count).astype(BF))
    flip_shape = (length, length)
    s.flip[...] = (
        lax.broadcasted_iota(jnp.int32, flip_shape, 0) + lax.broadcasted_iota(jnp.int32, flip_shape, 1)
        == length - 1
    ).astype(BF)

    def at(ref, row):
        return ref[row : row + 1, :].astype(F32)

    enc_gains, enc_shifts = small_in.enc_gains, small_in.enc_shifts
    dec_gains, dec_shifts = small_in.dec_gains, small_in.dec_shifts

    get_x_enc.wait()
    norm_forward(v.x_enc, at(enc_gains, 0), at(enc_shifts, 0), v.xe_qkv)
    store(v.xe_qkv, out.xe_qkv)
    get_e_qkv.wait()
    project(v.xe_qkv, s.e_qkv, v.ge_qkv)
    attend(v.ge_qkv, 0, v.ge_qkv, width, v.ge_qkv, 2 * width, s.mask_enc, s.p_enc, v.xe_out, s.bias)
    store(v.xe_out, out.xe_out)
    get_e_out.wait()
    project_add(v.xe_out, s.e_out, v.x_enc, s.x1)
    norm_forward(s.x1, at(enc_gains, 1), at(enc_shifts, 1), v.xe_up)
    store(v.xe_up, out.xe_up)
    get_e_up.wait()
    feed_up(v.xe_up, s.up, v.xe_down, v.ge_up)
    get_d_up = load(hbm.d_up, s.up)
    store(v.xe_down, out.xe_down)
    get_e_down.wait()
    project_add(v.xe_down, s.down, s.x1, v.memory)
    get_d_down = load(hbm.d_down, s.down)
    store(v.memory, out.memory)

    get_x_dec.wait()
    norm_forward(v.x_dec, at(dec_gains, 0), at(dec_shifts, 0), v.xd_qkv)
    store(v.xd_qkv, out.xd_qkv)
    get_d_qkv.wait()
    project(v.xd_qkv, s.d_qkv, v.gd_qkv)
    attend(v.gd_qkv, 0, v.gd_qkv, width, v.gd_qkv, 2 * width, s.mask_dec, s.p_dec, v.xd_out)
    store(v.xd_out, out.xd_out)
    get_d_out.wait()
    project_add(v.xd_out, s.d_out, v.x_dec, s.d1)
    norm_forward(s.d1, at(dec_gains, 1), at(dec_shifts, 1), v.xc_query)
    store(v.xc_query, out.xc_query)
    get_c_query.wait()
    project(v.xc_query, s.c_query, v.gc_query)
    get_c_kv.wait()
    project(v.memory, s.c_kv, v.gc_kv)
    attend(v.gc_query, 0, v.gc_kv, 0, v.gc_kv, width, s.mask_cross, s.p_cross, v.xc_out)
    store(v.xc_out, out.xc_out)
    get_c_out.wait()
    project_add(v.xc_out, s.c_out, s.d1, s.d2)
    norm_forward(s.d2, at(dec_gains, 2), at(dec_shifts, 2), v.xd_up)
    store(v.xd_up, out.xd_up)
    get_d_up.wait()
    feed_up(v.xd_up, s.up, v.xd_down, v.gd_up)
    store(v.xd_down, out.xd_down)
    get_d_down.wait()
    project_add(v.xd_down, s.down, s.d2, v.decoded)
    store(v.decoded, out.decoded)

    stream, sums = s.stream, s.sums
    get_cot.wait()
    stream[...] = v.cot[...].astype(F32)
    feed_down_back(v.cot, s.down, v.gd_up)
    get_e_down = load(hbm.e_down, s.down)
    store(v.gd_up, out.gd_up)
    project_back(v.gd_up, s.up, s.dn)
    get_e_up = load(hbm.e_up, s.up)
    norm_backward(s.d2, at(dec_gains, 2), s.dn, stream, sums, 6, 9)
    v.gc_out[...] = stream[...].astype(BF)
    store(v.gc_out, out.gc_out)
    project_back(v.gc_out, s.c_out, s.do)
    attend_back(v.gc_query, 0, v.gc_kv, 0, v.gc_kv, width, s.p_cross, s.do)
    store(v.gc_kv, out.gc_kv)
    store(v.gc_query, out.gc_query)
    project_back(v.gc_kv, s.c_kv, v.ge_down)
    store(v.ge_down, out.ge_down)
    project_back(v.gc_query, s.c_query, s.dn)
    norm_backward(s.d1, at(dec_gains, 1), s.dn, stream, sums, 5, 8)
    v.gd_out[...] = stream[...].astype(BF)
    store(v.gd_out, out.gd_out)
    project_back(v.gd_out, s.d_out, s.do)
    attend_back(v.gd_qkv, 0, v.gd_qkv, width, v.gd_qkv, 2 * width, s.p_dec, s.do)
    store(v.gd_qkv, out.gd_qkv)
    project_back(v.gd_qkv, s.d_qkv, s.dn)
    norm_backward(v.x_dec, at(dec_gains, 0), s.dn, stream, sums, 4, 7)
    v.dx_dec[...] = stream[...].astype(BF)
    store(v.dx_dec, out.dx_dec)

    stream[...] = v.ge_down[...].astype(F32)
    get_e_down.wait()
    feed_down_back(v.ge_down, s.down, v.ge_up)
    store(v.ge_up, out.ge_up)
    get_e_up.wait()
    project_back(v.ge_up, s.up, s.dn)
    norm_backward(s.x1, at(enc_gains, 1), s.dn, stream, sums, 1, 3)
    v.ge_out[...] = stream[...].astype(BF)
    store(v.ge_out, out.ge_out)
    project_back(v.ge_out, s.e_out, s.do)
    s.diag[...] = jnp.zeros_like(s.diag)
    attend_back(
        v.ge_qkv, 0, v.ge_qkv, width, v.ge_qkv, 2 * width, s.p_enc, s.do, s.diag, s.flip
    )
    store(v.ge_qkv, out.ge_qkv)
    project_back(v.ge_qkv, s.e_qkv, s.dn)
    norm_backward(v.x_enc, at(enc_gains, 0), s.dn, stream, sums, 0, 2)
    v.dx_enc[...] = stream[...].astype(BF)
    store(v.dx_enc, out.dx_enc)

    onehot = bucket_onehot(buckets, bucket_count).astype(BF)
    rest = s.diag[...]
    table_grad = jnp.zeros((bucket_count, rest.shape[0]), F32)
    for unused in range(3):
        part = rest.astype(BF)
        rest = rest - part.astype(F32)
        table_grad = table_grad + dot_nt(onehot, part)
    small = out.small
    small[...] = jnp.zeros_like(small)
    lanes = width // blocks
    table_rows = bucket_count // blocks
    for block in range(blocks):
        small[block, 0:GAIN_ROWS, 0:lanes] = sums[:, block * lanes : (block + 1) * lanes]
        small[block, GAIN_ROWS : GAIN_ROWS + table_rows, 0 : rest.shape[0]] = table_grad[
            block * table_rows : (block + 1) * table_rows, :
        ]
    for copy in pending:
        copy.wait()


def run_layers(blocks, inputs, small_in, weights):
    length, width = inputs["x_enc"].shape
    hidden = weights["e_up"].shape[1]
    hbm = dict(inputs, **weights)
    any_spec = pl.BlockSpec(memory_space=pl.ANY)
    vmem_spec = pl.BlockSpec(memory_space=pltpu.VMEM)
    columns = dict(
        xe_qkv=width, xe_out=width, xe_up=width, xe_down=hidden, memory=width,
        xd_qkv=width, xd_out=width, xc_query=width, xc_out=width, xd_up=width, xd_down=hidden,
        ge_qkv=3 * width, ge_out=width, ge_up=hidden, ge_down=width,
        gd_qkv=3 * width, gd_out=width, gc_query=width, gc_kv=2 * width, gc_out=width,
        gd_up=hidden, decoded=width, dx_enc=width, dx_dec=width,
    )
    table_rows = small_in["table"].shape[0] // blocks
    small_rows = -(-(GAIN_ROWS + table_rows) // 16) * 16
    outs = {name: jax.ShapeDtypeStruct((length, n), BF) for name, n in columns.items()}
    outs["small"] = jax.ShapeDtypeStruct((blocks, small_rows, 128), F32)
    held = {name: pltpu.VMEM((length, n), BF) for name, n in columns.items()}
    held.update({name: pltpu.VMEM((length, width), BF) for name in inputs})
    probabilities = pltpu.VMEM((HEADS, length, length), BF)
    square = pltpu.VMEM((length, length), F32)
    rows = pltpu.VMEM((length, width), F32)
    per_offset = pltpu.VMEM((16, 2 * length), F32)
    scratch = {
        name: pltpu.VMEM(w.shape, BF) for name, w in weights.items() if hidden not in w.shape
    }
    scratch.update(
        up=pltpu.VMEM((width, hidden), BF), down=pltpu.VMEM((hidden, width), BF),
        p_enc=probabilities, p_dec=probabilities, p_cross=probabilities,
        mask_enc=square, mask_dec=square, mask_cross=square,
        x1=rows, d1=rows, d2=rows, stream=rows, dn=rows,
        do=pltpu.VMEM((length, width), BF), flip=pltpu.VMEM((length, length), BF),
        bias=per_offset, diag=per_offset, sums=pltpu.VMEM((GAIN_ROWS, width), F32),
        sem_in=pltpu.SemaphoreType.DMA((24,)), sem_out=pltpu.SemaphoreType.DMA((len(columns),)),
    )
    groups = [list(part) for part in (hbm, small_in, outs, held, scratch)]
    results = pl.pallas_call(
        functools.partial(layers_kernel, blocks, groups),
        out_shape=list(outs.values()),
        in_specs=[any_spec] * len(hbm) + [vmem_spec] * len(small_in),
        out_specs=[any_spec] * len(columns) + [vmem_spec],
        scratch_shapes=list(held.values()) + list(scratch.values()),
        compiler_params=pltpu.CompilerParams(vmem_limit_bytes=63 * 1024 * 1024),
        name="layers",
    )(*hbm.values(), *small_in.values())
    return dict(zip(outs, results))


MESH = pl.DeviceIdType.MESH


def step_order(units, hops, rests, window=6):
    big, small, delay = 6.6, 1.7, 2.0
    axis_free, z_free, clock = [0.0, 0.0], 0.0, 0.0
    arrived, steps = [], []
    for unit in range(units):
        clock = max(clock + 1.0, arrived[unit - window] if unit >= window else 0.0)
        steps.append((clock, 0, unit, 0))
        axis_free[unit % 2] = max(axis_free[unit % 2], clock) + big
        now = axis_free[unit % 2] + delay
        arrived.append(now)
        steps.append((now, 1, unit, 0))
        z_free = max(z_free, now) + 3 * small
        now = z_free + delay
        for hop in range(1, hops):
            steps.append((now, 2, unit, hop))
            now += delay + small * max(1, 3 - hop)
        steps.append((now, 3, unit, 0))
        for rest in range(rests):
            now += delay + small
            steps.append((now, 4, unit, rest))
        now += delay + small
        steps.append((now, 5, unit, 0))
    return [step[1:] for step in sorted(steps)]


def grads_kernel(micro_rows, tables, groups, *refs):
    spaces = []
    for names in groups:
        if isinstance(names, int):
            spaces.append(refs[:names])
            refs = refs[names:]
        else:
            spaces.append(SimpleNamespace(**dict(zip(names, refs))))
            refs = refs[len(names) :]
    xs, gs, hbm, grads, out, land_x, land_g, s = spaces
    n, bits, first_units, unit_weight = tables
    p, d, g = lax.axis_index("pipe"), lax.axis_index("dp"), lax.axis_index("group")
    units = len(unit_weight)
    length, width = xs[1].shape
    half = width // 2
    block = width // (2 * n)

    def bit_of(bit):
        return (g // 2**bit) % 2

    def across(bit):
        return (p, d, g + (1 - 2 * bit_of(bit)) * 2**bit)

    core = (1 - p, d, g)
    above, below = (p, d + 1, g), (p, d - 1, g)

    barrier = pltpu.get_barrier_semaphore()
    pl.semaphore_signal(barrier, inc=1, device_id=core, device_id_type=MESH)
    for bit in range(bits):
        pl.semaphore_signal(barrier, inc=1, device_id=across(bit), device_id_type=MESH)

    @pl.when(d > 0)
    def _():
        pl.semaphore_signal(barrier, inc=1, device_id=below, device_id_type=MESH)

    @pl.when(d < n - 1)
    def _():
        pl.semaphore_signal(barrier, inc=1, device_id=above, device_id_type=MESH)

    @pl.when((d > 0) & (d < n - 1))
    def _():
        pl.semaphore_wait(barrier, 3 + bits)

    @pl.when((d == 0) | (d == n - 1))
    def _():
        pl.semaphore_wait(barrier, 2 + bits)

    def remote(source, target, send_sem, recv_sem, device):
        return pltpu.make_async_remote_copy(
            src_ref=source, dst_ref=target, send_sem=send_sem, recv_sem=recv_sem,
            device_id=device, device_id_type=MESH,
        )

    sent = []

    def send(copy):
        copy.start()
        sent.append(copy.wait_send)
        return copy

    swaps = []
    for at in range(len(xs)):
        part = xs[at].shape[1] // 2
        theirs = pl.ds(pl.multiple_of((1 - p) * part, 128), part)
        copies = [
            send(remote(xs[at].at[:, theirs], land_x[at], s.swap_sent.at[2 * at], s.swap_got.at[2 * at], core))
        ]
        if at > 0:
            copies.append(
                send(remote(gs[at], land_g[at - 1], s.swap_sent.at[2 * at + 1], s.swap_got.at[2 * at + 1], core))
            )
        swaps.append(copies)

    small_swap = send(
        remote(hbm.small.at[pl.ds((1 - p) * n, n)], s.small_core, s.small_sent.at[0], s.small_got.at[0], core)
    )
    small_own = pltpu.make_async_copy(hbm.small.at[pl.ds(p * n, n)], s.small_kept, s.small_load)
    small_own.start()

    section_copies = []
    for at, (enc, dec, target) in enumerate(
        ((hbm.memory, hbm.decoded, out.outputs), (hbm.dx_enc, hbm.dx_dec, out.input_grads))
    ):
        for layer, keep, give in ((0, enc, dec), (1, dec, enc)):

            @pl.when(p == layer)
            def _(at=at, keep=keep, give=give, target=target):
                pltpu.make_async_copy(keep, target.at[0, p, 0], s.section_kept.at[at]).start()
                remote(give, target.at[0, p, 0], s.section_sent.at[at], s.section_got.at[at], core).start()

        section_copies.append(
            (
                pltpu.make_async_copy(enc, target.at[0, p, 0], s.section_kept.at[at]),
                remote(enc, target.at[0, 1 - p, 0], s.section_sent.at[at], s.section_got.at[at], core),
            )
        )

    def tiles_of(at):
        return xs[at].shape[1] // width

    def load_own(at):
        slot = at % 2
        copies = []
        part = xs[at].shape[1] // 2
        for tile in range(tiles_of(at)):
            mine = pl.ds(pl.multiple_of(p * part + tile * half, 128), half)
            copies.append(
                pltpu.make_async_copy(
                    xs[at].at[:, mine], s.x_stage.at[slot, tile, 0:length], s.loads.at[slot, 0, tile]
                )
            )
        source = gs[at].at[p, 0] if at == 0 else gs[at]
        columns = source.shape[1]
        copies.append(
            pltpu.make_async_copy(
                source, s.g_stage.at[slot, 0:length, 0:columns], s.loads.at[slot, 0, 4]
            )
        )
        for copy in copies:
            copy.start()
        return copies

    def load_landed(at):
        slot = at % 2
        for copy in swaps[at]:
            copy.wait_recv()
        copies = []
        for tile in range(tiles_of(at)):
            copies.append(
                pltpu.make_async_copy(
                    land_x[at].at[:, tile * half : (tile + 1) * half],
                    s.x_stage.at[slot, tile, length : 2 * length],
                    s.loads.at[slot, 1, tile],
                )
            )
        source = gs[at].at[1 - p, 0] if at == 0 else land_g[at - 1]
        columns = source.shape[1]
        copies.append(
            pltpu.make_async_copy(
                source, s.g_stage.at[slot, length : 2 * length, 0:columns], s.loads.at[slot, 1, 4]
            )
        )
        for copy in copies:
            copy.start()
        return copies

    own_loads = {0: load_own(0)}

    def first_bit(unit):
        return 0 if unit % 2 == 0 else bits - 1

    def first_copy(unit):
        return remote(
            s.given.at[unit], s.taken.at[unit], s.first_sent.at[unit], s.first_got.at[unit], across(first_bit(unit))
        )

    def product(unit, factor, slot, column, rows):
        mine = bit_of(first_bit(unit))
        for keep, which, target in ((0, 1 - mine, s.given), (1, mine, s.kept)):
            cols = pl.ds(pl.multiple_of(column * width + which * half, 128), half)
            value = dot(factor, s.g_stage[slot, :, cols]).astype(BF)
            for at, row in rows:
                target[unit, at] = value[row : row + block]

    def make(unit):
        at = unit_weight[unit]
        slot = at % 2
        base = first_units[at]
        tiles = tiles_of(at)
        if unit == base:
            copies = own_loads.pop(at) + load_landed(at)
            if at + 1 < len(xs):
                own_loads[at + 1] = load_own(at + 1)
            for copy in copies:
                copy.wait()
            for tile in range(tiles):
                s.factor[tile] = s.x_stage[slot, tile].T
        if tiles == 1:
            product(unit, s.factor[0], slot, unit - base, [(i, i * block) for i in range(n)])
        elif unit == base:
            for tile in range(tiles):
                split_product(base, tiles, tile, slot)
        first_copy(unit).start()

    def split_product(base, tiles, tile, slot):
        for which in range(2):
            value = dot(s.factor[tile], s.g_stage[slot, :, which * half : (which + 1) * half]).astype(BF)
            for i in range(n):
                unit = base + (tile * n + i) % tiles
                at = (tile * n + i) // tiles
                mine = bit_of(first_bit(unit))
                rows = value[i * block : (i + 1) * block]

                @pl.when(mine == which)
                def _(unit=unit, at=at, rows=rows):
                    s.kept[unit, at] = rows

                @pl.when(mine != which)
                def _(unit=unit, at=at, rows=rows):
                    s.given[unit, at] = rows

    def add(target, index, source, source_index):
        target[index] = (target[index].astype(F32) + source[source_index].astype(F32)).astype(target.dtype)

    def up_copy(line, dd):
        source = line.kept.at[1:n] if dd == 0 else line.passed.at[dd + 2 : n + 1]
        return remote(source, line.passed.at[dd + 2 : n + 1], line.sems.at[0], line.sems.at[1], above)

    def down_copy(line, dd):
        source = line.kept.at[0 : n - 1] if dd == n - 1 else line.passed.at[0:dd]
        return remote(source, line.passed.at[0:dd], line.sems.at[2], line.sems.at[3], below)

    def line_start(line):
        @pl.when(d == 0)
        def _():
            up_copy(line, 0).start()

        @pl.when(d == n - 1)
        def _():
            down_copy(line, n - 1).start()

    def line_hop(line, hop):
        @pl.when(d == hop)
        def _():
            up_copy(line, hop - 1).wait_recv()
            for i in range(hop + 1, n):
                add(line.passed, i + 1, line.kept, i)
            up_copy(line, hop).start()

        @pl.when(d == n - 1 - hop)
        def _():
            down_copy(line, n - hop).wait_recv()
            for i in range(n - 1 - hop):
                add(line.passed, i, line.kept, i)
            down_copy(line, n - 1 - hop).start()

    def line_end(line):
        @pl.when(d == n - 1)
        def _():
            up_copy(line, n - 2).wait_recv()
            line.kept[n - 1] = (
                line.kept[n - 1].astype(F32) + line.passed[n].astype(F32)
            ).astype(line.kept.dtype)

        @pl.when(d == 0)
        def _():
            down_copy(line, 1).wait_recv()
            line.kept[0] = (line.kept[0].astype(F32) + line.passed[0].astype(F32)).astype(line.kept.dtype)

        for dd in range(1, n - 1):

            @pl.when(d == dd)
            def _(dd=dd):
                line.kept[dd] = (
                    line.kept[dd].astype(F32) + line.passed[dd + 1].astype(F32) + line.passed[dd].astype(F32)
                ).astype(line.kept.dtype)

    def line_sent(line):
        for dd in range(n):

            @pl.when(d == dd)
            def _(dd=dd):
                if dd < n - 1:
                    up_copy(line, dd).wait_send()
                if dd > 0:
                    down_copy(line, dd).wait_send()

    def line_of(unit):
        return SimpleNamespace(
            kept=s.kept.at[unit], passed=s.passed.at[unit], sems=s.line_sems.at[unit]
        )

    def rest_bits(unit):
        return [bit for bit in range(bits) if bit != first_bit(unit)]

    def rest_copy(unit, at):
        source = s.kept.at[unit, d] if at == 0 else s.rest_sum.at[unit, at - 1]
        return remote(
            source, s.rest_got.at[unit, at], s.rest_sems.at[unit, at, 0], s.rest_sems.at[unit, at, 1],
            across(rest_bits(unit)[at]),
        )

    def last_copy(unit):
        return remote(
            s.rest_sum.at[unit, bits - 2], s.last_got.at[unit], s.last_sems.at[unit, 0], s.last_sems.at[unit, 1],
            across(first_bit(unit)),
        )

    def result_at(unit, which):
        at = unit_weight[unit]
        k = unit - first_units[at]
        target = grads[at]
        if tiles_of(at) == 1:
            return target.at[:, pl.ds(pl.multiple_of(k * width + which * half, 128), half)]
        return target.at[pl.ds(k * block, block), pl.ds(pl.multiple_of(which * half, 128), half)]

    def own_result(unit):
        return pltpu.make_async_copy(
            s.rest_sum.at[unit, bits - 2], result_at(unit, bit_of(first_bit(unit))), s.result_sems.at[unit, 0]
        )

    def got_result(unit):
        return pltpu.make_async_copy(
            s.last_got.at[unit], result_at(unit, 1 - bit_of(first_bit(unit))), s.result_sems.at[unit, 1]
        )

    def take_step(kind, unit, at):
        if kind == 0:
            make(unit)
        elif kind == 1:
            first_copy(unit).wait_recv()

            def body(i, carry):
                s.kept[unit, i] = (s.kept[unit, i].astype(F32) + s.taken[unit, i].astype(F32)).astype(BF)
                return carry

            lax.fori_loop(0, n, body, 0)
            line_start(line_of(unit))
        elif kind == 2:
            line_hop(line_of(unit), at)
        elif kind == 3:
            line_end(line_of(unit))
            rest_copy(unit, 0).start()
        elif kind == 4:
            rest_copy(unit, at).wait_recv()
            before = s.kept[unit, d] if at == 0 else s.rest_sum[unit, at - 1]
            s.rest_sum[unit, at] = (before.astype(F32) + s.rest_got[unit, at].astype(F32)).astype(BF)
            if at < bits - 2:
                rest_copy(unit, at + 1).start()
            else:
                last_copy(unit).start()
                own_result(unit).start()
        else:
            last_copy(unit).wait_recv()
            got_result(unit).start()

    small_line = SimpleNamespace(kept=s.small_kept, passed=s.small_passed, sems=s.small_line)

    def small_copy(bit):
        return remote(
            s.small_held.at[bit], s.small_group.at[bit], s.small_sent.at[1 + bit], s.small_got.at[1 + bit], across(bit)
        )

    def small_step(at):
        if at == 0:
            small_own.wait()
            small_swap.wait_recv()
            s.small_kept[...] += s.small_core[...]
        elif at <= bits:
            small_copy(at - 1).wait_recv()
            s.small_kept[...] += s.small_group[at - 1]
        if at < bits:
            s.small_held[at] = s.small_kept[...]
            small_copy(at).start()
        elif at == bits:
            line_start(small_line)
        elif at < bits + n - 1:
            line_hop(small_line, at - bits)
        else:
            line_end(small_line)
            total = s.small_kept[d]
            lanes = out.enc_gains.shape[1]
            for ref, row in (
                (out.enc_gains, 0), (out.enc_shifts, 2), (out.dec_gains, 4), (out.dec_shifts, 7)
            ):
                ref[...] = total[row : row + ref.shape[0], 0:lanes]
            out.table[...] = total[GAIN_ROWS : GAIN_ROWS + out.table.shape[0], 0:HEADS]

    small_steps = bits + n
    order = step_order(units, n - 1, bits - 1)
    every = len(order) // (small_steps + 2)
    for count, step in enumerate(order):
        take_step(*step)
        if count % every == every - 1 and count // every < small_steps:
            small_step(count // every)

    for unit in range(units):
        first_copy(unit).wait_send()
        line_sent(line_of(unit))
        for at in range(bits - 1):
            rest_copy(unit, at).wait_send()
        last_copy(unit).wait_send()
        own_result(unit).wait()
        got_result(unit).wait()
    for bit in range(bits):
        small_copy(bit).wait_send()
    line_sent(small_line)
    for wait in sent:
        wait()
    for kept, given in section_copies:
        kept.wait()
        given.wait()


def run_grads(n, bits, xs, gs, hbm, weights_out, lanes, table_shape):
    length, width = xs[1].shape
    half = width // 2
    block = width // (2 * n)
    first_units, unit_weight = [], []
    for at, x in enumerate(xs):
        first_units.append(len(unit_weight))
        count = max(x.shape[1] // width, gs[at].shape[-1] // width)
        unit_weight += [at] * count
    units = len(unit_weight)
    any_spec = pl.BlockSpec(memory_space=pl.ANY)
    vmem_spec = pl.BlockSpec(memory_space=pltpu.VMEM)
    micro = gs[0].shape[0]
    section = jax.ShapeDtypeStruct((1, micro, 1, length, width), BF)
    grads = [jax.ShapeDtypeStruct(shape, BF) for shape in weights_out]
    outs = dict(
        enc_gains=(2, lanes), enc_shifts=(2, lanes), dec_gains=(3, lanes), dec_shifts=(3, lanes), table=table_shape
    )
    outs = {name: jax.ShapeDtypeStruct(shape, F32) for name, shape in outs.items()}
    outs.update(outputs=section, input_grads=section)
    land_x = [jax.ShapeDtypeStruct((length, x.shape[1] // 2), BF) for x in xs]
    land_g = [jax.ShapeDtypeStruct(g.shape, BF) for g in gs[1:]]
    most = max(x.shape[1] for x in xs) // width
    rows = hbm["small"].shape[1]
    dma = pltpu.SemaphoreType.DMA
    small_all = pltpu.VMEM((n, rows, 128), F32)
    scratch = dict(
        x_stage=pltpu.VMEM((2, most, 2 * length, half), BF),
        g_stage=pltpu.VMEM((2, 2 * length, most * width), BF),
        factor=pltpu.VMEM((most, half, 2 * length), BF),
        kept=pltpu.VMEM((units, n, block, half), BF),
        given=pltpu.VMEM((units, n, block, half), BF),
        taken=pltpu.VMEM((units, n, block, half), BF),
        passed=pltpu.VMEM((units, n + 1, block, half), BF),
        rest_got=pltpu.VMEM((units, bits - 1, block, half), BF),
        rest_sum=pltpu.VMEM((units, bits - 1, block, half), BF),
        last_got=pltpu.VMEM((units, block, half), BF),
        small_kept=small_all, small_core=small_all,
        small_held=pltpu.VMEM((bits, n, rows, 128), F32),
        small_group=pltpu.VMEM((bits, n, rows, 128), F32),
        small_passed=pltpu.VMEM((n + 1, rows, 128), F32),
        swap_sent=dma((2 * len(xs),)), swap_got=dma((2 * len(xs),)),
        small_sent=dma((1 + bits,)), small_got=dma((1 + bits,)), small_load=dma, small_line=dma((4,)),
        section_kept=dma((2,)), section_sent=dma((2,)), section_got=dma((2,)),
        loads=dma((2, 2, 5)),
        first_sent=dma((units,)), first_got=dma((units,)), line_sems=dma((units, 4)),
        rest_sems=dma((units, bits - 1, 2)), last_sems=dma((units, 2)), result_sems=dma((units, 2)),
    )
    groups = [len(xs), len(gs), list(hbm), len(grads), list(outs), len(land_x), len(land_g), list(scratch)]
    out_specs = [any_spec] * len(grads) + [vmem_spec] * (len(outs) - 2) + [any_spec] * (2 + len(land_x) + len(land_g))
    results = pl.pallas_call(
        functools.partial(grads_kernel, micro, (n, bits, first_units, unit_weight), groups),
        out_shape=grads + list(outs.values()) + land_x + land_g,
        in_specs=[any_spec] * (len(xs) + len(gs) + len(hbm)),
        out_specs=out_specs,
        scratch_shapes=list(scratch.values()),
        compiler_params=pltpu.CompilerParams(
            collective_id=0, has_side_effects=True, vmem_limit_bytes=63 * 1024 * 1024
        ),
        name="grads",
    )(*xs, *gs, *hbm.values())
    return results[: len(grads)], dict(zip(outs, results[len(grads) :]))


def swap_pipe(array):
    devices = lax.axis_size("pipe")
    return lax.ppermute(array, "pipe", [(i, devices - 1 - i) for i in range(devices)])


def shards(
    section_inputs, cotangent, encoder_segments, decoder_segments, encoder_valid, decoder_valid,
    position_buckets, encoder_gains, encoder_shifts, encoder_qkv, encoder_out, encoder_up, encoder_down,
    position_table, decoder_gains, decoder_shifts, decoder_qkv, decoder_out, cross_query, cross_keyvalue,
    cross_out, decoder_up, decoder_down,
):
    own = section_inputs[0, :, 0]
    micro, length, width = own.shape
    pipe = lax.axis_index("pipe")
    dp = lax.axis_size("dp")
    bits = lax.axis_size("group").bit_length() - 1
    blocks = lax.axis_size("pipe") * dp
    mine = lax.dynamic_index_in_dim(own, pipe, keepdims=False)
    other = swap_pipe(lax.dynamic_index_in_dim(own, 1 - pipe, keepdims=False))
    is_encoder = pipe == 0
    x_enc = jnp.where(is_encoder, mine, other)
    x_dec = jnp.where(is_encoder, other, mine)
    weights = dict(
        e_qkv=encoder_qkv, e_out=encoder_out, e_up=encoder_up, e_down=encoder_down,
        d_qkv=decoder_qkv, d_out=decoder_out, c_query=cross_query, c_kv=cross_keyvalue,
        c_out=cross_out, d_up=decoder_up, d_down=decoder_down,
    )

    def per_row(array):
        return array.reshape(micro, length)

    small_in = dict(
        enc_seg=per_row(encoder_segments), dec_seg=per_row(decoder_segments),
        enc_valid=per_row(encoder_valid), dec_valid=per_row(decoder_valid),
        buckets=position_buckets.reshape(1, -1), enc_gains=encoder_gains, enc_shifts=encoder_shifts,
        dec_gains=decoder_gains, dec_shifts=decoder_shifts, table=position_table,
    )
    r = SimpleNamespace(
        **run_layers(blocks, dict(x_enc=x_enc, x_dec=x_dec, cot=cotangent), small_in, weights)
    )
    xs = [r.xd_down, r.xd_up, r.xc_out, r.memory, r.xc_query, r.xd_out, r.xd_qkv, r.xe_down, r.xe_up, r.xe_out, r.xe_qkv]
    gs = [cotangent, r.gd_up, r.gc_out, r.gc_kv, r.gc_query, r.gd_out, r.gd_qkv, r.ge_down, r.ge_up, r.ge_out, r.ge_qkv]
    order = [decoder_down, decoder_up, cross_out, cross_keyvalue, cross_query, decoder_out, decoder_qkv,
             encoder_down, encoder_up, encoder_out, encoder_qkv]
    cut = [(w.shape[0] // blocks, w.shape[1]) for w in order]
    hbm = dict(small=r.small, memory=r.memory, decoded=r.decoded, dx_enc=r.dx_enc, dx_dec=r.dx_dec)
    table_shape = (position_table.shape[0] // blocks, position_table.shape[1])
    grads, rest = run_grads(dp, bits, xs, gs, hbm, cut, width // blocks, table_shape)
    s = SimpleNamespace(**rest)
    d_down, d_up, c_out, c_kv, c_query, d_out, d_qkv, e_down, e_up, e_out, e_qkv = (a.astype(F32) for a in grads)
    return (
        s.outputs, s.input_grads, s.enc_gains, s.enc_shifts, e_qkv, e_out, e_up, e_down, s.table,
        s.dec_gains, s.dec_shifts, d_qkv, d_out, c_query, c_kv, c_out, d_up, d_down,
    )


def solution(mesh):
    section = P("pipe", None, ("dp", "group"), None, None)
    rows = P(None, ("dp", "group"), None)
    cut_rows = P(("pipe", "dp"), None)
    cut_lanes = P(None, ("pipe", "dp"))
    return jax.shard_map(
        shards,
        mesh=mesh,
        in_specs=(section, P(None, ("dp", "group"), None, None), rows, rows, rows, rows) + (P(),) * 17,
        out_specs=(section, section, cut_lanes, cut_lanes) + (cut_rows,) * 5 + (cut_lanes, cut_lanes) + (cut_rows,) * 7,
        check_vma=False,
    )
```

```python
import functools
from types import SimpleNamespace

import jax
import jax.numpy as jnp
from jax import lax
from jax.experimental import pallas as pl
from jax.experimental.pallas import tpu as pltpu
from jax.sharding import PartitionSpec as P

HEADS = 12
NEGATIVE = -1e30
BF, F32 = jnp.bfloat16, jnp.float32
GAIN_ROWS = 16


def dot(a, b):
    return jnp.dot(a, b, preferred_element_type=F32)


def dot_nt(a, b):
    return lax.dot_general(a, b, (((1,), (1,)), ((), ())), preferred_element_type=F32)


def dot_tn(a, b):
    return lax.dot_general(a, b, (((0,), (0,)), ((), ())), preferred_element_type=F32)


def row_loop(rows, chunk, body):
    def step(i, carry):
        body(pl.ds(pl.multiple_of(i * chunk, chunk), chunk))
        return carry

    lax.fori_loop(0, rows // chunk, step, 0)


def norm_stats(x):
    centre = x - jnp.mean(x, axis=-1, keepdims=True)
    spread = jnp.mean(centre * centre, axis=-1, keepdims=True)
    return centre, lax.rsqrt(spread + 1e-05)


def norm_forward(x_ref, gain, shift, n_ref):
    def body(rows):
        centre, inv = norm_stats(x_ref[rows, :].astype(F32))
        n_ref[rows, :] = (centre * inv * gain + shift).astype(BF)

    row_loop(x_ref.shape[0], 64, body)


def norm_backward(x_ref, gain, dn_ref, stream_ref, sums_ref, gain_at, shift_at):
    width = x_ref.shape[1]

    def step(i, carry):
        dgain, dshift = carry
        rows = pl.ds(pl.multiple_of(i * 64, 64), 64)
        centre, inv = norm_stats(x_ref[rows, :].astype(F32))
        hat = centre * inv
        dn = dn_ref[rows, :]
        dhat = dn * gain
        mean_one = jnp.mean(dhat, axis=-1, keepdims=True)
        mean_two = jnp.mean(dhat * hat, axis=-1, keepdims=True)
        stream_ref[rows, :] += inv * (dhat - mean_one - hat * mean_two)
        return (
            dgain + jnp.sum(dn * hat, axis=0, keepdims=True),
            dshift + jnp.sum(dn, axis=0, keepdims=True),
        )

    zero = jnp.zeros((1, width), F32)
    dgain, dshift = lax.fori_loop(0, x_ref.shape[0] // 64, step, (zero, zero))
    sums_ref[gain_at : gain_at + 1, :] = dgain
    sums_ref[shift_at : shift_at + 1, :] = dshift


def project(a_ref, w_ref, out_ref, tile=256):
    for start in range(0, w_ref.shape[1], tile):
        cols = slice(start, start + tile)
        out_ref[:, cols] = dot(a_ref[...], w_ref[:, cols]).astype(out_ref.dtype)


def project_add(a_ref, w_ref, resid_ref, out_ref, tile=256):
    for start in range(0, w_ref.shape[1], tile):
        cols = slice(start, start + tile)
        out_ref[:, cols] = (
            resid_ref[:, cols].astype(F32) + dot(a_ref[...], w_ref[:, cols])
        ).astype(out_ref.dtype)


def feed_up(n_ref, w_ref, z_ref, slope_ref, tile=512):
    for start in range(0, w_ref.shape[1], tile):
        cols = slice(start, start + tile)
        u = dot(n_ref[...], w_ref[:, cols])
        cdf = 0.5 * (1.0 + lax.erf(u * 0.7071067811865476))
        z_ref[:, cols] = (u * cdf).astype(BF)
        slope_ref[:, cols] = (cdf + u * (0.3989422804014327 * jnp.exp(-0.5 * u * u))).astype(BF)


def attend(q_ref, q_at, k_ref, k_at, v_ref, v_at, mask_ref, p_ref, o_ref, bias_ref=None):
    length = q_ref.shape[0]
    head = o_ref.shape[1] // HEADS
    pair = 2 * head
    scale = head**-0.5

    def step(i, carry):
        def cols(at):
            return pl.ds(pl.multiple_of(at + i * pair, pair), pair)

        low_half = lax.broadcasted_iota(jnp.int32, (length, pair), 1) < head
        q = q_ref[:, cols(q_at)] * jnp.asarray(scale, BF)
        k = k_ref[:, cols(k_at)]
        v = v_ref[:, cols(v_at)]
        outs = []
        for half in range(2):
            own = low_half if half == 0 else jnp.logical_not(low_half)
            s = dot_nt(jnp.where(own, q, jnp.zeros_like(q)), k) + mask_ref[...]
            if bias_ref is not None:
                wide = jnp.broadcast_to(
                    bias_ref[pl.ds(2 * i + half, 1), :], (length, 2 * length)
                )
                s = s + pltpu.roll(wide, length, 1, stride=1, stride_axis=0)[:, :length]
            e = jnp.exp(s - jnp.max(s, axis=-1, keepdims=True))
            p = (e * (1.0 / jnp.sum(e, axis=-1, keepdims=True))).astype(BF)
            p_ref[2 * i + half] = p
            outs.append(dot(p, v))
        o_ref[:, cols(0)] = jnp.where(low_half, outs[0], outs[1]).astype(BF)
        return carry

    lax.fori_loop(0, HEADS // 2, step, 0)


def attend_back(
    pairs, q_ref, q_at, k_ref, k_at, v_ref, v_at, p_ref, do_ref, diag_ref=None, flip_ref=None
):
    length = q_ref.shape[0]
    head = do_ref.shape[1] // HEADS
    pair = 2 * head
    scale = head**-0.5

    def step(i, carry):
        def cols(at):
            return pl.ds(pl.multiple_of(at + i * pair, pair), pair)

        low_half = lax.broadcasted_iota(jnp.int32, (length, pair), 1) < head
        q = q_ref[:, cols(q_at)]
        k = k_ref[:, cols(k_at)]
        v = v_ref[:, cols(v_at)]
        do = do_ref[:, cols(0)]
        dqs, dks, dvs = [], [], []
        for half in range(2):
            own = low_half if half == 0 else jnp.logical_not(low_half)
            p = p_ref[2 * i + half]
            dp = dot_nt(jnp.where(own, do, jnp.zeros_like(do)), v)
            wide_p = p.astype(F32)
            row = jnp.sum(wide_p * dp, axis=-1, keepdims=True)
            ds = (wide_p * (dp - row)).astype(BF)
            dvs.append(dot_tn(p, do))
            dqs.append(dot(ds, k))
            dks.append(dot_tn(ds, q))
            if diag_ref is not None:
                flipped = dot(flip_ref[...], ds)
                wide = jnp.concatenate([flipped, jnp.zeros_like(flipped)], axis=1)
                rolled = pltpu.roll(wide, 1, 1, stride=1, stride_axis=0)
                diag_ref[pl.ds(2 * i + half, 1), :] = jnp.sum(rolled, axis=0, keepdims=True)
        q_ref[:, cols(q_at)] = (jnp.where(low_half, dqs[0], dqs[1]) * scale).astype(BF)
        k_ref[:, cols(k_at)] = (jnp.where(low_half, dks[0], dks[1]) * scale).astype(BF)
        v_ref[:, cols(v_at)] = jnp.where(low_half, dvs[0], dvs[1]).astype(BF)
        return carry

    lax.fori_loop(pairs[0], pairs[1], step, 0)


def build_masks(eseg, dseg, evalid, dvalid, enc_ref, dec_ref, cross_ref):
    length = enc_ref.shape[0]
    shape = (length, length)
    key = lax.broadcasted_iota(jnp.int32, shape, 1)
    query = lax.broadcasted_iota(jnp.int32, shape, 0)
    eseg_key = jnp.broadcast_to(eseg.astype(F32), shape)
    dseg_key = jnp.broadcast_to(dseg.astype(F32), shape)
    eseg_query, dseg_query = eseg_key.T, dseg_key.T
    evalid_key = jnp.broadcast_to(evalid, shape) == 1
    dvalid_key = jnp.broadcast_to(dvalid, shape) == 1
    before = pltpu.roll(eseg_key, 1, 1)
    first = (key == 0) | (eseg_key != before)
    enc = (eseg_query == eseg_key) & (evalid_key | (key == query))
    dec = (dseg_query == dseg_key) & (dvalid_key | (key == query)) & (key <= query)
    cross = (dseg_query == eseg_key) & (evalid_key | first)
    enc_ref[...] = jnp.where(enc, 0.0, NEGATIVE)
    dec_ref[...] = jnp.where(dec, 0.0, NEGATIVE)
    cross_ref[...] = jnp.where(cross, 0.0, NEGATIVE)


def bucket_onehot(buckets, bucket_count):
    shape = (bucket_count, buckets.shape[1])
    return jnp.broadcast_to(buckets, shape) == lax.broadcasted_iota(jnp.int32, shape, 0)


def forward_kernel(groups, *refs):
    spaces = []
    for names in groups:
        spaces.append(SimpleNamespace(**dict(zip(names, refs))))
        refs = refs[len(names) :]
    hbm, small_in, out, v, s = spaces
    pipe = lax.axis_index("pipe")
    length, width = hbm.x_enc.shape
    started, pending = [], []

    def load(source, target):
        copy = pltpu.make_async_copy(source, target, s.sem_in.at[len(started)])
        copy.start()
        started.append(copy)
        return copy

    def store(source, target):
        copy = pltpu.make_async_copy(source, target, s.sem_out.at[len(pending)])
        copy.start()
        pending.append(copy)

    get_x_enc = load(hbm.x_enc, v.x_enc)
    get_e_qkv = load(hbm.e_qkv, s.e_qkv)
    get_e_out = load(hbm.e_out, s.e_out)
    get_e_up = load(hbm.e_up, s.up)
    get_e_down = load(hbm.e_down, s.down)
    get_x_dec = load(hbm.x_dec, v.x_dec)
    get_d_qkv = load(hbm.d_qkv, s.d_qkv)
    get_d_out = load(hbm.d_out, s.d_out)
    get_c_query = load(hbm.c_query, s.c_query)
    get_c_kv = load(hbm.c_kv, s.c_kv)
    get_c_out = load(hbm.c_out, s.c_out)

    own = pl.ds(pipe, 1)
    build_masks(
        small_in.enc_seg[own, :], small_in.dec_seg[own, :], small_in.enc_valid[own, :],
        small_in.dec_valid[own, :], s.mask_enc, s.mask_dec, s.mask_cross,
    )
    buckets = small_in.buckets[...]
    bucket_count = small_in.table.shape[0]
    s.bias[0:HEADS, :] = dot_tn(small_in.table[...], bucket_onehot(buckets, bucket_count).astype(BF))
    def at(ref, row):
        return ref[row : row + 1, :].astype(F32)

    enc_gains, enc_shifts = small_in.enc_gains, small_in.enc_shifts
    dec_gains, dec_shifts = small_in.dec_gains, small_in.dec_shifts

    get_x_enc.wait()
    norm_forward(v.x_enc, at(enc_gains, 0), at(enc_shifts, 0), v.xe_qkv)
    store(v.xe_qkv, out.xe_qkv)
    get_e_qkv.wait()
    project(v.xe_qkv, s.e_qkv, v.ge_qkv)
    attend(v.ge_qkv, 0, v.ge_qkv, width, v.ge_qkv, 2 * width, s.mask_enc, v.p_enc, v.xe_out, s.bias)
    store(v.ge_qkv, out.ge_qkv)
    store(v.p_enc, out.p_enc)
    store(v.xe_out, out.xe_out)
    get_e_out.wait()
    project_add(v.xe_out, s.e_out, v.x_enc, v.x1)
    store(v.x1, out.x1)
    norm_forward(v.x1, at(enc_gains, 1), at(enc_shifts, 1), v.xe_up)
    store(v.xe_up, out.xe_up)
    get_e_up.wait()
    feed_up(v.xe_up, s.up, v.xe_down, v.ge_up)
    get_d_up = load(hbm.d_up, s.up)
    store(v.xe_down, out.xe_down)
    store(v.ge_up, out.ge_up)
    get_e_down.wait()
    project_add(v.xe_down, s.down, v.x1, v.memory)
    get_d_down = load(hbm.d_down, s.down)
    store(v.memory, out.memory)

    get_x_dec.wait()
    norm_forward(v.x_dec, at(dec_gains, 0), at(dec_shifts, 0), v.xd_qkv)
    store(v.xd_qkv, out.xd_qkv)
    get_d_qkv.wait()
    project(v.xd_qkv, s.d_qkv, v.gd_qkv)
    attend(v.gd_qkv, 0, v.gd_qkv, width, v.gd_qkv, 2 * width, s.mask_dec, v.p_dec, v.xd_out)
    store(v.xd_out, out.xd_out)
    store(v.gd_qkv, out.gd_qkv)
    store(v.p_dec, out.p_dec)
    get_d_out.wait()
    project_add(v.xd_out, s.d_out, v.x_dec, v.d1)
    store(v.d1, out.d1)
    norm_forward(v.d1, at(dec_gains, 1), at(dec_shifts, 1), v.xc_query)
    store(v.xc_query, out.xc_query)
    get_c_query.wait()
    project(v.xc_query, s.c_query, v.gc_query)
    get_c_kv.wait()
    project(v.memory, s.c_kv, v.gc_kv)
    attend(v.gc_query, 0, v.gc_kv, 0, v.gc_kv, width, s.mask_cross, v.p_cross, v.xc_out)
    store(v.xc_out, out.xc_out)
    store(v.gc_query, out.gc_query)
    store(v.gc_kv, out.gc_kv)
    store(v.p_cross, out.p_cross)
    get_c_out.wait()
    project_add(v.xc_out, s.c_out, v.d1, v.d2)
    store(v.d2, out.d2)
    norm_forward(v.d2, at(dec_gains, 2), at(dec_shifts, 2), v.xd_up)
    store(v.xd_up, out.xd_up)
    get_d_up.wait()
    feed_up(v.xd_up, s.up, v.xd_down, v.gd_up)
    store(v.xd_down, out.xd_down)
    store(v.gd_up, out.gd_up)
    get_d_down.wait()
    project_add(v.xd_down, s.down, v.d2, v.decoded)
    store(v.decoded, out.decoded)

    for copy in pending:
        copy.wait()


def run_forward(inputs, small_in, weights):
    length, width = inputs["x_enc"].shape
    hidden = weights["e_up"].shape[1]
    hbm = dict(inputs, **weights)
    any_spec = pl.BlockSpec(memory_space=pl.ANY)
    vmem_spec = pl.BlockSpec(memory_space=pltpu.VMEM)
    columns = dict(
        xe_qkv=width, xe_out=width, xe_up=width, xe_down=hidden, memory=width,
        xd_qkv=width, xd_out=width, xc_query=width, xc_out=width, xd_up=width, xd_down=hidden,
        ge_qkv=3 * width, ge_up=hidden, gd_qkv=3 * width, gc_query=width, gc_kv=2 * width, gd_up=hidden,
        decoded=width,
    )
    outs = {name: jax.ShapeDtypeStruct((length, n), BF) for name, n in columns.items()}
    probabilities = jax.ShapeDtypeStruct((HEADS, length, length), BF)
    rows = jax.ShapeDtypeStruct((length, width), F32)
    outs.update(p_enc=probabilities, p_dec=probabilities, p_cross=probabilities, x1=rows, d1=rows, d2=rows)
    held = {name: pltpu.VMEM(shape.shape, shape.dtype) for name, shape in outs.items()}
    held.update({name: pltpu.VMEM((length, width), BF) for name in inputs})
    square = pltpu.VMEM((length, length), F32)
    scratch = {
        name: pltpu.VMEM(w.shape, BF) for name, w in weights.items() if hidden not in w.shape
    }
    scratch.update(
        up=pltpu.VMEM((width, hidden), BF), down=pltpu.VMEM((hidden, width), BF),
        mask_enc=square, mask_dec=square, mask_cross=square, bias=pltpu.VMEM((16, 2 * length), F32),
        sem_in=pltpu.SemaphoreType.DMA((16,)), sem_out=pltpu.SemaphoreType.DMA((len(outs),)),
    )
    groups = [list(part) for part in (hbm, small_in, outs, held, scratch)]
    results = pl.pallas_call(
        functools.partial(forward_kernel, groups),
        out_shape=list(outs.values()),
        in_specs=[any_spec] * len(hbm) + [vmem_spec] * len(small_in),
        out_specs=[any_spec] * len(outs),
        scratch_shapes=list(held.values()) + list(scratch.values()),
        compiler_params=pltpu.CompilerParams(vmem_limit_bytes=63 * 1024 * 1024),
        name="forward",
    )(*hbm.values(), *small_in.values())
    return dict(zip(outs, results))


MESH = pl.DeviceIdType.MESH


def step_order(work, small_after, units, n, bits, window=3):
    big, delay, cost = 6.6, 2.0, 0.5
    small = big / n
    sides, line = [0.0, 0.0], [0.0] * n
    waiting, steps = [], []
    flying = [0, 0]
    clock, made, done = 0.0, 0, 0

    def message(free, at, start, size):
        free[at] = max(free[at], start) + size
        return free[at] + delay

    while done < len(work) or waiting:
        ready = [event for event in waiting if event[0] <= clock]
        if ready:
            event = min(ready)
            waiting.remove(event)
            unused, kind, unit, at = event
            steps.append((kind, unit, at))
            clock += cost
            first, other = unit % 2, 1 - unit % 2
            if kind == 1:
                flying[first] -= 1
                waiting.append((message(line, 1, clock, (n - 1) * small), 2 if n > 2 else 3, unit, 1))
            elif kind == 2:
                arrival = message(line, at + 1, clock, (n - 1 - at) * small)
                waiting.append((arrival, 2 if at + 1 < n - 1 else 3, unit, at + 1))
            elif kind == 3:
                waiting.append((message(sides, other, clock, small), 4, unit, 0))
            elif kind == 4 and at + 2 < bits:
                waiting.append((message(sides, other, clock, small), 4, unit, at + 1))
            elif kind == 4:
                waiting.append((message(sides, first, clock, small), 5, unit, 0))
            elif kind == 6 and at + 1 < bits + n:
                waiting.append((clock + 2 * delay, 6, 0, at + 1))
        elif done < len(work) and (not work[done][1] or flying[made % 2] < window):
            clock += work[done][0]
            steps.append((0, done, 0))
            if work[done][1]:
                waiting.append((message(sides, made % 2, clock, big), 1, made, 0))
                flying[made % 2] += 1
                made += 1
            if done == small_after:
                waiting.append((clock + delay, 6, 0, 0))
            done += 1
        else:
            clock = min(waiting)[0]
    return steps


def backward_kernel(tables, groups, *refs):
    spaces = []
    for names in groups:
        if isinstance(names, int):
            spaces.append(refs[:names])
            refs = refs[names:]
        else:
            spaces.append(SimpleNamespace(**dict(zip(names, refs))))
            refs = refs[len(names) :]
    xs, hbm, small_in, grads, out, land_x, land_g, v, s = spaces
    n, bits, first_units, unit_weight = tables
    p, d, g = lax.axis_index("pipe"), lax.axis_index("dp"), lax.axis_index("group")
    units = len(unit_weight)
    length, width = v.stream.shape
    half = width // 2
    block = width // (2 * n)
    blocks = 2 * n
    gs = [
        v.cot, v.gd_up, v.gc_out, v.gc_kv, v.gc_query, v.gd_out, v.gd_qkv, v.ge_down, v.ge_up, v.ge_out, v.ge_qkv
    ]
    d_down, d_up, c_out, c_kv, c_query, d_out, d_qkv, e_down, e_up, e_out, e_qkv = range(len(gs))

    def bit_of(bit):
        return (g // 2**bit) % 2

    def across(bit):
        return (p, d, g + (1 - 2 * bit_of(bit)) * 2**bit)

    core = (1 - p, d, g)
    above, below = (p, d + 1, g), (p, d - 1, g)

    loads = []

    def load(source, target):
        copy = pltpu.make_async_copy(source, target, s.load_sems.at[len(loads)])
        copy.start()
        loads.append(copy)
        return copy

    get_cot = load(hbm.cot.at[p, 0], v.cot)

    slots = s.stream_w.shape[0]
    side = s.stream_w.shape[1]
    walk = []
    for ref in (
        hbm.d_down, hbm.d_up, hbm.c_out, hbm.c_kv, hbm.c_query, hbm.d_out, hbm.d_qkv, hbm.e_down, hbm.e_up,
        hbm.e_out, hbm.e_qkv,
    ):
        for row in range(0, ref.shape[0], side):
            for column in range(0, ref.shape[1], width):
                walk.append(ref.at[row : row + side, column : column + width])
    walked = [0]

    def weight_copy(at):
        return pltpu.make_async_copy(walk[at], s.stream_w.at[at % slots], s.stream_sems.at[at % slots])

    for at in range(slots):
        weight_copy(at).start()

    def times_next(value):
        at = walked[0]
        walked[0] += 1
        weight_copy(at).wait()
        result = dot_nt(value, s.stream_w[at % slots])
        if at + slots < len(walk):
            weight_copy(at + slots).start()
        return result

    def back_through(g_ref, out_ref):
        for row in range(0, out_ref.shape[1], side):
            total = times_next(g_ref[:, 0:width])
            for column in range(width, g_ref.shape[1], width):
                total += times_next(g_ref[:, column : column + width])
            out_ref[:, row : row + side] = total.astype(out_ref.dtype)

    def back_through_feed(g_ref, slope_ref, start, stop):
        for row in range(start, stop, side):
            cols = slice(row, row + side)
            slope_ref[:, cols] = (times_next(g_ref[...]) * slope_ref[:, cols].astype(F32)).astype(BF)

    get_gd_up = load(hbm.gd_up, v.gd_up)
    get_d2 = load(hbm.d2, v.d2)
    get_p = [load(hbm.p_cross, v.p)]
    get_gc_query = load(hbm.gc_query, v.gc_query)
    get_gc_kv = load(hbm.gc_kv, v.gc_kv)
    get_d1 = load(hbm.d1, v.d1)
    get_gd_qkv = load(hbm.gd_qkv, v.gd_qkv)
    get_x_dec = load(hbm.x_dec, v.x_dec)
    get_ge_up = load(hbm.ge_up, v.ge_up)
    get_x1 = load(hbm.x1, v.x1)
    get_ge_qkv = load(hbm.ge_qkv, v.ge_qkv)
    get_x_enc = load(hbm.x_enc, v.x_enc)

    barrier = pltpu.get_barrier_semaphore()
    pl.semaphore_signal(barrier, inc=1, device_id=core, device_id_type=MESH)
    for bit in range(bits):
        pl.semaphore_signal(barrier, inc=1, device_id=across(bit), device_id_type=MESH)

    @pl.when(d > 0)
    def _():
        pl.semaphore_signal(barrier, inc=1, device_id=below, device_id_type=MESH)

    @pl.when(d < n - 1)
    def _():
        pl.semaphore_signal(barrier, inc=1, device_id=above, device_id_type=MESH)

    @pl.when((d > 0) & (d < n - 1))
    def _():
        pl.semaphore_wait(barrier, 3 + bits)

    @pl.when((d == 0) | (d == n - 1))
    def _():
        pl.semaphore_wait(barrier, 2 + bits)

    def remote(source, target, send_sem, recv_sem, device):
        return pltpu.make_async_remote_copy(
            src_ref=source, dst_ref=target, send_sem=send_sem, recv_sem=recv_sem,
            device_id=device, device_id_type=MESH,
        )

    sent = []

    def send(copy):
        copy.start()
        sent.append(copy.wait_send)
        return copy

    x_swaps, g_swaps = [], {}
    for at in range(len(xs)):
        part = xs[at].shape[1] // 2
        theirs = pl.ds(pl.multiple_of((1 - p) * part, 128), part)
        x_swaps.append(
            send(remote(xs[at].at[:, theirs], land_x[at], s.swap_sent.at[2 * at], s.swap_got.at[2 * at], core))
        )

    def swap_g(at):
        g_swaps[at] = send(
            remote(gs[at], land_g[at - 1], s.swap_sent.at[2 * at + 1], s.swap_got.at[2 * at + 1], core)
        )

    for layer, keep, give in ((0, hbm.memory, hbm.decoded), (1, hbm.decoded, hbm.memory)):

        @pl.when(p == layer)
        def _(keep=keep, give=give):
            pltpu.make_async_copy(keep, out.outputs.at[0, p, 0], s.section_kept.at[0]).start()
            remote(give, out.outputs.at[0, p, 0], s.section_sent.at[0], s.section_got.at[0], core).start()

    def input_grad(layer, ref):
        @pl.when(p == layer)
        def _():
            pltpu.make_async_copy(ref, out.input_grads.at[0, p, 0], s.section_kept.at[1]).start()

        @pl.when(p != layer)
        def _():
            remote(ref, out.input_grads.at[0, p, 0], s.section_sent.at[1], s.section_got.at[1], core).start()

    section_copies = [
        (
            pltpu.make_async_copy(hbm.memory, target.at[0, p, 0], s.section_kept.at[at]),
            remote(hbm.memory, target.at[0, 1 - p, 0], s.section_sent.at[at], s.section_got.at[at], core),
        )
        for at, target in enumerate((out.outputs, out.input_grads))
    ]

    def tiles_of(at):
        return xs[at].shape[1] // width

    def fetch(at):
        copies = []
        part = xs[at].shape[1] // 2
        for tile in range(tiles_of(at)):
            mine = pl.ds(pl.multiple_of(p * part + tile * half, 128), half)
            copies.append((xs[at].at[:, mine], s.x_stage.at[tile, 0:length]))
        x_swaps[at].wait_recv()
        for tile in range(tiles_of(at)):
            copies.append(
                (land_x[at].at[:, tile * half : (tile + 1) * half], s.x_stage.at[tile, length : 2 * length])
            )
        if at > 0:
            g_swaps[at].wait_recv()
        source = hbm.cot.at[1 - p, 0] if at == 0 else land_g[at - 1]
        copies.append((source, s.g_stage.at[:, 0 : source.shape[1]]))
        started = []
        for count, (origin, target) in enumerate(copies):
            copy = pltpu.make_async_copy(origin, target, s.stage_sems.at[count])
            copy.start()
            started.append(copy)
        fetched[at] = started

    fetched = {}

    def first_bit(unit):
        return 0 if unit % 2 == 0 else bits - 1

    rooms = s.given.shape[0]

    def first_copy(unit):
        return remote(
            s.given.at[unit % rooms], s.taken.at[unit], s.first_sent.at[unit], s.first_got.at[unit],
            across(first_bit(unit)),
        )

    def product(at, tile, cols):
        value = dot(s.factor[tile, :, 0:length], gs[at][:, cols])
        return (value + dot(s.factor[tile, :, length : 2 * length], s.g_stage[:, cols])).astype(BF)

    def room_free(unit):
        if unit >= rooms:
            first_copy(unit - rooms).wait_send()

    def make(unit):
        at = unit_weight[unit]
        base = first_units[at]
        tiles = tiles_of(at)
        if unit == base:
            for copy in fetched.pop(at):
                copy.wait()
            for tile in range(tiles):
                s.factor[tile] = s.x_stage[tile].T
        if tiles == 1:
            room_free(unit)
            mine = bit_of(first_bit(unit))
            column = (unit - base) * width
            given = product(at, 0, pl.ds(pl.multiple_of(column + (1 - mine) * half, 128), half))
            for i in range(n):
                s.given[unit % rooms, i] = given[i * block : (i + 1) * block]
            first_copy(unit).start()
            kept = product(at, 0, pl.ds(pl.multiple_of(column + mine * half, 128), half))
            for i in range(n):
                s.kept[unit, i] = kept[i * block : (i + 1) * block]
            return
        if unit == base:
            for i in range(tiles):
                room_free(unit + i)
            for tile in range(tiles):
                for which in range(2):
                    split_rows(base, tiles, tile, which, product(at, tile, slice(which * half, (which + 1) * half)))
        first_copy(unit).start()

    def split_rows(base, tiles, tile, which, value):
        for i in range(n):
            unit = base + (tile * n + i) % tiles
            at = (tile * n + i) // tiles
            mine = bit_of(first_bit(unit))
            rows = value[i * block : (i + 1) * block]

            @pl.when(mine == which)
            def _(unit=unit, at=at, rows=rows):
                s.kept[unit, at] = rows

            @pl.when(mine != which)
            def _(unit=unit, at=at, rows=rows):
                s.given[unit % rooms, at] = rows

    def add(target, index, source, source_index):
        target[index] = (target[index].astype(F32) + source[source_index].astype(F32)).astype(target.dtype)

    def up_copy(line, dd):
        source = line.kept.at[1:n] if dd == 0 else line.passed.at[dd + 2 : n + 1]
        return remote(source, line.passed.at[dd + 2 : n + 1], line.sems.at[0], line.sems.at[1], above)

    def down_copy(line, dd):
        source = line.kept.at[0 : n - 1] if dd == n - 1 else line.passed.at[0:dd]
        return remote(source, line.passed.at[0:dd], line.sems.at[2], line.sems.at[3], below)

    def line_start(line):
        @pl.when(d == 0)
        def _():
            up_copy(line, 0).start()

        @pl.when(d == n - 1)
        def _():
            down_copy(line, n - 1).start()

    def line_hop(line, hop):
        @pl.when(d == hop)
        def _():
            up_copy(line, hop - 1).wait_recv()
            for i in range(hop + 1, n):
                add(line.passed, i + 1, line.kept, i)
            up_copy(line, hop).start()

        @pl.when(d == n - 1 - hop)
        def _():
            down_copy(line, n - hop).wait_recv()
            for i in range(n - 1 - hop):
                add(line.passed, i, line.kept, i)
            down_copy(line, n - 1 - hop).start()

    def line_end(line):
        @pl.when(d == n - 1)
        def _():
            up_copy(line, n - 2).wait_recv()
            line.kept[n - 1] = (
                line.kept[n - 1].astype(F32) + line.passed[n].astype(F32)
            ).astype(line.kept.dtype)

        @pl.when(d == 0)
        def _():
            down_copy(line, 1).wait_recv()
            line.kept[0] = (line.kept[0].astype(F32) + line.passed[0].astype(F32)).astype(line.kept.dtype)

        for dd in range(1, n - 1):

            @pl.when(d == dd)
            def _(dd=dd):
                line.kept[dd] = (
                    line.kept[dd].astype(F32) + line.passed[dd + 1].astype(F32) + line.passed[dd].astype(F32)
                ).astype(line.kept.dtype)

    def line_sent(line):
        for dd in range(n):

            @pl.when(d == dd)
            def _(dd=dd):
                if dd < n - 1:
                    up_copy(line, dd).wait_send()
                if dd > 0:
                    down_copy(line, dd).wait_send()

    def line_of(unit):
        return SimpleNamespace(
            kept=s.kept.at[unit], passed=s.passed.at[unit], sems=s.line_sems.at[unit]
        )

    def rest_bits(unit):
        return [bit for bit in range(bits) if bit != first_bit(unit)]

    def rest_copy(unit, at):
        source = s.kept.at[unit, d] if at == 0 else s.rest_sum.at[unit, at - 1]
        return remote(
            source, s.rest_got.at[unit, at], s.rest_sems.at[unit, at, 0], s.rest_sems.at[unit, at, 1],
            across(rest_bits(unit)[at]),
        )

    def last_copy(unit):
        return remote(
            s.rest_sum.at[unit, bits - 2], s.last_got.at[unit], s.last_sems.at[unit, 0], s.last_sems.at[unit, 1],
            across(first_bit(unit)),
        )

    def result_at(unit, which):
        at = unit_weight[unit]
        k = unit - first_units[at]
        target = grads[at]
        if tiles_of(at) == 1:
            return target.at[:, pl.ds(pl.multiple_of(k * width + which * half, 128), half)]
        return target.at[pl.ds(k * block, block), pl.ds(pl.multiple_of(which * half, 128), half)]

    def own_result(unit):
        return pltpu.make_async_copy(
            s.rest_sum.at[unit, bits - 2], result_at(unit, bit_of(first_bit(unit))), s.result_sems.at[unit, 0]
        )

    def got_result(unit):
        return pltpu.make_async_copy(
            s.last_got.at[unit], result_at(unit, 1 - bit_of(first_bit(unit))), s.result_sems.at[unit, 1]
        )

    small_line = SimpleNamespace(kept=s.small_kept, passed=s.small_passed, sems=s.small_line)
    small_swap = remote(
        s.small.at[pl.ds((1 - p) * n, n)], s.small_core, s.small_sent.at[0], s.small_got.at[0], core
    )

    def small_copy(bit):
        return remote(
            s.small_held.at[bit], s.small_group.at[bit], s.small_sent.at[1 + bit], s.small_got.at[1 + bit], across(bit)
        )

    def small_step(at):
        if at == 0:
            small_swap.wait_recv()
            s.small_kept[...] = s.small[pl.ds(p * n, n)] + s.small_core[...]
        elif at <= bits:
            small_copy(at - 1).wait_recv()
            s.small_kept[...] += s.small_group[at - 1]
        if at < bits:
            s.small_held[at] = s.small_kept[...]
            small_copy(at).start()
        elif at == bits:
            line_start(small_line)
        elif at < bits + n - 1:
            line_hop(small_line, at - bits)
        else:
            line_end(small_line)
            total = s.small_kept[d]
            lanes = out.enc_gains.shape[1]
            for ref, row in (
                (out.enc_gains, 0), (out.enc_shifts, 2), (out.dec_gains, 4), (out.dec_shifts, 7)
            ):
                ref[...] = total[row : row + ref.shape[0], 0:lanes]
            out.table[...] = total[GAIN_ROWS : GAIN_ROWS + out.table.shape[0], 0:HEADS]

    def gain(ref, row):
        return ref[row : row + 1, :].astype(F32)

    enc_gains, dec_gains = small_in.enc_gains, small_in.dec_gains
    pairs = HEADS // 2
    work = []

    def piece(time, body, *args):
        work.append((time, False, functools.partial(body, *args)))

    def make_all(at):
        count = max(tiles_of(at), gs[at].shape[1] // width)
        for i in range(count):
            first_time = 1.0 + 0.5 * tiles_of(at) + (2.0 if tiles_of(at) > 1 else 0.0)
            later = 0.2 if tiles_of(at) > 1 else 1.2
            work.append((first_time if i == 0 else later, True, functools.partial(make, first_units[at] + i)))

    def start_feed(g_ref, slope_ref, get):
        get.wait()
        back_through_feed(g_ref, slope_ref, 0, slope_ref.shape[1] // 2)

    def end_feed(g_ref, slope_ref, at):
        back_through_feed(g_ref, slope_ref, slope_ref.shape[1] // 2, slope_ref.shape[1])
        swap_g(at)

    def residual(x_ref, get, gain_row, gain_at, shift_at, low_ref):
        get.wait()
        norm_backward(x_ref, gain_row, v.dn, v.stream, s.sums, gain_at, shift_at)
        low_ref[...] = v.stream[...].astype(BF)

    def residual_swap(x_ref, get, gain_row, gain_at, shift_at, low_ref, at):
        residual(x_ref, get, gain_row, gain_at, shift_at, low_ref)
        swap_g(at)
        back_through(low_ref, v.do)

    def begin():
        s.sums[...] = jnp.zeros_like(s.sums)
        get_cot.wait()
        v.stream[...] = v.cot[...].astype(F32)
        start_feed(v.cot, v.gd_up, get_gd_up)

    def cross_part(first, last):
        if first == 0:
            get_p[0].wait()
            get_gc_query.wait()
            get_gc_kv.wait()
        attend_back((first, last), v.gc_query, 0, v.gc_kv, 0, v.gc_kv, width, v.p, v.do)
        if last == pairs:
            get_p.append(load(hbm.p_dec, v.p))
            swap_g(c_kv)
            swap_g(c_query)

    def dec_part(first, last):
        if first == 0:
            get_p[1].wait()
            get_gd_qkv.wait()
        attend_back((first, last), v.gd_qkv, 0, v.gd_qkv, width, v.gd_qkv, 2 * width, v.p, v.do)
        if last == pairs:
            get_p.append(load(hbm.p_enc, v.p))
            swap_g(d_qkv)

    def enc_part(first, last):
        if first == 0:
            get_p[2].wait()
            get_ge_qkv.wait()
            s.diag[...] = jnp.zeros_like(s.diag)
            flip_shape = (length, length)
            s.flip[...] = (
                lax.broadcasted_iota(jnp.int32, flip_shape, 0) + lax.broadcasted_iota(jnp.int32, flip_shape, 1)
                == length - 1
            ).astype(BF)
        attend_back(
            (first, last), v.ge_qkv, 0, v.ge_qkv, width, v.ge_qkv, 2 * width, v.p, v.do, s.diag, s.flip
        )
        if last == pairs:
            swap_g(e_qkv)

    def memory_part():
        back_through(v.gc_kv, v.ge_down)
        swap_g(e_down)

    def dec_end():
        residual(v.x_dec, get_x_dec, gain(dec_gains, 0), 4, 7, v.dx_dec)
        input_grad(1, v.dx_dec)
        v.stream[...] = v.ge_down[...].astype(F32)

    def small_part():
        residual(v.x_enc, get_x_enc, gain(enc_gains, 0), 0, 2, v.dx_enc)
        input_grad(0, v.dx_enc)
        buckets = small_in.buckets[...]
        bucket_count = out.table.shape[0] * blocks
        onehot = bucket_onehot(buckets, bucket_count).astype(BF)
        rest = s.diag[...]
        table_grad = jnp.zeros((bucket_count, rest.shape[0]), F32)
        for unused in range(3):
            part = rest.astype(BF)
            rest = rest - part.astype(F32)
            table_grad = table_grad + dot_nt(onehot, part)
        s.small[...] = jnp.zeros_like(s.small)
        lanes = width // blocks
        table_rows = bucket_count // blocks
        for at in range(blocks):
            s.small[at, 0:GAIN_ROWS, 0:lanes] = s.sums[:, at * lanes : (at + 1) * lanes]
            s.small[at, GAIN_ROWS : GAIN_ROWS + table_rows, 0 : rest.shape[0]] = table_grad[
                at * table_rows : (at + 1) * table_rows, :
            ]
        small_swap.start()

    piece(2.5, begin)
    piece(0.5, fetch, d_down)
    piece(2.0, end_feed, v.cot, v.gd_up, d_up)
    make_all(d_down)
    piece(3.5, back_through, v.gd_up, v.dn)
    piece(0.5, fetch, d_up)
    piece(2.5, residual_swap, v.d2, get_d2, gain(dec_gains, 2), 6, 9, v.gc_out, c_out)
    make_all(d_up)
    piece(0.5, fetch, c_out)
    piece(2.0, cross_part, 0, pairs // 2)
    make_all(c_out)
    piece(2.0, cross_part, pairs // 2, pairs)
    piece(2.0, memory_part)
    piece(0.5, fetch, c_kv)
    piece(1.0, back_through, v.gc_query, v.dn)
    make_all(c_kv)
    piece(0.5, fetch, c_query)
    piece(2.5, residual_swap, v.d1, get_d1, gain(dec_gains, 1), 5, 8, v.gd_out, d_out)
    make_all(c_query)
    piece(0.5, fetch, d_out)
    piece(2.0, dec_part, 0, pairs // 2)
    make_all(d_out)
    piece(2.0, dec_part, pairs // 2, pairs)
    piece(3.0, back_through, v.gd_qkv, v.dn)
    piece(0.5, fetch, d_qkv)
    piece(1.0, dec_end)
    make_all(d_qkv)
    piece(0.5, fetch, e_down)
    piece(2.5, start_feed, v.ge_down, v.ge_up, get_ge_up)
    make_all(e_down)
    piece(2.0, end_feed, v.ge_down, v.ge_up, e_up)
    piece(3.5, back_through, v.ge_up, v.dn)
    piece(0.5, fetch, e_up)
    piece(2.5, residual_swap, v.x1, get_x1, gain(enc_gains, 1), 1, 3, v.ge_out, e_out)
    make_all(e_up)
    piece(0.5, fetch, e_out)
    piece(2.5, enc_part, 0, pairs // 2)
    make_all(e_out)
    piece(2.5, enc_part, pairs // 2, pairs)
    piece(3.0, back_through, v.ge_qkv, v.dn)
    piece(0.5, fetch, e_qkv)
    small_after = len(work)
    piece(2.0, small_part)
    make_all(e_qkv)

    def take_step(kind, unit, at):
        if kind == 0:
            work[unit][2]()
        elif kind == 1:
            first_copy(unit).wait_recv()

            def body(i, carry):
                s.kept[unit, i] = (s.kept[unit, i].astype(F32) + s.taken[unit, i].astype(F32)).astype(BF)
                return carry

            lax.fori_loop(0, n, body, 0)
            line_start(line_of(unit))
        elif kind == 2:
            line_hop(line_of(unit), at)
        elif kind == 3:
            line_end(line_of(unit))
            rest_copy(unit, 0).start()
        elif kind == 4:
            rest_copy(unit, at).wait_recv()
            before = s.kept[unit, d] if at == 0 else s.rest_sum[unit, at - 1]
            s.rest_sum[unit, at] = (before.astype(F32) + s.rest_got[unit, at].astype(F32)).astype(BF)
            if at < bits - 2:
                rest_copy(unit, at + 1).start()
            else:
                last_copy(unit).start()
                own_result(unit).start()
        elif kind == 5:
            last_copy(unit).wait_recv()
            got_result(unit).start()
        else:
            small_step(at)

    plan = [(time, makes) for time, makes, unused in work]
    for step in step_order(plan, small_after, units, n, bits):
        take_step(*step)

    for unit in range(units):
        if unit + rooms >= units:
            first_copy(unit).wait_send()
        line_sent(line_of(unit))
        for at in range(bits - 1):
            rest_copy(unit, at).wait_send()
        last_copy(unit).wait_send()
        own_result(unit).wait()
        got_result(unit).wait()
    small_swap.wait_send()
    for bit in range(bits):
        small_copy(bit).wait_send()
    line_sent(small_line)
    for wait in sent:
        wait()
    for kept, given in section_copies:
        kept.wait()
        given.wait()


def run_backward(n, bits, xs, hbm, small_in, weights_out, g_columns, lanes, table_shape):
    length, width = xs[1].shape
    half = width // 2
    block = width // (2 * n)
    first_units, unit_weight = [], []
    for at, x in enumerate(xs):
        first_units.append(len(unit_weight))
        unit_weight += [at] * (max(x.shape[1], g_columns[at]) // width)
    units = len(unit_weight)
    any_spec = pl.BlockSpec(memory_space=pl.ANY)
    vmem_spec = pl.BlockSpec(memory_space=pltpu.VMEM)
    section = jax.ShapeDtypeStruct((1, hbm["cot"].shape[0], 1, length, width), BF)
    grads = [jax.ShapeDtypeStruct(shape, BF) for shape in weights_out]
    outs = dict(
        enc_gains=(2, lanes), enc_shifts=(2, lanes), dec_gains=(3, lanes), dec_shifts=(3, lanes), table=table_shape
    )
    outs = {name: jax.ShapeDtypeStruct(shape, F32) for name, shape in outs.items()}
    outs.update(outputs=section, input_grads=section)
    land_x = [jax.ShapeDtypeStruct((length, x.shape[1] // 2), BF) for x in xs]
    land_g = [jax.ShapeDtypeStruct((length, columns), BF) for columns in g_columns[1:]]
    most = max(x.shape[1] for x in xs) // width
    small_rows = -(-(GAIN_ROWS + table_shape[0]) // 16) * 16
    dma = pltpu.SemaphoreType.DMA
    small_all = pltpu.VMEM((n, small_rows, 128), F32)
    low = pltpu.VMEM((length, width), BF)
    wide = pltpu.VMEM((length, width), F32)
    held = dict(
        cot=low, x_dec=low, x_enc=low, gc_query=low, gc_out=low, gd_out=low, ge_out=low, ge_down=low, do=low,
        dx_dec=low, dx_enc=low, d2=wide, d1=wide, x1=wide, stream=wide, dn=wide,
        gd_up=pltpu.VMEM((length, most * width), BF), ge_up=pltpu.VMEM((length, most * width), BF),
        gd_qkv=pltpu.VMEM((length, 3 * width), BF), ge_qkv=pltpu.VMEM((length, 3 * width), BF),
        gc_kv=pltpu.VMEM((length, 2 * width), BF), p=pltpu.VMEM((HEADS, length, length), BF),
    )
    scratch = dict(
        stream_w=pltpu.VMEM((12, 256, width), BF),
        x_stage=pltpu.VMEM((most, 2 * length, half), BF),
        g_stage=pltpu.VMEM((length, most * width), BF),
        factor=pltpu.VMEM((most, half, 2 * length), BF),
        kept=pltpu.VMEM((units, n, block, half), BF),
        given=pltpu.VMEM((10, n, block, half), BF),
        taken=pltpu.VMEM((units, n, block, half), BF),
        passed=pltpu.VMEM((units, n + 1, block, half), BF),
        rest_got=pltpu.VMEM((units, bits - 1, block, half), BF),
        rest_sum=pltpu.VMEM((units, bits - 1, block, half), BF),
        last_got=pltpu.VMEM((units, block, half), BF),
        sums=pltpu.VMEM((GAIN_ROWS, width), F32), diag=pltpu.VMEM((16, 2 * length), F32),
        flip=pltpu.VMEM((length, length), BF), small=pltpu.VMEM((2 * n, small_rows, 128), F32),
        small_kept=small_all, small_core=small_all,
        small_held=pltpu.VMEM((bits, n, small_rows, 128), F32),
        small_group=pltpu.VMEM((bits, n, small_rows, 128), F32),
        small_passed=pltpu.VMEM((n + 1, small_rows, 128), F32),
        load_sems=dma((15,)), stream_sems=dma((12,)), stage_sems=dma((2 * most + 1,)),
        swap_sent=dma((2 * len(xs),)), swap_got=dma((2 * len(xs),)),
        small_sent=dma((1 + bits,)), small_got=dma((1 + bits,)), small_line=dma((4,)),
        section_kept=dma((2,)), section_sent=dma((2,)), section_got=dma((2,)),
        first_sent=dma((units,)), first_got=dma((units,)), line_sems=dma((units, 4)),
        rest_sems=dma((units, bits - 1, 2)), last_sems=dma((units, 2)), result_sems=dma((units, 2)),
    )
    groups = [
        len(xs), list(hbm), list(small_in), len(grads), list(outs), len(land_x), len(land_g), list(held), list(scratch)
    ]
    out_specs = [any_spec] * len(grads) + [vmem_spec] * (len(outs) - 2) + [any_spec] * (2 + len(land_x) + len(land_g))
    results = pl.pallas_call(
        functools.partial(backward_kernel, (n, bits, first_units, unit_weight), groups),
        out_shape=grads + list(outs.values()) + land_x + land_g,
        in_specs=[any_spec] * (len(xs) + len(hbm)) + [vmem_spec] * len(small_in),
        out_specs=out_specs,
        scratch_shapes=list(held.values()) + list(scratch.values()),
        compiler_params=pltpu.CompilerParams(
            collective_id=0, has_side_effects=True, vmem_limit_bytes=63 * 1024 * 1024
        ),
        name="backward",
    )(*xs, *hbm.values(), *small_in.values())
    return results[: len(grads)], dict(zip(outs, results[len(grads) :]))


def swap_pipe(array):
    devices = lax.axis_size("pipe")
    return lax.ppermute(array, "pipe", [(i, devices - 1 - i) for i in range(devices)])


def shards(
    section_inputs, cotangent, encoder_segments, decoder_segments, encoder_valid, decoder_valid,
    position_buckets, encoder_gains, encoder_shifts, encoder_qkv, encoder_out, encoder_up, encoder_down,
    position_table, decoder_gains, decoder_shifts, decoder_qkv, decoder_out, cross_query, cross_keyvalue,
    cross_out, decoder_up, decoder_down,
):
    own = section_inputs[0, :, 0]
    micro, length, width = own.shape
    pipe = lax.axis_index("pipe")
    dp = lax.axis_size("dp")
    bits = lax.axis_size("group").bit_length() - 1
    blocks = lax.axis_size("pipe") * dp
    mine = lax.dynamic_index_in_dim(own, pipe, keepdims=False)
    other = swap_pipe(lax.dynamic_index_in_dim(own, 1 - pipe, keepdims=False))
    is_encoder = pipe == 0
    x_enc = jnp.where(is_encoder, mine, other)
    x_dec = jnp.where(is_encoder, other, mine)
    weights = dict(
        e_qkv=encoder_qkv, e_out=encoder_out, e_up=encoder_up, e_down=encoder_down,
        d_qkv=decoder_qkv, d_out=decoder_out, c_query=cross_query, c_kv=cross_keyvalue,
        c_out=cross_out, d_up=decoder_up, d_down=decoder_down,
    )

    def per_row(array):
        return array.reshape(micro, length)

    small_in = dict(
        enc_seg=per_row(encoder_segments), dec_seg=per_row(decoder_segments),
        enc_valid=per_row(encoder_valid), dec_valid=per_row(decoder_valid),
        buckets=position_buckets.reshape(1, -1), enc_gains=encoder_gains, enc_shifts=encoder_shifts,
        dec_gains=decoder_gains, dec_shifts=decoder_shifts, table=position_table,
    )
    r = run_forward(dict(x_enc=x_enc, x_dec=x_dec), small_in, weights)
    f = SimpleNamespace(**r)
    xs = [f.xd_down, f.xd_up, f.xc_out, f.memory, f.xc_query, f.xd_out, f.xd_qkv, f.xe_down, f.xe_up, f.xe_out, f.xe_qkv]
    order = [decoder_down, decoder_up, cross_out, cross_keyvalue, cross_query, decoder_out, decoder_qkv,
             encoder_down, encoder_up, encoder_out, encoder_qkv]
    cut = [(w.shape[0] // blocks, w.shape[1]) for w in order]
    kept = dict(
        gd_up=f.gd_up, d2=f.d2, p_cross=f.p_cross, gc_query=f.gc_query, gc_kv=f.gc_kv, d1=f.d1, p_dec=f.p_dec,
        gd_qkv=f.gd_qkv, ge_up=f.ge_up, x1=f.x1, p_enc=f.p_enc, ge_qkv=f.ge_qkv, memory=f.memory, decoded=f.decoded,
    )
    hbm = dict(kept, cot=cotangent, x_enc=x_enc, x_dec=x_dec, **weights)
    small_back = dict(buckets=small_in["buckets"], enc_gains=encoder_gains, dec_gains=decoder_gains)
    table_shape = (position_table.shape[0] // blocks, position_table.shape[1])
    columns = [w.shape[1] for w in order]
    grads, rest = run_backward(dp, bits, xs, hbm, small_back, cut, columns, width // blocks, table_shape)
    s = SimpleNamespace(**rest)
    d_down, d_up, c_out, c_kv, c_query, d_out, d_qkv, e_down, e_up, e_out, e_qkv = (a.astype(F32) for a in grads)
    return (
        s.outputs, s.input_grads, s.enc_gains, s.enc_shifts, e_qkv, e_out, e_up, e_down, s.table,
        s.dec_gains, s.dec_shifts, d_qkv, d_out, c_query, c_kv, c_out, d_up, d_down,
    )


def solution(mesh):
    section = P("pipe", None, ("dp", "group"), None, None)
    rows = P(None, ("dp", "group"), None)
    cut_rows = P(("pipe", "dp"), None)
    cut_lanes = P(None, ("pipe", "dp"))
    return jax.shard_map(
        shards,
        mesh=mesh,
        in_specs=(section, P(None, ("dp", "group"), None, None), rows, rows, rows, rows) + (P(),) * 17,
        out_specs=(section, section, cut_lanes, cut_lanes) + (cut_rows,) * 5 + (cut_lanes, cut_lanes) + (cut_rows,) * 7,
        check_vma=False,
    )
```

```python
import functools
from types import SimpleNamespace

import jax
import jax.numpy as jnp
from jax import lax
from jax.experimental import pallas as pl
from jax.experimental.pallas import tpu as pltpu
from jax.sharding import PartitionSpec as P

HEADS = 12
MESH = pl.DeviceIdType.MESH
NEGATIVE = -1e30
BF, F32 = jnp.bfloat16, jnp.float32
GAIN_ROWS = 16


def dot(a, b):
    return jnp.dot(a, b, preferred_element_type=F32)


def dot_nt(a, b):
    return lax.dot_general(a, b, (((1,), (1,)), ((), ())), preferred_element_type=F32)


def dot_tn(a, b):
    return lax.dot_general(a, b, (((0,), (0,)), ((), ())), preferred_element_type=F32)


def row_loop(rows, chunk, body):
    def step(i, carry):
        body(pl.ds(pl.multiple_of(i * chunk, chunk), chunk))
        return carry

    lax.fori_loop(0, rows // chunk, step, 0)


def norm_stats(x):
    centre = x - jnp.mean(x, axis=-1, keepdims=True)
    spread = jnp.mean(centre * centre, axis=-1, keepdims=True)
    return centre, lax.rsqrt(spread + 1e-05)


def norm_forward(x_ref, gain, shift, n_ref):
    def body(rows):
        centre, inv = norm_stats(x_ref[rows, :].astype(F32))
        n_ref[rows, :] = (centre * inv * gain + shift).astype(BF)

    row_loop(x_ref.shape[0], 64, body)


def norm_backward(x_ref, gain, dn_ref, stream_ref, sums_ref, gain_at, shift_at):
    width = x_ref.shape[1]

    def step(i, carry):
        dgain, dshift = carry
        rows = pl.ds(pl.multiple_of(i * 64, 64), 64)
        centre, inv = norm_stats(x_ref[rows, :].astype(F32))
        hat = centre * inv
        dn = dn_ref[rows, :]
        dhat = dn * gain
        mean_one = jnp.mean(dhat, axis=-1, keepdims=True)
        mean_two = jnp.mean(dhat * hat, axis=-1, keepdims=True)
        stream_ref[rows, :] += inv * (dhat - mean_one - hat * mean_two)
        return (
            dgain + jnp.sum(dn * hat, axis=0, keepdims=True),
            dshift + jnp.sum(dn, axis=0, keepdims=True),
        )

    zero = jnp.zeros((1, width), F32)
    dgain, dshift = lax.fori_loop(0, x_ref.shape[0] // 64, step, (zero, zero))
    sums_ref[gain_at : gain_at + 1, :] = dgain
    sums_ref[shift_at : shift_at + 1, :] = dshift


def project(a_ref, w_ref, out_ref, tile=256):
    for start in range(0, w_ref.shape[1], tile):
        cols = slice(start, start + tile)
        out_ref[:, cols] = dot(a_ref[...], w_ref[:, cols]).astype(out_ref.dtype)


def project_add(a_ref, w_ref, resid_ref, out_ref, tile=256):
    for start in range(0, w_ref.shape[1], tile):
        cols = slice(start, start + tile)
        out_ref[:, cols] = (
            resid_ref[:, cols].astype(F32) + dot(a_ref[...], w_ref[:, cols])
        ).astype(out_ref.dtype)


def feed_up(n_ref, w_ref, z_ref, slope_ref, tile=512):
    for start in range(0, w_ref.shape[1], tile):
        cols = slice(start, start + tile)
        u = dot(n_ref[...], w_ref[:, cols])
        cdf = 0.5 * (1.0 + lax.erf(u * 0.7071067811865476))
        z_ref[:, cols] = (u * cdf).astype(BF)
        slope_ref[:, cols] = (cdf + u * (0.3989422804014327 * jnp.exp(-0.5 * u * u))).astype(BF)


def attend(q_ref, q_at, k_ref, k_at, v_ref, v_at, mask_ref, p_ref, o_ref, bias_ref=None):
    length = q_ref.shape[0]
    head = o_ref.shape[1] // HEADS
    pair = 2 * head
    scale = head**-0.5

    def step(i, carry):
        def cols(at):
            return pl.ds(pl.multiple_of(at + i * pair, pair), pair)

        low_half = lax.broadcasted_iota(jnp.int32, (length, pair), 1) < head
        q = q_ref[:, cols(q_at)] * jnp.asarray(scale, BF)
        k = k_ref[:, cols(k_at)]
        v = v_ref[:, cols(v_at)]
        outs = []
        for half in range(2):
            own = low_half if half == 0 else jnp.logical_not(low_half)
            s = dot_nt(jnp.where(own, q, jnp.zeros_like(q)), k) + mask_ref[...]
            if bias_ref is not None:
                wide = jnp.broadcast_to(
                    bias_ref[pl.ds(2 * i + half, 1), :], (length, 2 * length)
                )
                s = s + pltpu.roll(wide, length, 1, stride=1, stride_axis=0)[:, :length]
            e = jnp.exp(s - jnp.max(s, axis=-1, keepdims=True))
            p = (e * (1.0 / jnp.sum(e, axis=-1, keepdims=True))).astype(BF)
            p_ref[2 * i + half] = p
            outs.append(dot(p, v))
        o_ref[:, cols(0)] = jnp.where(low_half, outs[0], outs[1]).astype(BF)
        return carry

    lax.fori_loop(0, HEADS // 2, step, 0)


def attend_back(
    pairs, q_ref, q_at, k_ref, k_at, v_ref, v_at, p_ref, do_ref, diag_ref=None, flip_ref=None
):
    length = q_ref.shape[0]
    head = do_ref.shape[1] // HEADS
    pair = 2 * head
    scale = head**-0.5

    def step(i, carry):
        def cols(at):
            return pl.ds(pl.multiple_of(at + i * pair, pair), pair)

        low_half = lax.broadcasted_iota(jnp.int32, (length, pair), 1) < head
        q = q_ref[:, cols(q_at)]
        k = k_ref[:, cols(k_at)]
        v = v_ref[:, cols(v_at)]
        do = do_ref[:, cols(0)]
        dqs, dks, dvs = [], [], []
        for half in range(2):
            own = low_half if half == 0 else jnp.logical_not(low_half)
            p = p_ref[2 * i + half]
            dp = dot_nt(jnp.where(own, do, jnp.zeros_like(do)), v)
            wide_p = p.astype(F32)
            row = jnp.sum(wide_p * dp, axis=-1, keepdims=True)
            ds = (wide_p * (dp - row)).astype(BF)
            dvs.append(dot_tn(p, do))
            dqs.append(dot(ds, k))
            dks.append(dot_tn(ds, q))
            if diag_ref is not None:
                flipped = dot(flip_ref[...], ds)
                wide = jnp.concatenate([flipped, jnp.zeros_like(flipped)], axis=1)
                rolled = pltpu.roll(wide, 1, 1, stride=1, stride_axis=0)
                diag_ref[pl.ds(2 * i + half, 1), :] = jnp.sum(rolled, axis=0, keepdims=True)
        q_ref[:, cols(q_at)] = (jnp.where(low_half, dqs[0], dqs[1]) * scale).astype(BF)
        k_ref[:, cols(k_at)] = (jnp.where(low_half, dks[0], dks[1]) * scale).astype(BF)
        v_ref[:, cols(v_at)] = jnp.where(low_half, dvs[0], dvs[1]).astype(BF)
        return carry

    lax.fori_loop(pairs[0], pairs[1], step, 0)


def build_masks(eseg, dseg, evalid, dvalid, enc_ref, dec_ref, cross_ref):
    length = enc_ref.shape[0]
    shape = (length, length)
    key = lax.broadcasted_iota(jnp.int32, shape, 1)
    query = lax.broadcasted_iota(jnp.int32, shape, 0)
    eseg_key = jnp.broadcast_to(eseg.astype(F32), shape)
    dseg_key = jnp.broadcast_to(dseg.astype(F32), shape)
    eseg_query, dseg_query = eseg_key.T, dseg_key.T
    evalid_key = jnp.broadcast_to(evalid, shape) == 1
    dvalid_key = jnp.broadcast_to(dvalid, shape) == 1
    before = pltpu.roll(eseg_key, 1, 1)
    first = (key == 0) | (eseg_key != before)
    enc = (eseg_query == eseg_key) & (evalid_key | (key == query))
    dec = (dseg_query == dseg_key) & (dvalid_key | (key == query)) & (key <= query)
    cross = (dseg_query == eseg_key) & (evalid_key | first)
    enc_ref[...] = jnp.where(enc, 0.0, NEGATIVE)
    dec_ref[...] = jnp.where(dec, 0.0, NEGATIVE)
    cross_ref[...] = jnp.where(cross, 0.0, NEGATIVE)


def bucket_onehot(buckets, bucket_count):
    shape = (bucket_count, buckets.shape[1])
    return jnp.broadcast_to(buckets, shape) == lax.broadcasted_iota(jnp.int32, shape, 0)


def forward_kernel(groups, *refs):
    spaces = []
    for names in groups:
        spaces.append(SimpleNamespace(**dict(zip(names, refs))))
        refs = refs[len(names) :]
    hbm, small_in, out, v, s = spaces
    pipe = lax.axis_index("pipe")
    length, width = v.x_enc.shape
    started, pending = [], []

    def load(source, target):
        copy = pltpu.make_async_copy(source, target, s.sem_in.at[len(started)])
        copy.start()
        started.append(copy)
        return copy

    def store(source, target):
        copy = pltpu.make_async_copy(source, target, s.sem_out.at[len(pending)])
        copy.start()
        pending.append(copy)

    core = (1 - pipe, lax.axis_index("dp"), lax.axis_index("group"))
    barrier = pltpu.get_barrier_semaphore()
    pl.semaphore_signal(barrier, inc=1, device_id=core, device_id_type=MESH)
    mine, other = hbm.section_inputs.at[0, pipe, 0], hbm.section_inputs.at[0, 1 - pipe, 0]

    def keep(target):
        return pltpu.make_async_copy(mine, target, s.swap_sems.at[0])

    def give(target):
        return pltpu.make_async_remote_copy(
            src_ref=other, dst_ref=target, send_sem=s.swap_sems.at[1], recv_sem=s.swap_sems.at[2],
            device_id=core, device_id_type=MESH,
        )

    @pl.when(pipe == 0)
    def _():
        keep(v.x_enc).start()

    @pl.when(pipe == 1)
    def _():
        keep(v.x_dec).start()

    shared = []

    def share(source, target):
        part = source.shape[1] // 2
        ours = pl.ds(pl.multiple_of(pipe * part, 128), part)
        theirs = pl.ds(pl.multiple_of((1 - pipe) * part, 128), part)
        store(source.at[:, ours], target.at[0:length])
        copy = pltpu.make_async_remote_copy(
            src_ref=source.at[:, theirs], dst_ref=target.at[length : 2 * length],
            send_sem=s.share_sent.at[len(shared)], recv_sem=s.share_got.at[len(shared)],
            device_id=core, device_id_type=MESH,
        )
        copy.start()
        shared.append(copy)

    get_e_qkv = load(hbm.e_qkv, s.e_qkv)
    get_e_out = load(hbm.e_out, s.e_out)
    get_e_up = load(hbm.e_up, s.up)
    get_e_down = load(hbm.e_down, s.down)
    get_d_qkv = load(hbm.d_qkv, s.d_qkv)
    get_d_out = load(hbm.d_out, s.d_out)
    get_c_query = load(hbm.c_query, s.c_query)
    get_c_kv = load(hbm.c_kv, s.c_kv)
    get_c_out = load(hbm.c_out, s.c_out)
    pl.semaphore_wait(barrier, 1)

    @pl.when(pipe == 0)
    def _():
        give(v.x_enc).start()

    @pl.when(pipe == 1)
    def _():
        give(v.x_dec).start()


    build_masks(
        small_in.enc_seg[pipe], small_in.dec_seg[pipe], small_in.enc_valid[pipe], small_in.dec_valid[pipe],
        s.mask_enc, s.mask_dec, s.mask_cross,
    )
    buckets = small_in.buckets[...]
    s.bias[0:HEADS, :] = dot(small_in.table[...], bucket_onehot(buckets, small_in.table.shape[1]).astype(BF))
    def at(ref, row):
        return ref[row : row + 1, :].astype(F32)

    enc_gains, enc_shifts = small_in.enc_gains, small_in.enc_shifts
    dec_gains, dec_shifts = small_in.dec_gains, small_in.dec_shifts

    @pl.when(pipe == 0)
    def _():
        keep(v.x_enc).wait()

    @pl.when(pipe == 1)
    def _():
        give(v.x_enc).wait_recv()

    store(v.x_enc, out.x_enc)
    norm_forward(v.x_enc, at(enc_gains, 0), at(enc_shifts, 0), v.xe_qkv)
    share(v.xe_qkv, out.xe_qkv)
    get_e_qkv.wait()
    project(v.xe_qkv, s.e_qkv, v.ge_qkv)
    attend(v.ge_qkv, 0, v.ge_qkv, width, v.ge_qkv, 2 * width, s.mask_enc, v.p_enc, v.xe_out, s.bias)
    store(v.ge_qkv, out.ge_qkv)
    store(v.p_enc, out.p_enc)
    share(v.xe_out, out.xe_out)
    get_e_out.wait()
    project_add(v.xe_out, s.e_out, v.x_enc, v.x1)
    store(v.x1, out.x1)
    norm_forward(v.x1, at(enc_gains, 1), at(enc_shifts, 1), v.xe_up)
    share(v.xe_up, out.xe_up)
    get_e_up.wait()
    feed_up(v.xe_up, s.up, v.xe_down, v.ge_up)
    get_d_up = load(hbm.d_up, s.up)
    share(v.xe_down, out.xe_down)
    store(v.ge_up, out.ge_up)
    get_e_down.wait()
    project_add(v.xe_down, s.down, v.x1, v.memory)
    get_d_down = load(hbm.d_down, s.down)
    share(v.memory, out.memory_cut)

    @pl.when(pipe == 0)
    def _():
        give(v.x_dec).wait_recv()

    @pl.when(pipe == 1)
    def _():
        keep(v.x_dec).wait()

    store(v.x_dec, out.x_dec)
    norm_forward(v.x_dec, at(dec_gains, 0), at(dec_shifts, 0), v.xd_qkv)
    share(v.xd_qkv, out.xd_qkv)
    get_d_qkv.wait()
    project(v.xd_qkv, s.d_qkv, v.gd_qkv)
    attend(v.gd_qkv, 0, v.gd_qkv, width, v.gd_qkv, 2 * width, s.mask_dec, v.p_dec, v.xd_out)
    share(v.xd_out, out.xd_out)
    store(v.gd_qkv, out.gd_qkv)
    store(v.p_dec, out.p_dec)
    get_d_out.wait()
    project_add(v.xd_out, s.d_out, v.x_dec, v.d1)
    store(v.d1, out.d1)
    norm_forward(v.d1, at(dec_gains, 1), at(dec_shifts, 1), v.xc_query)
    share(v.xc_query, out.xc_query)
    get_c_query.wait()
    project(v.xc_query, s.c_query, v.gc_query)
    get_c_kv.wait()
    project(v.memory, s.c_kv, v.gc_kv)
    attend(v.gc_query, 0, v.gc_kv, 0, v.gc_kv, width, s.mask_cross, v.p_cross, v.xc_out)
    share(v.xc_out, out.xc_out)
    store(v.gc_query, out.gc_query)
    store(v.gc_kv, out.gc_kv)
    store(v.p_cross, out.p_cross)
    get_c_out.wait()
    project_add(v.xc_out, s.c_out, v.d1, v.d2)
    store(v.d2, out.d2)
    norm_forward(v.d2, at(dec_gains, 2), at(dec_shifts, 2), v.xd_up)
    share(v.xd_up, out.xd_up)
    get_d_up.wait()
    feed_up(v.xd_up, s.up, v.xd_down, v.gd_up)
    share(v.xd_down, out.xd_down)
    store(v.gd_up, out.gd_up)
    get_d_down.wait()
    project_add(v.xd_down, s.down, v.d2, v.decoded)

    def section(layer, ref):
        @pl.when(pipe == layer)
        def _():
            pltpu.make_async_copy(ref, out.outputs.at[0, pipe, 0], s.section_sems.at[0]).start()

        @pl.when(pipe != layer)
        def _():
            pltpu.make_async_remote_copy(
                src_ref=ref, dst_ref=out.outputs.at[0, pipe, 0], send_sem=s.section_sems.at[1],
                recv_sem=s.section_sems.at[2], device_id=core, device_id_type=MESH,
            ).start()

    section(0, v.memory)
    section(1, v.decoded)

    give(v.x_enc).wait_send()
    pltpu.make_async_copy(v.memory, out.outputs.at[0, pipe, 0], s.section_sems.at[0]).wait()
    pltpu.make_async_remote_copy(
        src_ref=v.memory, dst_ref=out.outputs.at[0, 1 - pipe, 0], send_sem=s.section_sems.at[1],
        recv_sem=s.section_sems.at[2], device_id=core, device_id_type=MESH,
    ).wait()
    for copy in pending + shared:
        copy.wait()


def run_forward(section_inputs, small_in, weights):
    unused, micro, unused, length, width = section_inputs.shape
    hidden = weights["e_up"].shape[1]
    hbm = dict(section_inputs=section_inputs, **weights)
    any_spec = pl.BlockSpec(memory_space=pl.ANY)
    vmem_spec = pl.BlockSpec(memory_space=pltpu.VMEM)
    columns = dict(
        ge_qkv=3 * width, ge_up=hidden, gd_qkv=3 * width, gc_query=width, gc_kv=2 * width, gd_up=hidden,
        x_enc=width, x_dec=width,
    )
    inputs = dict(
        xe_qkv=width, xe_out=width, xe_up=width, xe_down=hidden, xd_qkv=width, xd_out=width, xc_query=width,
        xc_out=width, xd_up=width, xd_down=hidden,
    )
    outs = {name: jax.ShapeDtypeStruct((length, n), BF) for name, n in columns.items()}
    probabilities = jax.ShapeDtypeStruct((HEADS, length, length), BF)
    rows = jax.ShapeDtypeStruct((length, width), F32)
    outs.update(p_enc=probabilities, p_dec=probabilities, p_cross=probabilities, x1=rows, d1=rows, d2=rows)
    held = {name: pltpu.VMEM(shape.shape, shape.dtype) for name, shape in outs.items()}
    held.update({name: pltpu.VMEM((length, n), BF) for name, n in inputs.items()})
    held.update(memory=pltpu.VMEM((length, width), BF), decoded=pltpu.VMEM((length, width), BF))
    outs.update({name: jax.ShapeDtypeStruct((2 * length, n // 2), BF) for name, n in inputs.items()})
    outs.update(outputs=jax.ShapeDtypeStruct((1, micro, 1, length, width), BF))
    outs.update(memory_cut=jax.ShapeDtypeStruct((2 * length, width // 2), BF))
    square = pltpu.VMEM((length, length), F32)
    scratch = {
        name: pltpu.VMEM(w.shape, BF) for name, w in weights.items() if hidden not in w.shape
    }
    scratch.update(
        up=pltpu.VMEM((width, hidden), BF), down=pltpu.VMEM((hidden, width), BF),
        mask_enc=square, mask_dec=square, mask_cross=square, bias=pltpu.VMEM((16, 2 * length), F32),
        section_sems=pltpu.SemaphoreType.DMA((3,)), swap_sems=pltpu.SemaphoreType.DMA((3,)), share_sent=pltpu.SemaphoreType.DMA((len(inputs) + 1,)),
        share_got=pltpu.SemaphoreType.DMA((len(inputs) + 1,)), sem_in=pltpu.SemaphoreType.DMA((16,)), sem_out=pltpu.SemaphoreType.DMA((len(outs),)),
    )
    groups = [list(part) for part in (hbm, small_in, outs, held, scratch)]
    results = pl.pallas_call(
        functools.partial(forward_kernel, groups),
        out_shape=list(outs.values()),
        in_specs=[any_spec] * len(hbm) + [vmem_spec] * len(small_in),
        out_specs=[any_spec] * len(outs),
        scratch_shapes=list(held.values()) + list(scratch.values()),
        compiler_params=pltpu.CompilerParams(
            collective_id=1, has_side_effects=True, vmem_limit_bytes=63 * 1024 * 1024
        ),
        name="forward",
    )(*hbm.values(), *small_in.values())
    return dict(zip(outs, results))


def step_order(work, small_after, units, n, bits, window=3):
    big, delay, cost = 6.6, 2.0, 0.5
    small = big / n
    sides, line = [0.0, 0.0], [0.0] * n
    waiting, steps = [], []
    flying = [0, 0]
    clock, made, done = 0.0, 0, 0

    def message(free, at, start, size):
        free[at] = max(free[at], start) + size
        return free[at] + delay

    while done < len(work) or waiting:
        ready = [event for event in waiting if event[0] <= clock]
        if ready:
            event = min(ready)
            waiting.remove(event)
            unused, kind, unit, at = event
            steps.append((kind, unit, at))
            clock += cost
            first, other = unit % 2, 1 - unit % 2
            if kind == 1:
                flying[first] -= 1
                waiting.append((message(line, 1, clock, (n - 1) * small), 2 if n > 2 else 3, unit, 1))
            elif kind == 2:
                arrival = message(line, at + 1, clock, (n - 1 - at) * small)
                waiting.append((arrival, 2 if at + 1 < n - 1 else 3, unit, at + 1))
            elif kind == 3:
                waiting.append((message(sides, other, clock, small), 4, unit, 0))
            elif kind == 4 and at + 2 < bits:
                waiting.append((message(sides, other, clock, small), 4, unit, at + 1))
            elif kind == 4:
                waiting.append((message(sides, first, clock, small), 5, unit, 0))
            elif kind == 6 and at + 1 < bits + n:
                waiting.append((clock + 2 * delay, 6, 0, at + 1))
        elif done < len(work) and (not work[done][1] or flying[made % 2] < window):
            clock += work[done][0]
            steps.append((0, done, 0))
            if work[done][1]:
                waiting.append((message(sides, made % 2, clock, big), 1, made, 0))
                flying[made % 2] += 1
                made += 1
            if done == small_after:
                waiting.append((clock + delay, 6, 0, 0))
            done += 1
        else:
            clock = min(waiting)[0]
    return steps


def backward_kernel(tables, groups, *refs):
    spaces = []
    for names in groups:
        if isinstance(names, int):
            spaces.append(refs[:names])
            refs = refs[names:]
        else:
            spaces.append(SimpleNamespace(**dict(zip(names, refs))))
            refs = refs[len(names) :]
    xs, hbm, small_in, grads, out, land_g, v, s = spaces
    n, bits, first_units, unit_weight = tables
    p, d, g = lax.axis_index("pipe"), lax.axis_index("dp"), lax.axis_index("group")
    units = len(unit_weight)
    length, width = v.stream.shape
    half = width // 2
    block = width // (2 * n)
    blocks = 2 * n
    gs = [
        v.cot, v.gd_up, v.gc_out, v.gc_kv, v.gc_query, v.gd_out, v.gd_qkv, v.ge_down, v.ge_up, v.ge_out, v.ge_qkv
    ]
    d_down, d_up, c_out, c_kv, c_query, d_out, d_qkv, e_down, e_up, e_out, e_qkv = range(len(gs))

    def bit_of(bit):
        return (g // 2**bit) % 2

    def across(bit):
        return (p, d, g + (1 - 2 * bit_of(bit)) * 2**bit)

    core = (1 - p, d, g)
    above, below = (p, d + 1, g), (p, d - 1, g)

    loads = []

    def load(source, target):
        copy = pltpu.make_async_copy(source, target, s.load_sems.at[len(loads)])
        copy.start()
        loads.append(copy)
        return copy

    get_cot = load(hbm.cot.at[p, 0], v.cot)

    def tiles_of(at):
        return xs[at].shape[1] // half

    fetched = {}

    def fetch_x(at):
        for tile in range(tiles_of(at)):
            copy = pltpu.make_async_copy(
                xs[at].at[:, tile * half : (tile + 1) * half], s.x_stage.at[tile], s.stage_sems.at[tile]
            )
            copy.start()
            fetched.setdefault(at, []).append(copy)

    def fetch_g(at):
        if at > 0:
            g_swaps[at].wait_recv()
        source = hbm.cot.at[1 - p, 0] if at == 0 else land_g[at - 1]
        copy = pltpu.make_async_copy(
            source, s.g_stage.at[:, 0 : source.shape[1]], s.stage_sems.at[s.stage_sems.shape[0] - 1]
        )
        copy.start()
        fetched[at].append(copy)

    fetch_x(d_down)
    fetch_g(d_down)

    slots, side, reach = s.stream_w.shape
    chunks = []
    for ref in (
        hbm.d_down, hbm.d_up, hbm.c_out, hbm.c_kv, hbm.c_query, hbm.d_out, hbm.d_qkv, hbm.e_down, hbm.e_up,
        hbm.e_out, hbm.e_qkv,
    ):
        columns = ref.shape[1]
        together = reach // columns
        for first in range(0, ref.shape[0], together * side):
            last = min(ref.shape[0], first + together * side)
            chunks.append([(ref.at[row : row + side, :], (row - first) // side * columns, columns) for row in range(first, last, side)])
    walked = [0]

    def chunk_copies(at):
        return [
            pltpu.make_async_copy(
                source, s.stream_w.at[at % slots, :, start : start + columns], s.stream_sems.at[at % slots, i]
            )
            for i, (source, start, columns) in enumerate(chunks[at])
        ]

    def start_chunk(at):
        if at < len(chunks):
            for copy in chunk_copies(at):
                copy.start()

    for at in range(slots):
        start_chunk(at)

    def next_rows(g_ref, put, row):
        at = walked[0]
        walked[0] += 1
        for copy in chunk_copies(at):
            copy.wait()
        for unused, start, columns in chunks[at]:
            put(slice(row, row + side), dot_nt(g_ref[...], s.stream_w[at % slots, :, start : start + columns]))
            row += side
        start_chunk(at + slots)
        return row

    def back_through(g_ref, out_ref):
        def put(cols, part):
            out_ref[:, cols] = part.astype(out_ref.dtype)

        row = 0
        while row < out_ref.shape[1]:
            row = next_rows(g_ref, put, row)

    def back_through_feed(g_ref, slope_ref, start, stop):
        def put(cols, part):
            slope_ref[:, cols] = (part * slope_ref[:, cols].astype(F32)).astype(BF)

        row = start
        while row < stop:
            row = next_rows(g_ref, put, row)

    get_gd_up = load(hbm.gd_up, v.gd_up)
    get_d2 = load(hbm.d2, v.d2)
    get_p = [load(hbm.p_cross, v.p)]
    get_gc_query = load(hbm.gc_query, v.gc_query)
    get_gc_kv = load(hbm.gc_kv, v.gc_kv)
    get_d1 = load(hbm.d1, v.d1)
    get_gd_qkv = load(hbm.gd_qkv, v.gd_qkv)
    get_x_dec = load(hbm.x_dec, v.x_dec)
    get_ge_up = load(hbm.ge_up, v.ge_up)
    get_ge_qkv = load(hbm.ge_qkv, v.ge_qkv)

    barrier = pltpu.get_barrier_semaphore()
    pl.semaphore_signal(barrier, inc=1, device_id=core, device_id_type=MESH)
    for bit in range(bits):
        pl.semaphore_signal(barrier, inc=1, device_id=across(bit), device_id_type=MESH)

    @pl.when(d > 0)
    def _():
        pl.semaphore_signal(barrier, inc=1, device_id=below, device_id_type=MESH)

    @pl.when(d < n - 1)
    def _():
        pl.semaphore_signal(barrier, inc=1, device_id=above, device_id_type=MESH)

    @pl.when((d > 0) & (d < n - 1))
    def _():
        pl.semaphore_wait(barrier, 3 + bits)

    @pl.when((d == 0) | (d == n - 1))
    def _():
        pl.semaphore_wait(barrier, 2 + bits)

    def remote(source, target, send_sem, recv_sem, device):
        return pltpu.make_async_remote_copy(
            src_ref=source, dst_ref=target, send_sem=send_sem, recv_sem=recv_sem,
            device_id=device, device_id_type=MESH,
        )

    sent = []

    def send(copy):
        copy.start()
        sent.append(copy.wait_send)
        return copy

    g_swaps = {}

    def swap_g(at):
        g_swaps[at] = send(
            remote(gs[at], land_g[at - 1], s.swap_sent.at[at], s.swap_got.at[at], core)
        )

    def input_grad(layer, ref):
        @pl.when(p == layer)
        def _():
            pltpu.make_async_copy(ref, out.input_grads.at[0, p, 0], s.section_kept).start()

        @pl.when(p != layer)
        def _():
            remote(ref, out.input_grads.at[0, p, 0], s.section_sent, s.section_got, core).start()

    section_kept = pltpu.make_async_copy(v.do, out.input_grads.at[0, p, 0], s.section_kept)
    section_given = remote(v.do, out.input_grads.at[0, 1 - p, 0], s.section_sent, s.section_got, core)

    def first_bit(unit):
        return 0 if unit % 2 == 0 else bits - 1

    rooms = s.given.shape[0]

    def first_copy(unit):
        return remote(
            s.given.at[unit % rooms], s.taken.at[unit], s.first_sent.at[unit], s.first_got.at[unit],
            across(first_bit(unit)),
        )

    def product(at, tile, cols):
        value = dot(s.factor[tile, :, 0:length], gs[at][:, cols])
        return (value + dot(s.factor[tile, :, length : 2 * length], s.g_stage[:, cols])).astype(BF)

    def room_free(unit):
        if unit >= rooms:
            first_copy(unit - rooms).wait_send()

    def make(unit):
        at = unit_weight[unit]
        base = first_units[at]
        tiles = tiles_of(at)
        if unit == base:
            if at == 0:
                get_cot.wait()
            for copy in fetched.pop(at):
                copy.wait()
            for tile in range(tiles):
                s.factor[tile] = s.x_stage[tile].T
        if tiles == 1:
            room_free(unit)
            mine = bit_of(first_bit(unit))
            column = (unit - base) * width
            given = product(at, 0, pl.ds(pl.multiple_of(column + (1 - mine) * half, 128), half))
            for i in range(n):
                s.given[unit % rooms, i] = given[i * block : (i + 1) * block]
            first_copy(unit).start()
            kept = product(at, 0, pl.ds(pl.multiple_of(column + mine * half, 128), half))
            for i in range(n):
                s.kept[unit, i] = kept[i * block : (i + 1) * block]
            return
        if unit == base:
            for i in range(tiles):
                room_free(unit + i)
            for tile in range(tiles):
                for which in range(2):
                    split_rows(base, tiles, tile, which, product(at, tile, slice(which * half, (which + 1) * half)))
        first_copy(unit).start()

    def split_rows(base, tiles, tile, which, value):
        for i in range(n):
            unit = base + (tile * n + i) % tiles
            at = (tile * n + i) // tiles
            mine = bit_of(first_bit(unit))
            rows = value[i * block : (i + 1) * block]

            @pl.when(mine == which)
            def _(unit=unit, at=at, rows=rows):
                s.kept[unit, at] = rows

            @pl.when(mine != which)
            def _(unit=unit, at=at, rows=rows):
                s.given[unit % rooms, at] = rows

    def add(target, index, source, source_index):
        target[index] = (target[index].astype(F32) + source[source_index].astype(F32)).astype(target.dtype)

    def up_copy(line, dd):
        source = line.kept.at[1:n] if dd == 0 else line.passed.at[dd + 2 : n + 1]
        return remote(source, line.passed.at[dd + 2 : n + 1], line.sems.at[0], line.sems.at[1], above)

    def down_copy(line, dd):
        source = line.kept.at[0 : n - 1] if dd == n - 1 else line.passed.at[0:dd]
        return remote(source, line.passed.at[0:dd], line.sems.at[2], line.sems.at[3], below)

    def line_start(line):
        @pl.when(d == 0)
        def _():
            up_copy(line, 0).start()

        @pl.when(d == n - 1)
        def _():
            down_copy(line, n - 1).start()

    def line_hop(line, hop):
        @pl.when(d == hop)
        def _():
            up_copy(line, hop - 1).wait_recv()
            for i in range(hop + 1, n):
                add(line.passed, i + 1, line.kept, i)
            up_copy(line, hop).start()

        @pl.when(d == n - 1 - hop)
        def _():
            down_copy(line, n - hop).wait_recv()
            for i in range(n - 1 - hop):
                add(line.passed, i, line.kept, i)
            down_copy(line, n - 1 - hop).start()

    def line_end(line):
        @pl.when(d == n - 1)
        def _():
            up_copy(line, n - 2).wait_recv()
            line.kept[n - 1] = (
                line.kept[n - 1].astype(F32) + line.passed[n].astype(F32)
            ).astype(line.kept.dtype)

        @pl.when(d == 0)
        def _():
            down_copy(line, 1).wait_recv()
            line.kept[0] = (line.kept[0].astype(F32) + line.passed[0].astype(F32)).astype(line.kept.dtype)

        for dd in range(1, n - 1):

            @pl.when(d == dd)
            def _(dd=dd):
                line.kept[dd] = (
                    line.kept[dd].astype(F32) + line.passed[dd + 1].astype(F32) + line.passed[dd].astype(F32)
                ).astype(line.kept.dtype)

    def line_sent(line):
        for dd in range(n):

            @pl.when(d == dd)
            def _(dd=dd):
                if dd < n - 1:
                    up_copy(line, dd).wait_send()
                if dd > 0:
                    down_copy(line, dd).wait_send()

    def line_of(unit):
        return SimpleNamespace(
            kept=s.kept.at[unit], passed=s.passed.at[unit], sems=s.line_sems.at[unit]
        )

    def rest_bits(unit):
        return [bit for bit in range(bits) if bit != first_bit(unit)]

    def rest_copy(unit, at):
        source = s.kept.at[unit, d] if at == 0 else s.rest_sum.at[unit, at - 1]
        return remote(
            source, s.rest_got.at[unit, at], s.rest_sems.at[unit, at, 0], s.rest_sems.at[unit, at, 1],
            across(rest_bits(unit)[at]),
        )

    def last_copy(unit):
        return remote(
            s.rest_sum.at[unit, bits - 2], s.last_got.at[unit], s.last_sems.at[unit, 0], s.last_sems.at[unit, 1],
            across(first_bit(unit)),
        )

    def result_at(unit, which):
        at = unit_weight[unit]
        k = unit - first_units[at]
        target = grads[at]
        if tiles_of(at) == 1:
            return target.at[:, pl.ds(pl.multiple_of(k * width + which * half, 128), half)]
        return target.at[pl.ds(k * block, block), pl.ds(pl.multiple_of(which * half, 128), half)]

    def own_result(unit):
        return pltpu.make_async_copy(
            s.rest_sum.at[unit, bits - 2], result_at(unit, bit_of(first_bit(unit))), s.result_sems.at[unit, 0]
        )

    def got_result(unit):
        return pltpu.make_async_copy(
            s.last_got.at[unit], result_at(unit, 1 - bit_of(first_bit(unit))), s.result_sems.at[unit, 1]
        )

    small_line = SimpleNamespace(kept=s.small_kept, passed=s.small_passed, sems=s.small_line)
    small_swap = remote(
        s.small.at[pl.ds((1 - p) * n, n)], s.small_core, s.small_sent.at[0], s.small_got.at[0], core
    )

    def small_copy(bit):
        return remote(
            s.small_held.at[bit], s.small_group.at[bit], s.small_sent.at[1 + bit], s.small_got.at[1 + bit], across(bit)
        )

    def small_step(at):
        if at == 0:
            small_swap.wait_recv()
            s.small_kept[...] = s.small[pl.ds(p * n, n)] + s.small_core[...]
        elif at <= bits:
            small_copy(at - 1).wait_recv()
            s.small_kept[...] += s.small_group[at - 1]
        if at < bits:
            s.small_held[at] = s.small_kept[...]
            small_copy(at).start()
        elif at == bits:
            line_start(small_line)
        elif at < bits + n - 1:
            line_hop(small_line, at - bits)
        else:
            line_end(small_line)
            total = s.small_kept[d]
            lanes = out.enc_gains.shape[1]
            for ref, row in (
                (out.enc_gains, 0), (out.enc_shifts, 2), (out.dec_gains, 4), (out.dec_shifts, 7)
            ):
                ref[...] = total[row : row + ref.shape[0], 0:lanes]
            out.table[...] = total[GAIN_ROWS:].T[0:HEADS, 0 : out.table.shape[1]]

    def gain(ref, row):
        return ref[row : row + 1, :].astype(F32)

    enc_gains, dec_gains = small_in.enc_gains, small_in.dec_gains
    pairs = HEADS // 2
    work = []

    def piece(time, body, *args):
        work.append((time, False, functools.partial(body, *args)))

    def make_all(at):
        count = max(tiles_of(at), gs[at].shape[1] // width)
        for i in range(count):
            first_time = 1.2 if tiles_of(at) == 1 else 1.1 * tiles_of(at)
            later = 0.8 if tiles_of(at) == 1 else 0.1
            work.append((first_time if i == 0 else later, True, functools.partial(make, first_units[at] + i)))

    def start_feed(g_ref, slope_ref, get):
        get.wait()
        back_through_feed(g_ref, slope_ref, 0, slope_ref.shape[1] // 3)

    def end_feed(g_ref, slope_ref, at):
        back_through_feed(g_ref, slope_ref, slope_ref.shape[1] // 3, slope_ref.shape[1])
        swap_g(at)

    get_late = []

    def residual(x_ref, get, gain_row, gain_at, shift_at, low_ref):
        (get_late.pop(0) if get is None else get).wait()
        norm_backward(x_ref, gain_row, v.dn, v.stream, s.sums, gain_at, shift_at)
        low_ref[...] = v.stream[...].astype(BF)

    def residual_swap(x_ref, get, gain_row, gain_at, shift_at, low_ref, at):
        residual(x_ref, get, gain_row, gain_at, shift_at, low_ref)
        if x_ref is v.d2 and at == c_out:
            get_late.append(load(hbm.x1, v.d2))
        swap_g(at)
        back_through(low_ref, v.do)

    def begin():
        s.sums[...] = jnp.zeros_like(s.sums)
        v.stream[...] = v.cot[...].astype(F32)
        start_feed(v.cot, v.gd_up, get_gd_up)

    def cross_part(first, last):
        if first == 0:
            get_p[0].wait()
            get_gc_query.wait()
            get_gc_kv.wait()
        attend_back((first, last), v.gc_query, 0, v.gc_kv, 0, v.gc_kv, width, v.p, v.do)
        if last == pairs:
            get_p.append(load(hbm.p_dec, v.p))
            swap_g(c_kv)
            swap_g(c_query)

    def dec_part(first, last):
        if first == 0:
            get_p[1].wait()
            get_gd_qkv.wait()
        attend_back((first, last), v.gd_qkv, 0, v.gd_qkv, width, v.gd_qkv, 2 * width, v.p, v.do)
        if last == pairs:
            get_p.append(load(hbm.p_enc, v.p))
            swap_g(d_qkv)

    def enc_part(first, last):
        if first == 0:
            get_p[2].wait()
            get_ge_qkv.wait()
            s.diag[...] = jnp.zeros_like(s.diag)
            flip_shape = (length, length)
            s.flip[...] = (
                lax.broadcasted_iota(jnp.int32, flip_shape, 0) + lax.broadcasted_iota(jnp.int32, flip_shape, 1)
                == length - 1
            ).astype(BF)
        attend_back(
            (first, last), v.ge_qkv, 0, v.ge_qkv, width, v.ge_qkv, 2 * width, v.p, v.do, s.diag, s.flip
        )
        if last == pairs:
            swap_g(e_qkv)

    def memory_part():
        back_through(v.gc_kv, v.ge_down)
        swap_g(e_down)

    def dec_end():
        residual(v.x_dec, get_x_dec, gain(dec_gains, 0), 4, 7, v.dx_dec)
        input_grad(1, v.dx_dec)
        get_late.append(load(hbm.x_enc, v.x_dec))
        v.stream[...] = v.ge_down[...].astype(F32)

    def small_part():
        residual(v.x_dec, None, gain(enc_gains, 0), 0, 2, v.do)
        input_grad(0, v.do)
        buckets = small_in.buckets[...]
        bucket_count = out.table.shape[1] * blocks
        onehot = bucket_onehot(buckets, bucket_count).astype(BF)
        rest = s.diag[...]
        table_grad = jnp.zeros((bucket_count, rest.shape[0]), F32)
        for unused in range(3):
            part = rest.astype(BF)
            rest = rest - part.astype(F32)
            table_grad = table_grad + dot_nt(onehot, part)
        s.small[...] = jnp.zeros_like(s.small)
        lanes = width // blocks
        table_rows = bucket_count // blocks
        for at in range(blocks):
            s.small[at, 0:GAIN_ROWS, 0:lanes] = s.sums[:, at * lanes : (at + 1) * lanes]
            s.small[at, GAIN_ROWS : GAIN_ROWS + table_rows, 0 : rest.shape[0]] = table_grad[
                at * table_rows : (at + 1) * table_rows, :
            ]
        small_swap.start()

    make_all(d_down)
    piece(0.2, fetch_x, d_up)
    piece(1.2, begin)
    piece(1.8, end_feed, v.cot, v.gd_up, d_up)
    piece(1.8, back_through, v.gd_up, v.dn)
    piece(0.2, fetch_g, d_up)
    piece(1.6, residual_swap, v.d2, get_d2, gain(dec_gains, 2), 6, 9, v.gc_out, c_out)
    make_all(d_up)
    piece(0.2, fetch_x, c_out)
    piece(2.5, cross_part, 0, pairs // 2)
    piece(0.2, fetch_g, c_out)
    piece(2.5, cross_part, pairs // 2, pairs)
    make_all(c_out)
    piece(0.2, fetch_x, c_kv)
    piece(1.0, memory_part)
    piece(0.2, fetch_g, c_kv)
    piece(0.5, back_through, v.gc_query, v.dn)
    make_all(c_kv)
    piece(0.2, fetch_x, c_query)
    piece(0.2, fetch_g, c_query)
    piece(1.6, residual_swap, v.d1, get_d1, gain(dec_gains, 1), 5, 8, v.gd_out, d_out)
    make_all(c_query)
    piece(0.2, fetch_x, d_out)
    piece(2.5, dec_part, 0, pairs // 2)
    piece(0.2, fetch_g, d_out)
    piece(2.5, dec_part, pairs // 2, pairs)
    make_all(d_out)
    piece(0.2, fetch_x, d_qkv)
    piece(1.4, back_through, v.gd_qkv, v.dn)
    piece(0.2, fetch_g, d_qkv)
    piece(1.0, dec_end)
    piece(1.2, start_feed, v.ge_down, v.ge_up, get_ge_up)
    make_all(d_qkv)
    piece(0.2, fetch_x, e_down)
    piece(0.2, fetch_g, e_down)
    piece(1.8, end_feed, v.ge_down, v.ge_up, e_up)
    make_all(e_down)
    piece(0.2, fetch_x, e_up)
    piece(1.8, back_through, v.ge_up, v.dn)
    piece(0.2, fetch_g, e_up)
    piece(1.6, residual_swap, v.d2, None, gain(enc_gains, 1), 1, 3, v.ge_out, e_out)
    make_all(e_up)
    piece(0.2, fetch_x, e_out)
    piece(3.0, enc_part, 0, pairs // 2)
    piece(0.2, fetch_g, e_out)
    piece(3.0, enc_part, pairs // 2, pairs)
    make_all(e_out)
    piece(0.2, fetch_x, e_qkv)
    piece(1.4, back_through, v.ge_qkv, v.dn)
    piece(0.2, fetch_g, e_qkv)
    small_after = len(work)
    piece(2.0, small_part)
    make_all(e_qkv)

    def take_step(kind, unit, at):
        if kind == 0:
            work[unit][2]()
        elif kind == 1:
            first_copy(unit).wait_recv()

            def body(i, carry):
                s.kept[unit, i] = (s.kept[unit, i].astype(F32) + s.taken[unit, i].astype(F32)).astype(BF)
                return carry

            lax.fori_loop(0, n, body, 0)
            line_start(line_of(unit))
        elif kind == 2:
            line_hop(line_of(unit), at)
        elif kind == 3:
            line_end(line_of(unit))
            rest_copy(unit, 0).start()
        elif kind == 4:
            rest_copy(unit, at).wait_recv()
            before = s.kept[unit, d] if at == 0 else s.rest_sum[unit, at - 1]
            s.rest_sum[unit, at] = (before.astype(F32) + s.rest_got[unit, at].astype(F32)).astype(BF)
            if at < bits - 2:
                rest_copy(unit, at + 1).start()
            else:
                last_copy(unit).start()
                own_result(unit).start()
        elif kind == 5:
            last_copy(unit).wait_recv()
            got_result(unit).start()
        else:
            small_step(at)

    plan = [(time, makes) for time, makes, unused in work]
    for step in step_order(plan, small_after, units, n, bits):
        take_step(*step)

    for unit in range(units):
        if unit + rooms >= units:
            first_copy(unit).wait_send()
        line_sent(line_of(unit))
        for at in range(bits - 1):
            rest_copy(unit, at).wait_send()
        last_copy(unit).wait_send()
        own_result(unit).wait()
        got_result(unit).wait()
    small_swap.wait_send()
    for bit in range(bits):
        small_copy(bit).wait_send()
    line_sent(small_line)
    for wait in sent:
        wait()
    section_kept.wait()
    section_given.wait()


def run_backward(n, bits, xs, hbm, small_in, weights_out, g_columns, lanes, table_shape):
    length, width = hbm["d1"].shape
    half = width // 2
    block = width // (2 * n)
    first_units, unit_weight = [], []
    for at, x in enumerate(xs):
        first_units.append(len(unit_weight))
        unit_weight += [at] * max(x.shape[1] // half, g_columns[at] // width)
    units = len(unit_weight)
    any_spec = pl.BlockSpec(memory_space=pl.ANY)
    vmem_spec = pl.BlockSpec(memory_space=pltpu.VMEM)
    section = jax.ShapeDtypeStruct((1, hbm["cot"].shape[0], 1, length, width), BF)
    grads = [jax.ShapeDtypeStruct(shape, BF) for shape in weights_out]
    outs = dict(
        enc_gains=(2, lanes), enc_shifts=(2, lanes), dec_gains=(3, lanes), dec_shifts=(3, lanes), table=table_shape
    )
    outs = {name: jax.ShapeDtypeStruct(shape, F32) for name, shape in outs.items()}
    outs.update(input_grads=section)
    land_g = [jax.ShapeDtypeStruct((length, columns), BF) for columns in g_columns[1:]]
    most = max(x.shape[1] for x in xs) // half
    small_rows = -(-(GAIN_ROWS + table_shape[1]) // 16) * 16
    dma = pltpu.SemaphoreType.DMA
    small_all = pltpu.VMEM((n, small_rows, 128), F32)
    low = pltpu.VMEM((length, width), BF)
    wide = pltpu.VMEM((length, width), F32)
    held = dict(
        cot=low, x_dec=low, gc_query=low, gc_out=low, gd_out=low, ge_out=low, ge_down=low, do=low,
        dx_dec=low, d2=wide, d1=wide, stream=wide, dn=wide,
        gd_up=pltpu.VMEM((length, most * width), BF), ge_up=pltpu.VMEM((length, most * width), BF),
        gd_qkv=pltpu.VMEM((length, 3 * width), BF), ge_qkv=pltpu.VMEM((length, 3 * width), BF),
        gc_kv=pltpu.VMEM((length, 2 * width), BF), p=pltpu.VMEM((HEADS, length, length), BF),
    )
    scratch = dict(
        stream_w=pltpu.VMEM((3, 256, most * width), BF),
        x_stage=pltpu.VMEM((most, 2 * length, half), BF),
        g_stage=pltpu.VMEM((length, most * width), BF),
        factor=pltpu.VMEM((most, half, 2 * length), BF),
        kept=pltpu.VMEM((units, n, block, half), BF),
        given=pltpu.VMEM((10, n, block, half), BF),
        taken=pltpu.VMEM((units, n, block, half), BF),
        passed=pltpu.VMEM((units, n + 1, block, half), BF),
        rest_got=pltpu.VMEM((units, bits - 1, block, half), BF),
        rest_sum=pltpu.VMEM((units, bits - 1, block, half), BF),
        last_got=pltpu.VMEM((units, block, half), BF),
        sums=pltpu.VMEM((GAIN_ROWS, width), F32), diag=pltpu.VMEM((16, 2 * length), F32),
        flip=pltpu.VMEM((length, length), BF), small=pltpu.VMEM((2 * n, small_rows, 128), F32),
        small_kept=small_all, small_core=small_all,
        small_held=pltpu.VMEM((bits, n, small_rows, 128), F32),
        small_group=pltpu.VMEM((bits, n, small_rows, 128), F32),
        small_passed=pltpu.VMEM((n + 1, small_rows, 128), F32),
        load_sems=dma((15,)), stream_sems=dma((3, most)), stage_sems=dma((most + 1,)),
        swap_sent=dma((len(xs),)), swap_got=dma((len(xs),)),
        small_sent=dma((1 + bits,)), small_got=dma((1 + bits,)), small_line=dma((4,)),
        section_kept=dma, section_sent=dma, section_got=dma,
        first_sent=dma((units,)), first_got=dma((units,)), line_sems=dma((units, 4)),
        rest_sems=dma((units, bits - 1, 2)), last_sems=dma((units, 2)), result_sems=dma((units, 2)),
    )
    groups = [
        len(xs), list(hbm), list(small_in), len(grads), list(outs), len(land_g), list(held), list(scratch)
    ]
    out_specs = [any_spec] * len(grads) + [vmem_spec] * (len(outs) - 1) + [any_spec] * (1 + len(land_g))
    results = pl.pallas_call(
        functools.partial(backward_kernel, (n, bits, first_units, unit_weight), groups),
        out_shape=grads + list(outs.values()) + land_g,
        in_specs=[any_spec] * (len(xs) + len(hbm)) + [vmem_spec] * len(small_in),
        out_specs=out_specs,
        scratch_shapes=list(held.values()) + list(scratch.values()),
        compiler_params=pltpu.CompilerParams(
            collective_id=0, has_side_effects=True, vmem_limit_bytes=63 * 1024 * 1024
        ),
        name="backward",
    )(*xs, *hbm.values(), *small_in.values())
    return results[: len(grads)], dict(zip(outs, results[len(grads) :]))


def finish_kernel(counts, *refs):
    wides, total = counts
    sources, targets = refs[:total], refs[total : 2 * total]
    held, widened, sems = refs[2 * total : 3 * total], refs[3 * total : -1], refs[-1]
    loads = [pltpu.make_async_copy(sources[i], held[i], sems.at[0, i]) for i in range(total)]
    for copy in loads:
        copy.start()
    stores = []
    for i in range(total):
        loads[i].wait()
        if i < wides:
            rows = held[i].shape[0]
            for at in range(0, rows, 16):
                widened[i][at : at + 16, :] = held[i][at : at + 16, :].astype(F32)
        stores.append(pltpu.make_async_copy(widened[i] if i < wides else held[i], targets[i], sems.at[1, i]))
        stores[i].start()
    for copy in stores:
        copy.wait()


def run_finish(grads, plain):
    any_spec = pl.BlockSpec(memory_space=pl.ANY)
    arrays = list(grads) + list(plain)
    shapes = [jax.ShapeDtypeStruct(a.shape, F32) for a in grads]
    shapes += [jax.ShapeDtypeStruct(a.shape, a.dtype) for a in plain]
    scratch = [pltpu.VMEM(a.shape, a.dtype) for a in arrays] + [pltpu.VMEM(a.shape, F32) for a in grads]
    results = pl.pallas_call(
        functools.partial(finish_kernel, (len(grads), len(arrays))),
        out_shape=shapes,
        in_specs=[any_spec] * len(arrays),
        out_specs=[any_spec] * len(arrays),
        scratch_shapes=scratch + [pltpu.SemaphoreType.DMA((2, len(arrays)))],
        compiler_params=pltpu.CompilerParams(vmem_limit_bytes=63 * 1024 * 1024),
        name="finish",
    )(*arrays)
    return results[: len(grads)], results[len(grads) :]


def shards(
    section_inputs, cotangent, encoder_segments, decoder_segments, encoder_valid, decoder_valid,
    position_buckets, encoder_gains, encoder_shifts, encoder_qkv, encoder_out, encoder_up, encoder_down,
    position_table, decoder_gains, decoder_shifts, decoder_qkv, decoder_out, cross_query, cross_keyvalue,
    cross_out, decoder_up, decoder_down,
):
    width = section_inputs.shape[-1]
    dp = lax.axis_size("dp")
    bits = lax.axis_size("group").bit_length() - 1
    blocks = lax.axis_size("pipe") * dp
    weights = dict(
        e_qkv=encoder_qkv, e_out=encoder_out, e_up=encoder_up, e_down=encoder_down,
        d_qkv=decoder_qkv, d_out=decoder_out, c_query=cross_query, c_kv=cross_keyvalue,
        c_out=cross_out, d_up=decoder_up, d_down=decoder_down,
    )

    small_in = dict(
        enc_seg=encoder_segments, dec_seg=decoder_segments, enc_valid=encoder_valid, dec_valid=decoder_valid,
        buckets=position_buckets.reshape(1, -1), enc_gains=encoder_gains, enc_shifts=encoder_shifts,
        dec_gains=decoder_gains, dec_shifts=decoder_shifts, table=position_table.T,
    )
    r = run_forward(section_inputs, small_in, weights)
    f = SimpleNamespace(**r)
    xs = [f.xd_down, f.xd_up, f.xc_out, f.memory_cut, f.xc_query, f.xd_out, f.xd_qkv, f.xe_down, f.xe_up, f.xe_out, f.xe_qkv]
    order = [decoder_down, decoder_up, cross_out, cross_keyvalue, cross_query, decoder_out, decoder_qkv,
             encoder_down, encoder_up, encoder_out, encoder_qkv]
    cut = [(w.shape[0] // blocks, w.shape[1]) for w in order]
    kept = dict(
        gd_up=f.gd_up, d2=f.d2, p_cross=f.p_cross, gc_query=f.gc_query, gc_kv=f.gc_kv, d1=f.d1, p_dec=f.p_dec,
        gd_qkv=f.gd_qkv, ge_up=f.ge_up, x1=f.x1, p_enc=f.p_enc, ge_qkv=f.ge_qkv,
    )
    hbm = dict(kept, cot=cotangent, x_enc=f.x_enc, x_dec=f.x_dec, **weights)
    small_back = dict(buckets=small_in["buckets"], enc_gains=encoder_gains, dec_gains=decoder_gains)
    table_shape = (position_table.shape[1], position_table.shape[0] // blocks)
    columns = [w.shape[1] for w in order]
    grads, rest = run_backward(dp, bits, xs, hbm, small_back, cut, columns, width // blocks, table_shape)
    rest.update(outputs=f.outputs)
    grads, plain = run_finish(grads, list(rest.values()))
    s = SimpleNamespace(**dict(zip(rest, plain)))
    d_down, d_up, c_out, c_kv, c_query, d_out, d_qkv, e_down, e_up, e_out, e_qkv = grads
    return (
        s.outputs, s.input_grads, s.enc_gains, s.enc_shifts, e_qkv, e_out, e_up, e_down, s.table.T,
        s.dec_gains, s.dec_shifts, d_qkv, d_out, c_query, c_kv, c_out, d_up, d_down,
    )


def solution(mesh):
    section = P("pipe", None, ("dp", "group"), None, None)
    rows = P(None, ("dp", "group"), None)
    cut_rows = P(("pipe", "dp"), None)
    cut_lanes = P(None, ("pipe", "dp"))
    return jax.shard_map(
        shards,
        mesh=mesh,
        in_specs=(section, P(None, ("dp", "group"), None, None), rows, rows, rows, rows) + (P(),) * 17,
        out_specs=(section, section, cut_lanes, cut_lanes) + (cut_rows,) * 5 + (cut_lanes, cut_lanes) + (cut_rows,) * 7,
        check_vma=False,
    )
```

```python
import functools
from types import SimpleNamespace

import jax
import jax.numpy as jnp
from jax import lax
from jax.experimental import pallas as pl
from jax.experimental.pallas import tpu as pltpu
from jax.sharding import PartitionSpec as P

HEADS = 12
MESH = pl.DeviceIdType.MESH
NEGATIVE = -1e30
BF, F32 = jnp.bfloat16, jnp.float32
GAIN_ROWS = 16


def dot(a, b):
    return jnp.dot(a, b, preferred_element_type=F32)


def dot_nt(a, b):
    return lax.dot_general(a, b, (((1,), (1,)), ((), ())), preferred_element_type=F32)


def dot_tn(a, b):
    return lax.dot_general(a, b, (((0,), (0,)), ((), ())), preferred_element_type=F32)


def row_loop(rows, chunk, body):
    def step(i, carry):
        body(pl.ds(pl.multiple_of(i * chunk, chunk), chunk))
        return carry

    lax.fori_loop(0, rows // chunk, step, 0)


def norm_stats(x):
    centre = x - jnp.mean(x, axis=-1, keepdims=True)
    spread = jnp.mean(centre * centre, axis=-1, keepdims=True)
    return centre, lax.rsqrt(spread + 1e-05)


def norm_forward(x_ref, gain, shift, n_ref):
    def body(rows):
        centre, inv = norm_stats(x_ref[rows, :].astype(F32))
        n_ref[rows, :] = (centre * inv * gain + shift).astype(BF)

    row_loop(x_ref.shape[0], 64, body)


def norm_backward(x_ref, gain, dn_ref, stream_ref, sums_ref, gain_at, shift_at):
    width = x_ref.shape[1]

    def step(i, carry):
        dgain, dshift = carry
        rows = pl.ds(pl.multiple_of(i * 64, 64), 64)
        centre, inv = norm_stats(x_ref[rows, :].astype(F32))
        hat = centre * inv
        dn = dn_ref[rows, :]
        dhat = dn * gain
        mean_one = jnp.mean(dhat, axis=-1, keepdims=True)
        mean_two = jnp.mean(dhat * hat, axis=-1, keepdims=True)
        stream_ref[rows, :] += inv * (dhat - mean_one - hat * mean_two)
        return (
            dgain + jnp.sum(dn * hat, axis=0, keepdims=True),
            dshift + jnp.sum(dn, axis=0, keepdims=True),
        )

    zero = jnp.zeros((1, width), F32)
    dgain, dshift = lax.fori_loop(0, x_ref.shape[0] // 64, step, (zero, zero))
    sums_ref[gain_at : gain_at + 1, :] = dgain
    sums_ref[shift_at : shift_at + 1, :] = dshift


def project(a_ref, w_ref, out_ref, tile=256):
    for start in range(0, w_ref.shape[1], tile):
        cols = slice(start, start + tile)
        out_ref[:, cols] = dot(a_ref[...], w_ref[:, cols]).astype(out_ref.dtype)


def project_add(a_ref, w_ref, resid_ref, out_ref, tile=256):
    for start in range(0, w_ref.shape[1], tile):
        cols = slice(start, start + tile)
        out_ref[:, cols] = (
            resid_ref[:, cols].astype(F32) + dot(a_ref[...], w_ref[:, cols])
        ).astype(out_ref.dtype)


def feed_up(n_ref, w_ref, z_ref, slope_ref, tile=512):
    for start in range(0, w_ref.shape[1], tile):
        cols = slice(start, start + tile)
        u = dot(n_ref[...], w_ref[:, cols])
        cdf = 0.5 * (1.0 + lax.erf(u * 0.7071067811865476))
        z_ref[:, cols] = (u * cdf).astype(BF)
        slope_ref[:, cols] = (cdf + u * (0.3989422804014327 * jnp.exp(-0.5 * u * u))).astype(BF)


def attend(q_ref, q_at, k_ref, k_at, v_ref, v_at, mask_ref, p_ref, o_ref, bias_ref=None):
    length = q_ref.shape[0]
    head = o_ref.shape[1] // HEADS
    pair = 2 * head
    scale = head**-0.5

    def step(i):
        def cols(at):
            return slice(at + i * pair, at + (i + 1) * pair)

        low_half = lax.broadcasted_iota(jnp.int32, (length, pair), 1) < head
        q = q_ref[:, cols(q_at)] * jnp.asarray(scale, BF)
        k = k_ref[:, cols(k_at)]
        v = v_ref[:, cols(v_at)]
        outs = []
        for half in range(2):
            own = low_half if half == 0 else jnp.logical_not(low_half)
            s = dot_nt(jnp.where(own, q, jnp.zeros_like(q)), k) + mask_ref[...]
            if bias_ref is not None:
                wide = jnp.broadcast_to(
                    bias_ref[2 * i + half : 2 * i + half + 1, :], (length, 2 * length)
                )
                s = s + pltpu.roll(wide, length, 1, stride=1, stride_axis=0)[:, :length]
            e = jnp.exp(s - jnp.max(s, axis=-1, keepdims=True))
            p = (e * (1.0 / jnp.sum(e, axis=-1, keepdims=True))).astype(BF)
            p_ref[2 * i + half] = p
            outs.append(dot(p, v))
        o_ref[:, cols(0)] = jnp.where(low_half, outs[0], outs[1]).astype(BF)

    for i in range(HEADS // 2):
        step(i)


def attend_back(
    pairs, q_ref, q_at, k_ref, k_at, v_ref, v_at, p_ref, do_ref, diag_ref=None, flip_ref=None
):
    length = q_ref.shape[0]
    head = do_ref.shape[1] // HEADS
    pair = 2 * head
    scale = head**-0.5

    def step(i):
        def cols(at):
            return slice(at + i * pair, at + (i + 1) * pair)

        low_half = lax.broadcasted_iota(jnp.int32, (length, pair), 1) < head
        q = q_ref[:, cols(q_at)]
        k = k_ref[:, cols(k_at)]
        v = v_ref[:, cols(v_at)]
        do = do_ref[:, cols(0)]
        dqs, dks, dvs = [], [], []
        for half in range(2):
            own = low_half if half == 0 else jnp.logical_not(low_half)
            p = p_ref[2 * i + half]
            dp = dot_nt(jnp.where(own, do, jnp.zeros_like(do)), v)
            wide_p = p.astype(F32)
            row = jnp.sum(wide_p * dp, axis=-1, keepdims=True)
            ds = (wide_p * (dp - row)).astype(BF)
            dvs.append(dot_tn(p, do))
            dqs.append(dot(ds, k))
            dks.append(dot_tn(ds, q))
            if diag_ref is not None:
                flipped = dot(flip_ref[...], ds)
                wide = jnp.concatenate([flipped, jnp.zeros_like(flipped)], axis=1)
                rolled = pltpu.roll(wide, 1, 1, stride=1, stride_axis=0)
                diag_ref[2 * i + half : 2 * i + half + 1, :] = jnp.sum(rolled, axis=0, keepdims=True)
        q_ref[:, cols(q_at)] = (jnp.where(low_half, dqs[0], dqs[1]) * scale).astype(BF)
        k_ref[:, cols(k_at)] = (jnp.where(low_half, dks[0], dks[1]) * scale).astype(BF)
        v_ref[:, cols(v_at)] = jnp.where(low_half, dvs[0], dvs[1]).astype(BF)

    for i in range(pairs[0], pairs[1]):
        step(i)


def build_masks(eseg, dseg, evalid, dvalid, enc_ref, dec_ref, cross_ref):
    length = enc_ref.shape[0]
    shape = (length, length)
    key = lax.broadcasted_iota(jnp.int32, shape, 1)
    query = lax.broadcasted_iota(jnp.int32, shape, 0)
    eseg_key = jnp.broadcast_to(eseg.astype(F32), shape)
    dseg_key = jnp.broadcast_to(dseg.astype(F32), shape)
    eseg_query, dseg_query = eseg_key.T, dseg_key.T
    evalid_key = jnp.broadcast_to(evalid, shape) == 1
    dvalid_key = jnp.broadcast_to(dvalid, shape) == 1
    before = pltpu.roll(eseg_key, 1, 1)
    first = (key == 0) | (eseg_key != before)
    enc = (eseg_query == eseg_key) & (evalid_key | (key == query))
    dec = (dseg_query == dseg_key) & (dvalid_key | (key == query)) & (key <= query)
    cross = (dseg_query == eseg_key) & (evalid_key | first)
    enc_ref[...] = jnp.where(enc, 0.0, NEGATIVE)
    dec_ref[...] = jnp.where(dec, 0.0, NEGATIVE)
    cross_ref[...] = jnp.where(cross, 0.0, NEGATIVE)


def bucket_onehot(buckets, bucket_count):
    shape = (bucket_count, buckets.shape[1])
    return jnp.broadcast_to(buckets, shape) == lax.broadcasted_iota(jnp.int32, shape, 0)


def forward_kernel(groups, *refs):
    spaces = []
    for names in groups:
        spaces.append(SimpleNamespace(**dict(zip(names, refs))))
        refs = refs[len(names) :]
    hbm, small_in, out, v, s = spaces
    pipe = lax.axis_index("pipe")
    length, width = v.x_enc.shape
    started, pending = [], []

    def load(source, target):
        copy = pltpu.make_async_copy(source, target, s.sem_in.at[len(started)])
        copy.start()
        started.append(copy)
        return copy

    def store(source, target):
        copy = pltpu.make_async_copy(source, target, s.sem_out.at[len(pending)])
        copy.start()
        pending.append(copy)

    core = (1 - pipe, lax.axis_index("dp"), lax.axis_index("group"))
    barrier = pltpu.get_barrier_semaphore()
    pl.semaphore_signal(barrier, inc=1, device_id=core, device_id_type=MESH)
    mine, other = hbm.section_inputs.at[0, pipe, 0], hbm.section_inputs.at[0, 1 - pipe, 0]

    def keep(target):
        return pltpu.make_async_copy(mine, target, s.swap_sems.at[0])

    def give(target):
        return pltpu.make_async_remote_copy(
            src_ref=other, dst_ref=target, send_sem=s.swap_sems.at[1], recv_sem=s.swap_sems.at[2],
            device_id=core, device_id_type=MESH,
        )

    @pl.when(pipe == 0)
    def _():
        keep(v.x_enc).start()

    @pl.when(pipe == 1)
    def _():
        keep(v.x_dec).start()

    shared = []

    def share(source, target):
        part = source.shape[1] // 2
        ours = pl.ds(pl.multiple_of(pipe * part, 128), part)
        theirs = pl.ds(pl.multiple_of((1 - pipe) * part, 128), part)
        store(source.at[:, ours], target.at[0:length])
        copy = pltpu.make_async_remote_copy(
            src_ref=source.at[:, theirs], dst_ref=target.at[length : 2 * length],
            send_sem=s.share_sent.at[len(shared)], recv_sem=s.share_got.at[len(shared)],
            device_id=core, device_id_type=MESH,
        )
        copy.start()
        shared.append(copy)

    get_e_qkv = load(hbm.e_qkv, s.e_qkv)
    get_e_out = load(hbm.e_out, s.e_out)
    get_e_up = load(hbm.e_up, s.up)
    get_e_down = load(hbm.e_down, s.down)
    get_d_qkv = load(hbm.d_qkv, s.d_qkv)
    get_d_out = load(hbm.d_out, s.d_out)
    get_c_query = load(hbm.c_query, s.c_query)
    get_c_kv = load(hbm.c_kv, s.c_kv)
    get_c_out = load(hbm.c_out, s.c_out)
    pl.semaphore_wait(barrier, 1)

    @pl.when(pipe == 0)
    def _():
        give(v.x_enc).start()

    @pl.when(pipe == 1)
    def _():
        give(v.x_dec).start()


    build_masks(
        small_in.enc_seg[pipe], small_in.dec_seg[pipe], small_in.enc_valid[pipe], small_in.dec_valid[pipe],
        s.mask_enc, s.mask_dec, s.mask_cross,
    )
    buckets = small_in.buckets[...]
    s.bias[0:HEADS, :] = dot(small_in.table[...], bucket_onehot(buckets, small_in.table.shape[1]).astype(BF))
    def at(ref, row):
        return ref[row : row + 1, :].astype(F32)

    enc_gains, enc_shifts = small_in.enc_gains, small_in.enc_shifts
    dec_gains, dec_shifts = small_in.dec_gains, small_in.dec_shifts

    @pl.when(pipe == 0)
    def _():
        keep(v.x_enc).wait()

    @pl.when(pipe == 1)
    def _():
        give(v.x_enc).wait_recv()

    store(v.x_enc, out.x_enc)
    norm_forward(v.x_enc, at(enc_gains, 0), at(enc_shifts, 0), v.xe_qkv)
    share(v.xe_qkv, out.xe_qkv)
    get_e_qkv.wait()
    project(v.xe_qkv, s.e_qkv, v.ge_qkv)
    attend(v.ge_qkv, 0, v.ge_qkv, width, v.ge_qkv, 2 * width, s.mask_enc, v.p_enc, v.xe_out, s.bias)
    store(v.ge_qkv, out.ge_qkv)
    store(v.p_enc, out.p_enc)
    share(v.xe_out, out.xe_out)
    get_e_out.wait()
    project_add(v.xe_out, s.e_out, v.x_enc, v.x1)
    store(v.x1, out.x1)
    norm_forward(v.x1, at(enc_gains, 1), at(enc_shifts, 1), v.xe_up)
    share(v.xe_up, out.xe_up)
    get_e_up.wait()
    feed_up(v.xe_up, s.up, v.xe_down, v.ge_up)
    get_d_up = load(hbm.d_up, s.up)
    share(v.xe_down, out.xe_down)
    store(v.ge_up, out.ge_up)
    get_e_down.wait()
    project_add(v.xe_down, s.down, v.x1, v.memory)
    get_d_down = load(hbm.d_down, s.down)
    share(v.memory, out.memory_cut)

    @pl.when(pipe == 0)
    def _():
        give(v.x_dec).wait_recv()

    @pl.when(pipe == 1)
    def _():
        keep(v.x_dec).wait()

    store(v.x_dec, out.x_dec)
    norm_forward(v.x_dec, at(dec_gains, 0), at(dec_shifts, 0), v.xd_qkv)
    share(v.xd_qkv, out.xd_qkv)
    get_d_qkv.wait()
    project(v.xd_qkv, s.d_qkv, v.gd_qkv)
    attend(v.gd_qkv, 0, v.gd_qkv, width, v.gd_qkv, 2 * width, s.mask_dec, v.p_dec, v.xd_out)
    share(v.xd_out, out.xd_out)
    store(v.gd_qkv, out.gd_qkv)
    store(v.p_dec, out.p_dec)
    get_d_out.wait()
    project_add(v.xd_out, s.d_out, v.x_dec, v.d1)
    store(v.d1, out.d1)
    norm_forward(v.d1, at(dec_gains, 1), at(dec_shifts, 1), v.xc_query)
    share(v.xc_query, out.xc_query)
    get_c_query.wait()
    project(v.xc_query, s.c_query, v.gc_query)
    get_c_kv.wait()
    project(v.memory, s.c_kv, v.gc_kv)
    attend(v.gc_query, 0, v.gc_kv, 0, v.gc_kv, width, s.mask_cross, v.p_cross, v.xc_out)
    share(v.xc_out, out.xc_out)
    store(v.gc_query, out.gc_query)
    store(v.gc_kv, out.gc_kv)
    store(v.p_cross, out.p_cross)
    get_c_out.wait()
    project_add(v.xc_out, s.c_out, v.d1, v.d2)
    store(v.d2, out.d2)
    norm_forward(v.d2, at(dec_gains, 2), at(dec_shifts, 2), v.xd_up)
    share(v.xd_up, out.xd_up)
    get_d_up.wait()
    feed_up(v.xd_up, s.up, v.xd_down, v.gd_up)
    share(v.xd_down, out.xd_down)
    store(v.gd_up, out.gd_up)
    get_d_down.wait()
    project_add(v.xd_down, s.down, v.d2, v.decoded)

    def section(layer, ref):
        @pl.when(pipe == layer)
        def _():
            pltpu.make_async_copy(ref, out.outputs.at[0, pipe, 0], s.section_sems.at[0]).start()

        @pl.when(pipe != layer)
        def _():
            pltpu.make_async_remote_copy(
                src_ref=ref, dst_ref=out.outputs.at[0, pipe, 0], send_sem=s.section_sems.at[1],
                recv_sem=s.section_sems.at[2], device_id=core, device_id_type=MESH,
            ).start()

    section(0, v.memory)
    section(1, v.decoded)

    give(v.x_enc).wait_send()
    pltpu.make_async_copy(v.memory, out.outputs.at[0, pipe, 0], s.section_sems.at[0]).wait()
    pltpu.make_async_remote_copy(
        src_ref=v.memory, dst_ref=out.outputs.at[0, 1 - pipe, 0], send_sem=s.section_sems.at[1],
        recv_sem=s.section_sems.at[2], device_id=core, device_id_type=MESH,
    ).wait()
    for copy in pending + shared:
        copy.wait()


def run_forward(section_inputs, small_in, weights):
    unused, micro, unused, length, width = section_inputs.shape
    hidden = weights["e_up"].shape[1]
    hbm = dict(section_inputs=section_inputs, **weights)
    any_spec = pl.BlockSpec(memory_space=pl.ANY)
    vmem_spec = pl.BlockSpec(memory_space=pltpu.VMEM)
    columns = dict(
        ge_qkv=3 * width, ge_up=hidden, gd_qkv=3 * width, gc_query=width, gc_kv=2 * width, gd_up=hidden,
        x_enc=width, x_dec=width,
    )
    inputs = dict(
        xe_qkv=width, xe_out=width, xe_up=width, xe_down=hidden, xd_qkv=width, xd_out=width, xc_query=width,
        xc_out=width, xd_up=width, xd_down=hidden,
    )
    outs = {name: jax.ShapeDtypeStruct((length, n), BF) for name, n in columns.items()}
    probabilities = jax.ShapeDtypeStruct((HEADS, length, length), BF)
    rows = jax.ShapeDtypeStruct((length, width), F32)
    outs.update(p_enc=probabilities, p_dec=probabilities, p_cross=probabilities, x1=rows, d1=rows, d2=rows)
    held = {name: pltpu.VMEM(shape.shape, shape.dtype) for name, shape in outs.items()}
    held.update({name: pltpu.VMEM((length, n), BF) for name, n in inputs.items()})
    held.update(memory=pltpu.VMEM((length, width), BF), decoded=pltpu.VMEM((length, width), BF))
    outs.update({name: jax.ShapeDtypeStruct((2 * length, n // 2), BF) for name, n in inputs.items()})
    outs.update(outputs=jax.ShapeDtypeStruct((1, micro, 1, length, width), BF))
    outs.update(memory_cut=jax.ShapeDtypeStruct((2 * length, width // 2), BF))
    square = pltpu.VMEM((length, length), F32)
    scratch = {
        name: pltpu.VMEM(w.shape, BF) for name, w in weights.items() if hidden not in w.shape
    }
    scratch.update(
        up=pltpu.VMEM((width, hidden), BF), down=pltpu.VMEM((hidden, width), BF),
        mask_enc=square, mask_dec=square, mask_cross=square, bias=pltpu.VMEM((16, 2 * length), F32),
        section_sems=pltpu.SemaphoreType.DMA((3,)), swap_sems=pltpu.SemaphoreType.DMA((3,)), share_sent=pltpu.SemaphoreType.DMA((len(inputs) + 1,)),
        share_got=pltpu.SemaphoreType.DMA((len(inputs) + 1,)), sem_in=pltpu.SemaphoreType.DMA((16,)), sem_out=pltpu.SemaphoreType.DMA((len(outs),)),
    )
    groups = [list(part) for part in (hbm, small_in, outs, held, scratch)]
    results = pl.pallas_call(
        functools.partial(forward_kernel, groups),
        out_shape=list(outs.values()),
        in_specs=[any_spec] * len(hbm) + [vmem_spec] * len(small_in),
        out_specs=[any_spec] * len(outs),
        scratch_shapes=list(held.values()) + list(scratch.values()),
        compiler_params=pltpu.CompilerParams(
            collective_id=1, has_side_effects=True, vmem_limit_bytes=63 * 1024 * 1024
        ),
        name="forward",
    )(*hbm.values(), *small_in.values())
    return dict(zip(outs, results))


def step_order(work, small_after, units, n, bits, window=3):
    big, delay, cost = 6.6, 2.0, 0.5
    small = big / n
    sides, line = [0.0, 0.0], [0.0] * n
    waiting, steps = [], []
    flying = [0, 0]
    clock, made, done = 0.0, 0, 0

    def message(free, at, start, size):
        free[at] = max(free[at], start) + size
        return free[at] + delay

    while done < len(work) or waiting:
        ready = [event for event in waiting if event[0] <= clock]
        if ready:
            event = min(ready)
            waiting.remove(event)
            unused, kind, unit, at = event
            steps.append((kind, unit, at))
            clock += cost
            first, other = unit % 2, 1 - unit % 2
            if kind == 1:
                flying[first] -= 1
                waiting.append((message(line, 1, clock, (n - 1) * small), 2 if n > 2 else 3, unit, 1))
            elif kind == 2:
                arrival = message(line, at + 1, clock, (n - 1 - at) * small)
                waiting.append((arrival, 2 if at + 1 < n - 1 else 3, unit, at + 1))
            elif kind == 3:
                waiting.append((message(sides, other, clock, small), 4, unit, 0))
            elif kind == 4 and at + 2 < bits:
                waiting.append((message(sides, other, clock, small), 4, unit, at + 1))
            elif kind == 4:
                waiting.append((message(sides, first, clock, small), 5, unit, 0))
            elif kind == 6 and at + 1 < bits + n:
                waiting.append((clock + 2 * delay, 6, 0, at + 1))
        elif done < len(work) and (not work[done][1] or flying[made % 2] < window):
            clock += work[done][0]
            steps.append((0, done, 0))
            if work[done][1]:
                waiting.append((message(sides, made % 2, clock, big), 1, made, 0))
                flying[made % 2] += 1
                made += 1
            if done == small_after:
                waiting.append((clock + delay, 6, 0, 0))
            done += 1
        else:
            clock = min(waiting)[0]
    return steps


def backward_kernel(tables, groups, *refs):
    spaces = []
    for names in groups:
        if isinstance(names, int):
            spaces.append(refs[:names])
            refs = refs[names:]
        else:
            spaces.append(SimpleNamespace(**dict(zip(names, refs))))
            refs = refs[len(names) :]
    xs, hbm, small_in, grads, out, land_g, v, s = spaces
    n, bits, first_units, unit_weight = tables
    p, d, g = lax.axis_index("pipe"), lax.axis_index("dp"), lax.axis_index("group")
    units = len(unit_weight)
    length, width = v.stream.shape
    half = width // 2
    block = width // (2 * n)
    blocks = 2 * n
    gs = [
        v.cot, v.gd_up, v.gc_out, v.gc_kv, v.gc_query, v.gd_out, v.gd_qkv, v.ge_down, v.ge_up, v.ge_out, v.ge_qkv
    ]
    d_down, d_up, c_out, c_kv, c_query, d_out, d_qkv, e_down, e_up, e_out, e_qkv = range(len(gs))

    def bit_of(bit):
        return (g // 2**bit) % 2

    def across(bit):
        return (p, d, g + (1 - 2 * bit_of(bit)) * 2**bit)

    core = (1 - p, d, g)
    above, below = (p, d + 1, g), (p, d - 1, g)

    loads = []

    def load(source, target):
        copy = pltpu.make_async_copy(source, target, s.load_sems.at[len(loads)])
        copy.start()
        loads.append(copy)
        return copy

    get_cot = load(hbm.cot.at[p, 0], v.cot)

    def tiles_of(at):
        return xs[at].shape[1] // half

    fetched = {}

    def fetch_x(at):
        for tile in range(tiles_of(at)):
            copy = pltpu.make_async_copy(
                xs[at].at[:, tile * half : (tile + 1) * half], s.x_stage.at[tile], s.stage_sems.at[tile]
            )
            copy.start()
            fetched.setdefault(at, []).append(copy)

    def fetch_g(at):
        if at > 0:
            g_swaps[at].wait_recv()
        source = hbm.cot.at[1 - p, 0] if at == 0 else land_g[at - 1]
        copy = pltpu.make_async_copy(
            source, s.g_stage.at[:, 0 : source.shape[1]], s.stage_sems.at[s.stage_sems.shape[0] - 1]
        )
        copy.start()
        fetched[at].append(copy)

    fetch_x(d_down)
    fetch_g(d_down)

    slots, side, reach = s.stream_w.shape
    chunks = []
    for ref in (
        hbm.d_down, hbm.d_up, hbm.c_out, hbm.c_kv, hbm.c_query, hbm.d_out, hbm.d_qkv, hbm.e_down, hbm.e_up,
        hbm.e_out, hbm.e_qkv,
    ):
        columns = ref.shape[1]
        together = reach // columns
        for first in range(0, ref.shape[0], together * side):
            last = min(ref.shape[0], first + together * side)
            chunks.append([(ref.at[row : row + side, :], (row - first) // side * columns, columns) for row in range(first, last, side)])
    walked = [0]

    def chunk_copies(at):
        return [
            pltpu.make_async_copy(
                source, s.stream_w.at[at % slots, :, start : start + columns], s.stream_sems.at[at % slots, i]
            )
            for i, (source, start, columns) in enumerate(chunks[at])
        ]

    def start_chunk(at):
        if at < len(chunks):
            for copy in chunk_copies(at):
                copy.start()

    for at in range(slots):
        start_chunk(at)

    def next_rows(g_ref, put, row):
        at = walked[0]
        walked[0] += 1
        for copy in chunk_copies(at):
            copy.wait()
        for unused, start, columns in chunks[at]:
            put(slice(row, row + side), dot_nt(g_ref[...], s.stream_w[at % slots, :, start : start + columns]))
            row += side
        start_chunk(at + slots)
        return row

    def back_through(g_ref, out_ref):
        def put(cols, part):
            out_ref[:, cols] = part.astype(out_ref.dtype)

        row = 0
        while row < out_ref.shape[1]:
            row = next_rows(g_ref, put, row)

    def back_through_feed(g_ref, slope_ref, start, stop):
        def put(cols, part):
            slope_ref[:, cols] = (part * slope_ref[:, cols].astype(F32)).astype(BF)

        row = start
        while row < stop:
            row = next_rows(g_ref, put, row)

    get_gd_up = load(hbm.gd_up, v.gd_up)
    get_d2 = load(hbm.d2, v.d2)
    get_p = [load(hbm.p_cross, v.p)]
    get_gc_query = load(hbm.gc_query, v.gc_query)
    get_gc_kv = load(hbm.gc_kv, v.gc_kv)
    get_d1 = load(hbm.d1, v.d1)
    get_gd_qkv = load(hbm.gd_qkv, v.gd_qkv)
    get_x_dec = load(hbm.x_dec, v.x_dec)
    get_ge_up = load(hbm.ge_up, v.ge_up)
    get_ge_qkv = load(hbm.ge_qkv, v.ge_qkv)

    barrier = pltpu.get_barrier_semaphore()
    pl.semaphore_signal(barrier, inc=1, device_id=core, device_id_type=MESH)
    for bit in range(bits):
        pl.semaphore_signal(barrier, inc=1, device_id=across(bit), device_id_type=MESH)

    @pl.when(d > 0)
    def _():
        pl.semaphore_signal(barrier, inc=1, device_id=below, device_id_type=MESH)

    @pl.when(d < n - 1)
    def _():
        pl.semaphore_signal(barrier, inc=1, device_id=above, device_id_type=MESH)

    @pl.when((d > 0) & (d < n - 1))
    def _():
        pl.semaphore_wait(barrier, 3 + bits)

    @pl.when((d == 0) | (d == n - 1))
    def _():
        pl.semaphore_wait(barrier, 2 + bits)

    def remote(source, target, send_sem, recv_sem, device):
        return pltpu.make_async_remote_copy(
            src_ref=source, dst_ref=target, send_sem=send_sem, recv_sem=recv_sem,
            device_id=device, device_id_type=MESH,
        )

    sent = []

    def send(copy):
        copy.start()
        sent.append(copy.wait_send)
        return copy

    g_swaps = {}

    def swap_g(at):
        g_swaps[at] = send(
            remote(gs[at], land_g[at - 1], s.swap_sent.at[at], s.swap_got.at[at], core)
        )

    def input_grad(layer, ref):
        @pl.when(p == layer)
        def _():
            pltpu.make_async_copy(ref, out.input_grads.at[0, p, 0], s.section_kept).start()

        @pl.when(p != layer)
        def _():
            remote(ref, out.input_grads.at[0, p, 0], s.section_sent, s.section_got, core).start()

    section_kept = pltpu.make_async_copy(v.do, out.input_grads.at[0, p, 0], s.section_kept)
    section_given = remote(v.do, out.input_grads.at[0, 1 - p, 0], s.section_sent, s.section_got, core)

    def first_bit(unit):
        return 0 if unit % 2 == 0 else bits - 1

    rooms = s.given.shape[0]

    def first_copy(unit):
        return remote(
            s.given.at[unit % rooms], s.taken.at[unit], s.first_sent.at[unit], s.first_got.at[unit],
            across(first_bit(unit)),
        )

    def product(at, tile, cols):
        value = dot(s.factor[tile, :, 0:length], gs[at][:, cols])
        return (value + dot(s.factor[tile, :, length : 2 * length], s.g_stage[:, cols])).astype(BF)

    def room_free(unit):
        if unit >= rooms:
            first_copy(unit - rooms).wait_send()

    def make(unit):
        at = unit_weight[unit]
        base = first_units[at]
        tiles = tiles_of(at)
        if unit == base:
            if at == 0:
                get_cot.wait()
            for copy in fetched.pop(at):
                copy.wait()
            for tile in range(tiles):
                s.factor[tile] = s.x_stage[tile].T
        if tiles == 1:
            room_free(unit)
            mine = bit_of(first_bit(unit))
            column = (unit - base) * width
            given = product(at, 0, pl.ds(pl.multiple_of(column + (1 - mine) * half, 128), half))
            for i in range(n):
                s.given[unit % rooms, i] = given[i * block : (i + 1) * block]
            first_copy(unit).start()
            kept = product(at, 0, pl.ds(pl.multiple_of(column + mine * half, 128), half))
            for i in range(n):
                s.kept[unit, i] = kept[i * block : (i + 1) * block]
            return
        if unit == base:
            for i in range(tiles):
                room_free(unit + i)
            for tile in range(tiles):
                for which in range(2):
                    split_rows(base, tiles, tile, which, product(at, tile, slice(which * half, (which + 1) * half)))
        first_copy(unit).start()

    def split_rows(base, tiles, tile, which, value):
        for i in range(n):
            unit = base + (tile * n + i) % tiles
            at = (tile * n + i) // tiles
            mine = bit_of(first_bit(unit))
            rows = value[i * block : (i + 1) * block]

            @pl.when(mine == which)
            def _(unit=unit, at=at, rows=rows):
                s.kept[unit, at] = rows

            @pl.when(mine != which)
            def _(unit=unit, at=at, rows=rows):
                s.given[unit % rooms, at] = rows

    def add(target, index, source, source_index):
        target[index] = (target[index].astype(F32) + source[source_index].astype(F32)).astype(target.dtype)

    def up_copy(line, dd):
        source = line.kept.at[1:n] if dd == 0 else line.passed.at[dd + 2 : n + 1]
        return remote(source, line.passed.at[dd + 2 : n + 1], line.sems.at[0], line.sems.at[1], above)

    def down_copy(line, dd):
        source = line.kept.at[0 : n - 1] if dd == n - 1 else line.passed.at[0:dd]
        return remote(source, line.passed.at[0:dd], line.sems.at[2], line.sems.at[3], below)

    def line_start(line):
        @pl.when(d == 0)
        def _():
            up_copy(line, 0).start()

        @pl.when(d == n - 1)
        def _():
            down_copy(line, n - 1).start()

    def line_hop(line, hop):
        @pl.when(d == hop)
        def _():
            up_copy(line, hop - 1).wait_recv()
            for i in range(hop + 1, n):
                add(line.passed, i + 1, line.kept, i)
            up_copy(line, hop).start()

        @pl.when(d == n - 1 - hop)
        def _():
            down_copy(line, n - hop).wait_recv()
            for i in range(n - 1 - hop):
                add(line.passed, i, line.kept, i)
            down_copy(line, n - 1 - hop).start()

    def line_end(line):
        @pl.when(d == n - 1)
        def _():
            up_copy(line, n - 2).wait_recv()
            line.kept[n - 1] = (
                line.kept[n - 1].astype(F32) + line.passed[n].astype(F32)
            ).astype(line.kept.dtype)

        @pl.when(d == 0)
        def _():
            down_copy(line, 1).wait_recv()
            line.kept[0] = (line.kept[0].astype(F32) + line.passed[0].astype(F32)).astype(line.kept.dtype)

        for dd in range(1, n - 1):

            @pl.when(d == dd)
            def _(dd=dd):
                line.kept[dd] = (
                    line.kept[dd].astype(F32) + line.passed[dd + 1].astype(F32) + line.passed[dd].astype(F32)
                ).astype(line.kept.dtype)

    def line_sent(line):
        for dd in range(n):

            @pl.when(d == dd)
            def _(dd=dd):
                if dd < n - 1:
                    up_copy(line, dd).wait_send()
                if dd > 0:
                    down_copy(line, dd).wait_send()

    def line_of(unit):
        return SimpleNamespace(
            kept=s.kept.at[unit], passed=s.passed.at[unit], sems=s.line_sems.at[unit]
        )

    def rest_bits(unit):
        return [bit for bit in range(bits) if bit != first_bit(unit)]

    def rest_copy(unit, at):
        source = s.kept.at[unit, d] if at == 0 else s.rest_sum.at[unit, at - 1]
        return remote(
            source, s.rest_got.at[unit, at], s.rest_sems.at[unit, at, 0], s.rest_sems.at[unit, at, 1],
            across(rest_bits(unit)[at]),
        )

    def last_copy(unit):
        return remote(
            s.rest_sum.at[unit, bits - 2], s.last_got.at[unit], s.last_sems.at[unit, 0], s.last_sems.at[unit, 1],
            across(first_bit(unit)),
        )

    def result_at(unit, which):
        at = unit_weight[unit]
        k = unit - first_units[at]
        target = grads[at]
        if tiles_of(at) == 1:
            return target.at[:, pl.ds(pl.multiple_of(k * width + which * half, 128), half)]
        return target.at[pl.ds(k * block, block), pl.ds(pl.multiple_of(which * half, 128), half)]

    def own_result(unit):
        return pltpu.make_async_copy(
            s.rest_sum.at[unit, bits - 2], result_at(unit, bit_of(first_bit(unit))), s.result_sems.at[unit, 0]
        )

    def got_result(unit):
        return pltpu.make_async_copy(
            s.last_got.at[unit], result_at(unit, 1 - bit_of(first_bit(unit))), s.result_sems.at[unit, 1]
        )

    small_line = SimpleNamespace(kept=s.small_kept, passed=s.small_passed, sems=s.small_line)
    small_swap = remote(
        s.small.at[pl.ds((1 - p) * n, n)], s.small_core, s.small_sent.at[0], s.small_got.at[0], core
    )

    def small_copy(bit):
        return remote(
            s.small_held.at[bit], s.small_group.at[bit], s.small_sent.at[1 + bit], s.small_got.at[1 + bit], across(bit)
        )

    def small_step(at):
        if at == 0:
            small_swap.wait_recv()
            s.small_kept[...] = s.small[pl.ds(p * n, n)] + s.small_core[...]
        elif at <= bits:
            small_copy(at - 1).wait_recv()
            s.small_kept[...] += s.small_group[at - 1]
        if at < bits:
            s.small_held[at] = s.small_kept[...]
            small_copy(at).start()
        elif at == bits:
            line_start(small_line)
        elif at < bits + n - 1:
            line_hop(small_line, at - bits)
        else:
            line_end(small_line)
            total = s.small_kept[d]
            lanes = out.enc_gains.shape[1]
            for ref, row in (
                (out.enc_gains, 0), (out.enc_shifts, 2), (out.dec_gains, 4), (out.dec_shifts, 7)
            ):
                ref[...] = total[row : row + ref.shape[0], 0:lanes]
            out.table[...] = total[GAIN_ROWS:].T[0:HEADS, 0 : out.table.shape[1]]

    def gain(ref, row):
        return ref[row : row + 1, :].astype(F32)

    enc_gains, dec_gains = small_in.enc_gains, small_in.dec_gains
    pairs = HEADS // 2
    work = []

    def piece(time, body, *args):
        work.append((time, False, functools.partial(body, *args)))

    def make_all(at):
        count = max(tiles_of(at), gs[at].shape[1] // width)
        for i in range(count):
            first_time = 1.2 if tiles_of(at) == 1 else 1.1 * tiles_of(at)
            later = 0.8 if tiles_of(at) == 1 else 0.1
            work.append((first_time if i == 0 else later, True, functools.partial(make, first_units[at] + i)))

    def start_feed(g_ref, slope_ref, get):
        get.wait()
        back_through_feed(g_ref, slope_ref, 0, slope_ref.shape[1] // 3)

    def end_feed(g_ref, slope_ref, at):
        back_through_feed(g_ref, slope_ref, slope_ref.shape[1] // 3, slope_ref.shape[1])
        swap_g(at)

    get_late = []

    def residual(x_ref, get, gain_row, gain_at, shift_at, low_ref):
        (get_late.pop(0) if get is None else get).wait()
        norm_backward(x_ref, gain_row, v.dn, v.stream, s.sums, gain_at, shift_at)
        low_ref[...] = v.stream[...].astype(BF)

    def residual_swap(x_ref, get, gain_row, gain_at, shift_at, low_ref, at):
        residual(x_ref, get, gain_row, gain_at, shift_at, low_ref)
        if x_ref is v.d2 and at == c_out:
            get_late.append(load(hbm.x1, v.d2))
        swap_g(at)
        back_through(low_ref, v.do)

    def begin():
        s.sums[...] = jnp.zeros_like(s.sums)
        v.stream[...] = v.cot[...].astype(F32)
        start_feed(v.cot, v.gd_up, get_gd_up)

    def cross_part(first, last):
        if first == 0:
            get_p[0].wait()
            get_gc_query.wait()
            get_gc_kv.wait()
        attend_back((first, last), v.gc_query, 0, v.gc_kv, 0, v.gc_kv, width, v.p, v.do)
        if last == pairs:
            get_p.append(load(hbm.p_dec, v.p))
            swap_g(c_kv)
            swap_g(c_query)

    def dec_part(first, last):
        if first == 0:
            get_p[1].wait()
            get_gd_qkv.wait()
        attend_back((first, last), v.gd_qkv, 0, v.gd_qkv, width, v.gd_qkv, 2 * width, v.p, v.do)
        if last == pairs:
            get_p.append(load(hbm.p_enc, v.p))
            swap_g(d_qkv)

    def enc_part(first, last):
        if first == 0:
            get_p[2].wait()
            get_ge_qkv.wait()
            s.diag[...] = jnp.zeros_like(s.diag)
            flip_shape = (length, length)
            s.flip[...] = (
                lax.broadcasted_iota(jnp.int32, flip_shape, 0) + lax.broadcasted_iota(jnp.int32, flip_shape, 1)
                == length - 1
            ).astype(BF)
        attend_back(
            (first, last), v.ge_qkv, 0, v.ge_qkv, width, v.ge_qkv, 2 * width, v.p, v.do, s.diag, s.flip
        )
        if last == pairs:
            swap_g(e_qkv)

    def memory_part():
        back_through(v.gc_kv, v.ge_down)
        swap_g(e_down)

    def dec_end():
        residual(v.x_dec, get_x_dec, gain(dec_gains, 0), 4, 7, v.dx_dec)
        input_grad(1, v.dx_dec)
        get_late.append(load(hbm.x_enc, v.x_dec))
        v.stream[...] = v.ge_down[...].astype(F32)

    def small_part():
        residual(v.x_dec, None, gain(enc_gains, 0), 0, 2, v.do)
        input_grad(0, v.do)
        buckets = small_in.buckets[...]
        bucket_count = out.table.shape[1] * blocks
        onehot = bucket_onehot(buckets, bucket_count).astype(BF)
        rest = s.diag[...]
        table_grad = jnp.zeros((bucket_count, rest.shape[0]), F32)
        for unused in range(3):
            part = rest.astype(BF)
            rest = rest - part.astype(F32)
            table_grad = table_grad + dot_nt(onehot, part)
        s.small[...] = jnp.zeros_like(s.small)
        lanes = width // blocks
        table_rows = bucket_count // blocks
        for at in range(blocks):
            s.small[at, 0:GAIN_ROWS, 0:lanes] = s.sums[:, at * lanes : (at + 1) * lanes]
            s.small[at, GAIN_ROWS : GAIN_ROWS + table_rows, 0 : rest.shape[0]] = table_grad[
                at * table_rows : (at + 1) * table_rows, :
            ]
        small_swap.start()

    make_all(d_down)
    piece(0.2, fetch_x, d_up)
    piece(1.2, begin)
    piece(1.8, end_feed, v.cot, v.gd_up, d_up)
    piece(1.8, back_through, v.gd_up, v.dn)
    piece(0.2, fetch_g, d_up)
    piece(1.6, residual_swap, v.d2, get_d2, gain(dec_gains, 2), 6, 9, v.gc_out, c_out)
    make_all(d_up)
    piece(0.2, fetch_x, c_out)
    piece(2.5, cross_part, 0, pairs // 2)
    piece(0.2, fetch_g, c_out)
    piece(2.5, cross_part, pairs // 2, pairs)
    make_all(c_out)
    piece(0.2, fetch_x, c_kv)
    piece(1.0, memory_part)
    piece(0.2, fetch_g, c_kv)
    piece(0.5, back_through, v.gc_query, v.dn)
    make_all(c_kv)
    piece(0.2, fetch_x, c_query)
    piece(0.2, fetch_g, c_query)
    piece(1.6, residual_swap, v.d1, get_d1, gain(dec_gains, 1), 5, 8, v.gd_out, d_out)
    make_all(c_query)
    piece(0.2, fetch_x, d_out)
    piece(2.5, dec_part, 0, pairs // 2)
    piece(0.2, fetch_g, d_out)
    piece(2.5, dec_part, pairs // 2, pairs)
    make_all(d_out)
    piece(0.2, fetch_x, d_qkv)
    piece(1.4, back_through, v.gd_qkv, v.dn)
    piece(0.2, fetch_g, d_qkv)
    piece(1.0, dec_end)
    piece(1.2, start_feed, v.ge_down, v.ge_up, get_ge_up)
    make_all(d_qkv)
    piece(0.2, fetch_x, e_down)
    piece(0.2, fetch_g, e_down)
    piece(1.8, end_feed, v.ge_down, v.ge_up, e_up)
    make_all(e_down)
    piece(0.2, fetch_x, e_up)
    piece(1.8, back_through, v.ge_up, v.dn)
    piece(0.2, fetch_g, e_up)
    piece(1.6, residual_swap, v.d2, None, gain(enc_gains, 1), 1, 3, v.ge_out, e_out)
    make_all(e_up)
    piece(0.2, fetch_x, e_out)
    piece(3.0, enc_part, 0, pairs // 2)
    piece(0.2, fetch_g, e_out)
    piece(3.0, enc_part, pairs // 2, pairs)
    make_all(e_out)
    piece(0.2, fetch_x, e_qkv)
    piece(1.4, back_through, v.ge_qkv, v.dn)
    piece(0.2, fetch_g, e_qkv)
    small_after = len(work)
    piece(2.0, small_part)
    make_all(e_qkv)

    def take_step(kind, unit, at):
        if kind == 0:
            work[unit][2]()
        elif kind == 1:
            first_copy(unit).wait_recv()

            def body(i, carry):
                s.kept[unit, i] = (s.kept[unit, i].astype(F32) + s.taken[unit, i].astype(F32)).astype(BF)
                return carry

            lax.fori_loop(0, n, body, 0)
            line_start(line_of(unit))
        elif kind == 2:
            line_hop(line_of(unit), at)
        elif kind == 3:
            line_end(line_of(unit))
            rest_copy(unit, 0).start()
        elif kind == 4:
            rest_copy(unit, at).wait_recv()
            before = s.kept[unit, d] if at == 0 else s.rest_sum[unit, at - 1]
            s.rest_sum[unit, at] = (before.astype(F32) + s.rest_got[unit, at].astype(F32)).astype(BF)
            if at < bits - 2:
                rest_copy(unit, at + 1).start()
            else:
                last_copy(unit).start()
                own_result(unit).start()
        elif kind == 5:
            last_copy(unit).wait_recv()
            got_result(unit).start()
        else:
            small_step(at)

    plan = [(time, makes) for time, makes, unused in work]
    for step in step_order(plan, small_after, units, n, bits):
        take_step(*step)

    for unit in range(units):
        if unit + rooms >= units:
            first_copy(unit).wait_send()
        line_sent(line_of(unit))
        for at in range(bits - 1):
            rest_copy(unit, at).wait_send()
        last_copy(unit).wait_send()
        own_result(unit).wait()
        got_result(unit).wait()
    small_swap.wait_send()
    for bit in range(bits):
        small_copy(bit).wait_send()
    line_sent(small_line)
    for wait in sent:
        wait()
    section_kept.wait()
    section_given.wait()


def run_backward(n, bits, xs, hbm, small_in, weights_out, g_columns, lanes, table_shape):
    length, width = hbm["d1"].shape
    half = width // 2
    block = width // (2 * n)
    first_units, unit_weight = [], []
    for at, x in enumerate(xs):
        first_units.append(len(unit_weight))
        unit_weight += [at] * max(x.shape[1] // half, g_columns[at] // width)
    units = len(unit_weight)
    any_spec = pl.BlockSpec(memory_space=pl.ANY)
    vmem_spec = pl.BlockSpec(memory_space=pltpu.VMEM)
    section = jax.ShapeDtypeStruct((1, hbm["cot"].shape[0], 1, length, width), BF)
    grads = [jax.ShapeDtypeStruct(shape, BF) for shape in weights_out]
    outs = dict(
        enc_gains=(2, lanes), enc_shifts=(2, lanes), dec_gains=(3, lanes), dec_shifts=(3, lanes), table=table_shape
    )
    outs = {name: jax.ShapeDtypeStruct(shape, F32) for name, shape in outs.items()}
    outs.update(input_grads=section)
    land_g = [jax.ShapeDtypeStruct((length, columns), BF) for columns in g_columns[1:]]
    most = max(x.shape[1] for x in xs) // half
    small_rows = -(-(GAIN_ROWS + table_shape[1]) // 16) * 16
    dma = pltpu.SemaphoreType.DMA
    small_all = pltpu.VMEM((n, small_rows, 128), F32)
    low = pltpu.VMEM((length, width), BF)
    wide = pltpu.VMEM((length, width), F32)
    held = dict(
        cot=low, x_dec=low, gc_query=low, gc_out=low, gd_out=low, ge_out=low, ge_down=low, do=low,
        dx_dec=low, d2=wide, d1=wide, stream=wide, dn=wide,
        gd_up=pltpu.VMEM((length, most * width), BF), ge_up=pltpu.VMEM((length, most * width), BF),
        gd_qkv=pltpu.VMEM((length, 3 * width), BF), ge_qkv=pltpu.VMEM((length, 3 * width), BF),
        gc_kv=pltpu.VMEM((length, 2 * width), BF), p=pltpu.VMEM((HEADS, length, length), BF),
    )
    scratch = dict(
        stream_w=pltpu.VMEM((3, 256, most * width), BF),
        x_stage=pltpu.VMEM((most, 2 * length, half), BF),
        g_stage=pltpu.VMEM((length, most * width), BF),
        factor=pltpu.VMEM((most, half, 2 * length), BF),
        kept=pltpu.VMEM((units, n, block, half), BF),
        given=pltpu.VMEM((10, n, block, half), BF),
        taken=pltpu.VMEM((units, n, block, half), BF),
        passed=pltpu.VMEM((units, n + 1, block, half), BF),
        rest_got=pltpu.VMEM((units, bits - 1, block, half), BF),
        rest_sum=pltpu.VMEM((units, bits - 1, block, half), BF),
        last_got=pltpu.VMEM((units, block, half), BF),
        sums=pltpu.VMEM((GAIN_ROWS, width), F32), diag=pltpu.VMEM((16, 2 * length), F32),
        flip=pltpu.VMEM((length, length), BF), small=pltpu.VMEM((2 * n, small_rows, 128), F32),
        small_kept=small_all, small_core=small_all,
        small_held=pltpu.VMEM((bits, n, small_rows, 128), F32),
        small_group=pltpu.VMEM((bits, n, small_rows, 128), F32),
        small_passed=pltpu.VMEM((n + 1, small_rows, 128), F32),
        load_sems=dma((15,)), stream_sems=dma((3, most)), stage_sems=dma((most + 1,)),
        swap_sent=dma((len(xs),)), swap_got=dma((len(xs),)),
        small_sent=dma((1 + bits,)), small_got=dma((1 + bits,)), small_line=dma((4,)),
        section_kept=dma, section_sent=dma, section_got=dma,
        first_sent=dma((units,)), first_got=dma((units,)), line_sems=dma((units, 4)),
        rest_sems=dma((units, bits - 1, 2)), last_sems=dma((units, 2)), result_sems=dma((units, 2)),
    )
    groups = [
        len(xs), list(hbm), list(small_in), len(grads), list(outs), len(land_g), list(held), list(scratch)
    ]
    out_specs = [any_spec] * len(grads) + [vmem_spec] * (len(outs) - 1) + [any_spec] * (1 + len(land_g))
    results = pl.pallas_call(
        functools.partial(backward_kernel, (n, bits, first_units, unit_weight), groups),
        out_shape=grads + list(outs.values()) + land_g,
        in_specs=[any_spec] * (len(xs) + len(hbm)) + [vmem_spec] * len(small_in),
        out_specs=out_specs,
        scratch_shapes=list(held.values()) + list(scratch.values()),
        compiler_params=pltpu.CompilerParams(
            collective_id=0, has_side_effects=True, vmem_limit_bytes=63 * 1024 * 1024
        ),
        name="backward",
    )(*xs, *hbm.values(), *small_in.values())
    return results[: len(grads)], dict(zip(outs, results[len(grads) :]))


def finish_kernel(counts, *refs):
    wides, total = counts
    sources, targets = refs[:total], refs[total : 2 * total]
    held, widened, sems = refs[2 * total : 3 * total], refs[3 * total : -1], refs[-1]
    loads = [pltpu.make_async_copy(sources[i], held[i], sems.at[0, i]) for i in range(total)]
    for copy in loads:
        copy.start()
    stores = []
    for i in range(total):
        loads[i].wait()
        if i < wides:
            rows = held[i].shape[0]
            for at in range(0, rows, 16):
                widened[i][at : at + 16, :] = held[i][at : at + 16, :].astype(F32)
        stores.append(pltpu.make_async_copy(widened[i] if i < wides else held[i], targets[i], sems.at[1, i]))
        stores[i].start()
    for copy in stores:
        copy.wait()


def run_finish(grads, plain):
    any_spec = pl.BlockSpec(memory_space=pl.ANY)
    arrays = list(grads) + list(plain)
    shapes = [jax.ShapeDtypeStruct(a.shape, F32) for a in grads]
    shapes += [jax.ShapeDtypeStruct(a.shape, a.dtype) for a in plain]
    scratch = [pltpu.VMEM(a.shape, a.dtype) for a in arrays] + [pltpu.VMEM(a.shape, F32) for a in grads]
    results = pl.pallas_call(
        functools.partial(finish_kernel, (len(grads), len(arrays))),
        out_shape=shapes,
        in_specs=[any_spec] * len(arrays),
        out_specs=[any_spec] * len(arrays),
        scratch_shapes=scratch + [pltpu.SemaphoreType.DMA((2, len(arrays)))],
        compiler_params=pltpu.CompilerParams(vmem_limit_bytes=63 * 1024 * 1024),
        name="finish",
    )(*arrays)
    return results[: len(grads)], results[len(grads) :]


def shards(
    section_inputs, cotangent, encoder_segments, decoder_segments, encoder_valid, decoder_valid,
    position_buckets, encoder_gains, encoder_shifts, encoder_qkv, encoder_out, encoder_up, encoder_down,
    position_table, decoder_gains, decoder_shifts, decoder_qkv, decoder_out, cross_query, cross_keyvalue,
    cross_out, decoder_up, decoder_down,
):
    width = section_inputs.shape[-1]
    dp = lax.axis_size("dp")
    bits = lax.axis_size("group").bit_length() - 1
    blocks = lax.axis_size("pipe") * dp
    weights = dict(
        e_qkv=encoder_qkv, e_out=encoder_out, e_up=encoder_up, e_down=encoder_down,
        d_qkv=decoder_qkv, d_out=decoder_out, c_query=cross_query, c_kv=cross_keyvalue,
        c_out=cross_out, d_up=decoder_up, d_down=decoder_down,
    )

    small_in = dict(
        enc_seg=encoder_segments, dec_seg=decoder_segments, enc_valid=encoder_valid, dec_valid=decoder_valid,
        buckets=position_buckets.reshape(1, -1), enc_gains=encoder_gains, enc_shifts=encoder_shifts,
        dec_gains=decoder_gains, dec_shifts=decoder_shifts, table=position_table.T,
    )
    r = run_forward(section_inputs, small_in, weights)
    f = SimpleNamespace(**r)
    xs = [f.xd_down, f.xd_up, f.xc_out, f.memory_cut, f.xc_query, f.xd_out, f.xd_qkv, f.xe_down, f.xe_up, f.xe_out, f.xe_qkv]
    order = [decoder_down, decoder_up, cross_out, cross_keyvalue, cross_query, decoder_out, decoder_qkv,
             encoder_down, encoder_up, encoder_out, encoder_qkv]
    cut = [(w.shape[0] // blocks, w.shape[1]) for w in order]
    kept = dict(
        gd_up=f.gd_up, d2=f.d2, p_cross=f.p_cross, gc_query=f.gc_query, gc_kv=f.gc_kv, d1=f.d1, p_dec=f.p_dec,
        gd_qkv=f.gd_qkv, ge_up=f.ge_up, x1=f.x1, p_enc=f.p_enc, ge_qkv=f.ge_qkv,
    )
    hbm = dict(kept, cot=cotangent, x_enc=f.x_enc, x_dec=f.x_dec, **weights)
    small_back = dict(buckets=small_in["buckets"], enc_gains=encoder_gains, dec_gains=decoder_gains)
    table_shape = (position_table.shape[1], position_table.shape[0] // blocks)
    columns = [w.shape[1] for w in order]
    grads, rest = run_backward(dp, bits, xs, hbm, small_back, cut, columns, width // blocks, table_shape)
    rest.update(outputs=f.outputs)
    grads, plain = run_finish(grads, list(rest.values()))
    s = SimpleNamespace(**dict(zip(rest, plain)))
    d_down, d_up, c_out, c_kv, c_query, d_out, d_qkv, e_down, e_up, e_out, e_qkv = grads
    return (
        s.outputs, s.input_grads, s.enc_gains, s.enc_shifts, e_qkv, e_out, e_up, e_down, s.table.T,
        s.dec_gains, s.dec_shifts, d_qkv, d_out, c_query, c_kv, c_out, d_up, d_down,
    )


def solution(mesh):
    section = P("pipe", None, ("dp", "group"), None, None)
    rows = P(None, ("dp", "group"), None)
    cut_rows = P(("pipe", "dp"), None)
    cut_lanes = P(None, ("pipe", "dp"))
    return jax.shard_map(
        shards,
        mesh=mesh,
        in_specs=(section, P(None, ("dp", "group"), None, None), rows, rows, rows, rows) + (P(),) * 17,
        out_specs=(section, section, cut_lanes, cut_lanes) + (cut_rows,) * 5 + (cut_lanes, cut_lanes) + (cut_rows,) * 7,
        check_vma=False,
    )
```

```python
import functools
from types import SimpleNamespace

import jax
import jax.numpy as jnp
from jax import lax
from jax.experimental import pallas as pl
from jax.experimental.pallas import tpu as pltpu
from jax.sharding import PartitionSpec as P

HEADS = 12
MESH = pl.DeviceIdType.MESH
NEGATIVE = -1e30
BF, F32 = jnp.bfloat16, jnp.float32
GAIN_ROWS = 16


def dot(a, b):
    return jnp.dot(a, b, preferred_element_type=F32)


def dot_nt(a, b):
    return lax.dot_general(a, b, (((1,), (1,)), ((), ())), preferred_element_type=F32)


def dot_tn(a, b):
    return lax.dot_general(a, b, (((0,), (0,)), ((), ())), preferred_element_type=F32)


def norm_stats(x):
    centre = x - jnp.mean(x, axis=-1, keepdims=True)
    spread = jnp.mean(centre * centre, axis=-1, keepdims=True)
    return centre, lax.rsqrt(spread + 1e-05)


def norm_forward(x_ref, gain, shift, n_ref):
    def body(rows):
        centre, inv = norm_stats(x_ref[rows, :].astype(F32))
        n_ref[rows, :] = (centre * inv * gain + shift).astype(BF)

    for start in range(0, x_ref.shape[0], 64):
        body(slice(start, start + 64))


def norm_backward(x_ref, gain, dn_ref, stream_ref, sums_ref, gain_at, shift_at):
    width = x_ref.shape[1]

    def step(start, dgain, dshift):
        rows = slice(start, start + 64)
        centre, inv = norm_stats(x_ref[rows, :].astype(F32))
        hat = centre * inv
        dn = dn_ref[rows, :]
        dhat = dn * gain
        mean_one = jnp.mean(dhat, axis=-1, keepdims=True)
        mean_two = jnp.mean(dhat * hat, axis=-1, keepdims=True)
        stream_ref[rows, :] += inv * (dhat - mean_one - hat * mean_two)
        return (
            dgain + jnp.sum(dn * hat, axis=0, keepdims=True),
            dshift + jnp.sum(dn, axis=0, keepdims=True),
        )

    dgain = dshift = jnp.zeros((1, width), F32)
    for start in range(0, x_ref.shape[0], 64):
        dgain, dshift = step(start, dgain, dshift)
    sums_ref[gain_at : gain_at + 1, :] = dgain
    sums_ref[shift_at : shift_at + 1, :] = dshift


def project(a_ref, w_ref, out_ref, tile=256):
    for start in range(0, w_ref.shape[1], tile):
        cols = slice(start, start + tile)
        out_ref[:, cols] = dot(a_ref[...], w_ref[:, cols]).astype(out_ref.dtype)


def project_add(a_ref, w_ref, resid_ref, out_ref, tile=256):
    for start in range(0, w_ref.shape[1], tile):
        cols = slice(start, start + tile)
        out_ref[:, cols] = (
            resid_ref[:, cols].astype(F32) + dot(a_ref[...], w_ref[:, cols])
        ).astype(out_ref.dtype)


def feed_up(n_ref, w_ref, z_ref, slope_ref, tile=512):
    for start in range(0, w_ref.shape[1], tile):
        cols = slice(start, start + tile)
        u = dot(n_ref[...], w_ref[:, cols])
        cdf = 0.5 * (1.0 + lax.erf(u * 0.7071067811865476))
        z_ref[:, cols] = (u * cdf).astype(BF)
        slope_ref[:, cols] = (cdf + u * (0.3989422804014327 * jnp.exp(-0.5 * u * u))).astype(BF)


def attend(q_ref, q_at, k_ref, k_at, v_ref, v_at, mask_ref, p_ref, o_ref, bias_ref=None):
    length = q_ref.shape[0]
    head = o_ref.shape[1] // HEADS
    pair = 2 * head
    scale = head**-0.5

    def step(i):
        def cols(at):
            return slice(at + i * pair, at + (i + 1) * pair)

        low_half = lax.broadcasted_iota(jnp.int32, (length, pair), 1) < head
        q = q_ref[:, cols(q_at)] * jnp.asarray(scale, BF)
        k = k_ref[:, cols(k_at)]
        v = v_ref[:, cols(v_at)]
        outs = []
        for half in range(2):
            own = low_half if half == 0 else jnp.logical_not(low_half)
            s = dot_nt(jnp.where(own, q, jnp.zeros_like(q)), k) + mask_ref[...]
            if bias_ref is not None:
                wide = jnp.broadcast_to(
                    bias_ref[2 * i + half : 2 * i + half + 1, :], (length, 2 * length)
                )
                s = s + pltpu.roll(wide, length, 1, stride=1, stride_axis=0)[:, :length]
            e = jnp.exp(s - jnp.max(s, axis=-1, keepdims=True))
            p = (e * (1.0 / jnp.sum(e, axis=-1, keepdims=True))).astype(BF)
            p_ref[2 * i + half] = p
            outs.append(dot(p, v))
        o_ref[:, cols(0)] = jnp.where(low_half, outs[0], outs[1]).astype(BF)

    for i in range(HEADS // 2):
        step(i)


def attend_back(
    pairs, q_ref, q_at, k_ref, k_at, v_ref, v_at, p_ref, do_ref, diag_ref=None, flip_ref=None
):
    length = q_ref.shape[0]
    head = do_ref.shape[1] // HEADS
    pair = 2 * head
    scale = head**-0.5

    def step(i):
        def cols(at):
            return slice(at + i * pair, at + (i + 1) * pair)

        low_half = lax.broadcasted_iota(jnp.int32, (length, pair), 1) < head
        q = q_ref[:, cols(q_at)]
        k = k_ref[:, cols(k_at)]
        v = v_ref[:, cols(v_at)]
        do = do_ref[:, cols(0)]
        dqs, dks, dvs = [], [], []
        for half in range(2):
            own = low_half if half == 0 else jnp.logical_not(low_half)
            p = p_ref[2 * i + half]
            dp = dot_nt(jnp.where(own, do, jnp.zeros_like(do)), v)
            wide_p = p.astype(F32)
            row = jnp.sum(wide_p * dp, axis=-1, keepdims=True)
            ds = (wide_p * (dp - row)).astype(BF)
            dvs.append(dot_tn(p, do))
            dqs.append(dot(ds, k))
            dks.append(dot_tn(ds, q))
            if diag_ref is not None:
                flipped = dot(flip_ref[...], ds)
                wide = jnp.concatenate([flipped, jnp.zeros_like(flipped)], axis=1)
                rolled = pltpu.roll(wide, 1, 1, stride=1, stride_axis=0)
                diag_ref[2 * i + half : 2 * i + half + 1, :] = jnp.sum(rolled, axis=0, keepdims=True)
        q_ref[:, cols(q_at)] = (jnp.where(low_half, dqs[0], dqs[1]) * scale).astype(BF)
        k_ref[:, cols(k_at)] = (jnp.where(low_half, dks[0], dks[1]) * scale).astype(BF)
        v_ref[:, cols(v_at)] = jnp.where(low_half, dvs[0], dvs[1]).astype(BF)

    for i in range(pairs[0], pairs[1]):
        step(i)


def build_masks(eseg, dseg, evalid, dvalid, enc_ref, dec_ref, cross_ref):
    length = enc_ref.shape[0]
    shape = (length, length)
    key = lax.broadcasted_iota(jnp.int32, shape, 1)
    query = lax.broadcasted_iota(jnp.int32, shape, 0)
    eseg_key = jnp.broadcast_to(eseg.astype(F32), shape)
    dseg_key = jnp.broadcast_to(dseg.astype(F32), shape)
    eseg_query, dseg_query = eseg_key.T, dseg_key.T
    evalid_key = jnp.broadcast_to(evalid, shape) == 1
    dvalid_key = jnp.broadcast_to(dvalid, shape) == 1
    before = pltpu.roll(eseg_key, 1, 1)
    first = (key == 0) | (eseg_key != before)
    enc = (eseg_query == eseg_key) & (evalid_key | (key == query))
    dec = (dseg_query == dseg_key) & (dvalid_key | (key == query)) & (key <= query)
    cross = (dseg_query == eseg_key) & (evalid_key | first)
    enc_ref[...] = jnp.where(enc, 0.0, NEGATIVE)
    dec_ref[...] = jnp.where(dec, 0.0, NEGATIVE)
    cross_ref[...] = jnp.where(cross, 0.0, NEGATIVE)


def bucket_onehot(buckets, bucket_count):
    shape = (bucket_count, buckets.shape[1])
    return jnp.broadcast_to(buckets, shape) == lax.broadcasted_iota(jnp.int32, shape, 0)


def forward_kernel(groups, *refs):
    spaces = []
    for names in groups:
        spaces.append(SimpleNamespace(**dict(zip(names, refs))))
        refs = refs[len(names) :]
    hbm, small_in, out, v, s = spaces
    pipe = lax.axis_index("pipe")
    length, width = v.x_enc.shape
    started, pending = [], []

    def load(source, target):
        copy = pltpu.make_async_copy(source, target, s.sem_in.at[len(started)])
        copy.start()
        started.append(copy)
        return copy

    def store(source, target):
        copy = pltpu.make_async_copy(source, target, s.sem_out.at[len(pending)])
        copy.start()
        pending.append(copy)

    core = (1 - pipe, lax.axis_index("dp"), lax.axis_index("group"))
    barrier = pltpu.get_barrier_semaphore()
    pl.semaphore_signal(barrier, inc=1, device_id=core, device_id_type=MESH)
    mine, other = hbm.section_inputs.at[0, pipe, 0], hbm.section_inputs.at[0, 1 - pipe, 0]

    def keep(target):
        return pltpu.make_async_copy(mine, target, s.swap_sems.at[0])

    def give(target):
        return pltpu.make_async_remote_copy(
            src_ref=other, dst_ref=target, send_sem=s.swap_sems.at[1], recv_sem=s.swap_sems.at[2],
            device_id=core, device_id_type=MESH,
        )

    @pl.when(pipe == 0)
    def _():
        keep(v.x_enc).start()

    @pl.when(pipe == 1)
    def _():
        keep(v.x_dec).start()

    shared = []

    def share(source, target):
        part = source.shape[1] // 2
        ours = pl.ds(pl.multiple_of(pipe * part, 128), part)
        theirs = pl.ds(pl.multiple_of((1 - pipe) * part, 128), part)
        store(source.at[:, ours], target.at[0:length])
        copy = pltpu.make_async_remote_copy(
            src_ref=source.at[:, theirs], dst_ref=target.at[length : 2 * length],
            send_sem=s.share_sent.at[len(shared)], recv_sem=s.share_got.at[len(shared)],
            device_id=core, device_id_type=MESH,
        )
        copy.start()
        shared.append(copy)

    get_e_qkv = load(hbm.e_qkv, s.e_qkv)
    get_e_out = load(hbm.e_out, s.e_out)
    get_e_up = load(hbm.e_up, s.up)
    get_e_down = load(hbm.e_down, s.down)
    get_d_qkv = load(hbm.d_qkv, s.d_qkv)
    get_d_out = load(hbm.d_out, s.d_out)
    get_c_query = load(hbm.c_query, s.c_query)
    get_c_kv = load(hbm.c_kv, s.c_kv)
    get_c_out = load(hbm.c_out, s.c_out)
    pl.semaphore_wait(barrier, 1)

    @pl.when(pipe == 0)
    def _():
        give(v.x_enc).start()

    @pl.when(pipe == 1)
    def _():
        give(v.x_dec).start()


    build_masks(
        small_in.enc_seg[pipe], small_in.dec_seg[pipe], small_in.enc_valid[pipe], small_in.dec_valid[pipe],
        s.mask_enc, s.mask_dec, s.mask_cross,
    )
    buckets = small_in.buckets[...]
    s.bias[0:HEADS, :] = dot(small_in.table[...], bucket_onehot(buckets, small_in.table.shape[1]).astype(BF))
    def at(ref, row):
        return ref[row : row + 1, :].astype(F32)

    enc_gains, enc_shifts = small_in.enc_gains, small_in.enc_shifts
    dec_gains, dec_shifts = small_in.dec_gains, small_in.dec_shifts

    @pl.when(pipe == 0)
    def _():
        keep(v.x_enc).wait()

    @pl.when(pipe == 1)
    def _():
        give(v.x_enc).wait_recv()

    store(v.x_enc, out.x_enc)
    norm_forward(v.x_enc, at(enc_gains, 0), at(enc_shifts, 0), v.xe_qkv)
    share(v.xe_qkv, out.xe_qkv)
    get_e_qkv.wait()
    project(v.xe_qkv, s.e_qkv, v.ge_qkv)
    attend(v.ge_qkv, 0, v.ge_qkv, width, v.ge_qkv, 2 * width, s.mask_enc, v.p_enc, v.xe_out, s.bias)
    store(v.ge_qkv, out.ge_qkv)
    store(v.p_enc, out.p_enc)
    share(v.xe_out, out.xe_out)
    get_e_out.wait()
    project_add(v.xe_out, s.e_out, v.x_enc, v.x1)
    store(v.x1, out.x1)
    norm_forward(v.x1, at(enc_gains, 1), at(enc_shifts, 1), v.xe_up)
    share(v.xe_up, out.xe_up)
    get_e_up.wait()
    feed_up(v.xe_up, s.up, v.xe_down, v.ge_up)
    get_d_up = load(hbm.d_up, s.up)
    share(v.xe_down, out.xe_down)
    store(v.ge_up, out.ge_up)
    get_e_down.wait()
    project_add(v.xe_down, s.down, v.x1, v.memory)
    get_d_down = load(hbm.d_down, s.down)
    share(v.memory, out.memory_cut)

    @pl.when(pipe == 0)
    def _():
        give(v.x_dec).wait_recv()

    @pl.when(pipe == 1)
    def _():
        keep(v.x_dec).wait()

    store(v.x_dec, out.x_dec)
    norm_forward(v.x_dec, at(dec_gains, 0), at(dec_shifts, 0), v.xd_qkv)
    share(v.xd_qkv, out.xd_qkv)
    get_d_qkv.wait()
    project(v.xd_qkv, s.d_qkv, v.gd_qkv)
    attend(v.gd_qkv, 0, v.gd_qkv, width, v.gd_qkv, 2 * width, s.mask_dec, v.p_dec, v.xd_out)
    share(v.xd_out, out.xd_out)
    store(v.gd_qkv, out.gd_qkv)
    store(v.p_dec, out.p_dec)
    get_d_out.wait()
    project_add(v.xd_out, s.d_out, v.x_dec, v.d1)
    store(v.d1, out.d1)
    norm_forward(v.d1, at(dec_gains, 1), at(dec_shifts, 1), v.xc_query)
    share(v.xc_query, out.xc_query)
    get_c_query.wait()
    project(v.xc_query, s.c_query, v.gc_query)
    get_c_kv.wait()
    project(v.memory, s.c_kv, v.gc_kv)
    attend(v.gc_query, 0, v.gc_kv, 0, v.gc_kv, width, s.mask_cross, v.p_cross, v.xc_out)
    share(v.xc_out, out.xc_out)
    store(v.gc_query, out.gc_query)
    store(v.gc_kv, out.gc_kv)
    store(v.p_cross, out.p_cross)
    get_c_out.wait()
    project_add(v.xc_out, s.c_out, v.d1, v.d2)
    store(v.d2, out.d2)
    norm_forward(v.d2, at(dec_gains, 2), at(dec_shifts, 2), v.xd_up)
    share(v.xd_up, out.xd_up)
    get_d_up.wait()
    feed_up(v.xd_up, s.up, v.xd_down, v.gd_up)
    share(v.xd_down, out.xd_down)
    store(v.gd_up, out.gd_up)
    get_d_down.wait()
    project_add(v.xd_down, s.down, v.d2, v.decoded)

    def section(layer, ref):
        @pl.when(pipe == layer)
        def _():
            pltpu.make_async_copy(ref, out.outputs.at[0, pipe, 0], s.section_sems.at[0]).start()

        @pl.when(pipe != layer)
        def _():
            pltpu.make_async_remote_copy(
                src_ref=ref, dst_ref=out.outputs.at[0, pipe, 0], send_sem=s.section_sems.at[1],
                recv_sem=s.section_sems.at[2], device_id=core, device_id_type=MESH,
            ).start()

    section(0, v.memory)
    section(1, v.decoded)

    give(v.x_enc).wait_send()
    pltpu.make_async_copy(v.memory, out.outputs.at[0, pipe, 0], s.section_sems.at[0]).wait()
    pltpu.make_async_remote_copy(
        src_ref=v.memory, dst_ref=out.outputs.at[0, 1 - pipe, 0], send_sem=s.section_sems.at[1],
        recv_sem=s.section_sems.at[2], device_id=core, device_id_type=MESH,
    ).wait()
    for copy in pending + shared:
        copy.wait()


def run_forward(section_inputs, small_in, weights):
    unused, micro, unused, length, width = section_inputs.shape
    hidden = weights["e_up"].shape[1]
    hbm = dict(section_inputs=section_inputs, **weights)
    any_spec = pl.BlockSpec(memory_space=pl.ANY)
    vmem_spec = pl.BlockSpec(memory_space=pltpu.VMEM)
    columns = dict(
        ge_qkv=3 * width, ge_up=hidden, gd_qkv=3 * width, gc_query=width, gc_kv=2 * width, gd_up=hidden,
        x_enc=width, x_dec=width,
    )
    inputs = dict(
        xe_qkv=width, xe_out=width, xe_up=width, xe_down=hidden, xd_qkv=width, xd_out=width, xc_query=width,
        xc_out=width, xd_up=width, xd_down=hidden,
    )
    outs = {name: jax.ShapeDtypeStruct((length, n), BF) for name, n in columns.items()}
    probabilities = jax.ShapeDtypeStruct((HEADS, length, length), BF)
    rows = jax.ShapeDtypeStruct((length, width), F32)
    outs.update(p_enc=probabilities, p_dec=probabilities, p_cross=probabilities, x1=rows, d1=rows, d2=rows)
    held = {name: pltpu.VMEM(shape.shape, shape.dtype) for name, shape in outs.items()}
    held.update({name: pltpu.VMEM((length, n), BF) for name, n in inputs.items()})
    held.update(memory=pltpu.VMEM((length, width), BF), decoded=pltpu.VMEM((length, width), BF))
    outs.update({name: jax.ShapeDtypeStruct((2 * length, n // 2), BF) for name, n in inputs.items()})
    outs.update(outputs=jax.ShapeDtypeStruct((1, micro, 1, length, width), BF))
    outs.update(memory_cut=jax.ShapeDtypeStruct((2 * length, width // 2), BF))
    square = pltpu.VMEM((length, length), F32)
    scratch = {
        name: pltpu.VMEM(w.shape, BF) for name, w in weights.items() if hidden not in w.shape
    }
    scratch.update(
        up=pltpu.VMEM((width, hidden), BF), down=pltpu.VMEM((hidden, width), BF),
        mask_enc=square, mask_dec=square, mask_cross=square, bias=pltpu.VMEM((16, 2 * length), F32),
        section_sems=pltpu.SemaphoreType.DMA((3,)), swap_sems=pltpu.SemaphoreType.DMA((3,)), share_sent=pltpu.SemaphoreType.DMA((len(inputs) + 1,)),
        share_got=pltpu.SemaphoreType.DMA((len(inputs) + 1,)), sem_in=pltpu.SemaphoreType.DMA((16,)), sem_out=pltpu.SemaphoreType.DMA((len(outs),)),
    )
    groups = [list(part) for part in (hbm, small_in, outs, held, scratch)]
    results = pl.pallas_call(
        functools.partial(forward_kernel, groups),
        out_shape=list(outs.values()),
        in_specs=[any_spec] * len(hbm) + [vmem_spec] * len(small_in),
        out_specs=[any_spec] * len(outs),
        scratch_shapes=list(held.values()) + list(scratch.values()),
        compiler_params=pltpu.CompilerParams(
            collective_id=1, has_side_effects=True, vmem_limit_bytes=63 * 1024 * 1024
        ),
        name="forward",
    )(*hbm.values(), *small_in.values())
    return dict(zip(outs, results))


PAIRED = ()


def step_order(work, small_after, sides_of, pairs, n, bits, window=3):
    big, delay, cost = 6.6, 2.0, 0.5
    small = big / n
    sides, line = [0.0, 0.0], [0.0] * n
    waiting, steps = [], []
    flying = [0, 0]
    clock, made, done = 0.0, 0, 0

    def message(free, at, start, size):
        free[at] = max(free[at], start) + size
        return free[at] + delay

    while done < len(work) or waiting:
        ready = [event for event in waiting if event[0] <= clock]
        if ready:
            event = min(ready)
            waiting.remove(event)
            unused, kind, unit, at = event
            steps.append((kind, unit, at))
            clock += cost
            first = sides_of[unit]
            other = 1 - first
            paired = unit in pairs
            if kind == 1:
                flying[first] -= 1
                if unit - 1 in pairs:
                    waiting.append((message(sides, other, clock, big), 7, unit - 1, 0))
            if kind == 7 or kind == 1 and not paired and unit - 1 not in pairs:
                waiting.append((message(line, 1, clock, (n - 1) * small), 2 if n > 2 else 3, unit, 1))
            elif kind == 2:
                arrival = message(line, at + 1, clock, (n - 1 - at) * small)
                waiting.append((arrival, 2 if at + 1 < n - 1 else 3, unit, at + 1))
            elif kind == 3 or kind == 4:
                following = 0 if kind == 3 else at + 1
                if following < bits - 1 - paired:
                    waiting.append((message(sides, other, clock, small), 4, unit, following))
                elif paired:
                    waiting.append((message(sides, other, clock, small), 8, unit, 0))
                else:
                    waiting.append((message(sides, first, clock, small), 5, unit, 0))
            elif kind == 8:
                waiting.append((message(sides, first, clock, 2 * small), 5, unit, 0))
            elif kind == 6 and at + 1 < bits + n:
                waiting.append((clock + 2 * delay, 6, 0, at + 1))
        elif done < len(work) and (not work[done][1] or flying[sides_of[made]] < window):
            clock += work[done][0]
            steps.append((0, done, 0))
            if work[done][1]:
                waiting.append((message(sides, sides_of[made], clock, big), 1, made, 0))
                flying[sides_of[made]] += 1
                made += 1
            if done == small_after:
                waiting.append((clock + delay, 6, 0, 0))
            done += 1
        else:
            clock = min(waiting)[0]
    return steps


def pick_sides(pairs, units):
    sides, loads = [], [0.0, 0.0]
    for unit in range(units):
        if unit - 1 in pairs:
            side = sides[-1]
            loads[side] += 1.0
        elif unit in pairs:
            side = 0 if loads[0] <= loads[1] else 1
            loads[side] += 1.0
            loads[1 - side] += 1.0
        else:
            side = 0 if loads[0] <= loads[1] else 1
            loads[side] += 1.0
        sides.append(side)
    return sides


def backward_kernel(tables, groups, *refs):
    spaces = []
    for names in groups:
        if isinstance(names, int):
            spaces.append(refs[:names])
            refs = refs[names:]
        else:
            spaces.append(SimpleNamespace(**dict(zip(names, refs))))
            refs = refs[len(names) :]
    xs, hbm, small_in, grads, out, land_g, v, s = spaces
    n, bits, first_units, unit_weight, pairs, sides_of = tables
    p, d, g = lax.axis_index("pipe"), lax.axis_index("dp"), lax.axis_index("group")
    units = len(unit_weight)
    length, width = v.stream.shape
    half = width // 2
    block = width // (2 * n)
    blocks = 2 * n
    gs = [
        v.cot, v.gd_up, v.gc_out, v.gc_kv, v.gc_query, v.gd_out, v.gd_qkv, v.ge_down, v.ge_up, v.ge_out, v.ge_qkv
    ]
    d_down, d_up, c_out, c_kv, c_query, d_out, d_qkv, e_down, e_up, e_out, e_qkv = range(len(gs))

    def bit_of(bit):
        return (g // 2**bit) % 2

    def across(bit):
        return (p, d, g + (1 - 2 * bit_of(bit)) * 2**bit)

    core = (1 - p, d, g)
    above, below = (p, d + 1, g), (p, d - 1, g)

    loads = []

    def load(source, target):
        copy = pltpu.make_async_copy(source, target, s.load_sems.at[len(loads)])
        copy.start()
        loads.append(copy)
        return copy

    get_cot = load(hbm.cot.at[p, 0], v.cot)

    def tiles_of(at):
        return xs[at].shape[1] // half

    fetched = {}

    def fetch_x(at):
        for tile in range(tiles_of(at)):
            copy = pltpu.make_async_copy(
                xs[at].at[:, tile * half : (tile + 1) * half], s.x_stage.at[tile], s.stage_sems.at[tile]
            )
            copy.start()
            fetched.setdefault(at, []).append(copy)

    def fetch_g(at):
        if at > 0:
            g_swaps[at].wait_recv()
        source = hbm.cot.at[1 - p, 0] if at == 0 else land_g[at - 1]
        copy = pltpu.make_async_copy(
            source, s.g_stage.at[:, 0 : source.shape[1]], s.stage_sems.at[s.stage_sems.shape[0] - 1]
        )
        copy.start()
        fetched[at].append(copy)

    fetch_x(d_down)
    fetch_g(d_down)

    slots, side, reach = s.stream_w.shape
    chunks = []
    for ref in (
        hbm.d_down, hbm.d_up, hbm.c_out, hbm.c_kv, hbm.c_query, hbm.d_out, hbm.d_qkv, hbm.e_down, hbm.e_up,
        hbm.e_out, hbm.e_qkv,
    ):
        columns = ref.shape[1]
        together = reach // columns
        for first in range(0, ref.shape[0], together * side):
            last = min(ref.shape[0], first + together * side)
            chunks.append([(ref.at[row : row + side, :], (row - first) // side * columns, columns) for row in range(first, last, side)])
    walked = [0]

    def chunk_copies(at):
        return [
            pltpu.make_async_copy(
                source, s.stream_w.at[at % slots, :, start : start + columns], s.stream_sems.at[at % slots, i]
            )
            for i, (source, start, columns) in enumerate(chunks[at])
        ]

    def start_chunk(at):
        if at < len(chunks):
            for copy in chunk_copies(at):
                copy.start()

    for at in range(slots):
        start_chunk(at)

    def next_rows(g_ref, put, row):
        at = walked[0]
        walked[0] += 1
        for copy in chunk_copies(at):
            copy.wait()
        for unused, start, columns in chunks[at]:
            put(slice(row, row + side), dot_nt(g_ref[...], s.stream_w[at % slots, :, start : start + columns]))
            row += side
        start_chunk(at + slots)
        return row

    def back_through(g_ref, out_ref):
        def put(cols, part):
            out_ref[:, cols] = part.astype(out_ref.dtype)

        row = 0
        while row < out_ref.shape[1]:
            row = next_rows(g_ref, put, row)

    def back_through_feed(g_ref, slope_ref, start, stop):
        def put(cols, part):
            slope_ref[:, cols] = (part * slope_ref[:, cols].astype(F32)).astype(BF)

        row = start
        while row < stop:
            row = next_rows(g_ref, put, row)

    get_gd_up = load(hbm.gd_up, v.gd_up)
    get_d2 = load(hbm.d2, v.d2)
    get_p = [load(hbm.p_cross, v.p)]
    get_gc_query = load(hbm.gc_query, v.gc_query)
    get_gc_kv = load(hbm.gc_kv, v.gc_kv)
    get_d1 = load(hbm.d1, v.d1)
    get_gd_qkv = load(hbm.gd_qkv, v.gd_qkv)
    get_x_dec = load(hbm.x_dec, v.x_dec)
    get_ge_up = load(hbm.ge_up, v.ge_up)
    get_ge_qkv = load(hbm.ge_qkv, v.ge_qkv)

    barrier = pltpu.get_barrier_semaphore()
    pl.semaphore_signal(barrier, inc=1, device_id=core, device_id_type=MESH)
    for bit in range(bits):
        pl.semaphore_signal(barrier, inc=1, device_id=across(bit), device_id_type=MESH)

    @pl.when(d > 0)
    def _():
        pl.semaphore_signal(barrier, inc=1, device_id=below, device_id_type=MESH)

    @pl.when(d < n - 1)
    def _():
        pl.semaphore_signal(barrier, inc=1, device_id=above, device_id_type=MESH)

    @pl.when((d > 0) & (d < n - 1))
    def _():
        pl.semaphore_wait(barrier, 3 + bits)

    @pl.when((d == 0) | (d == n - 1))
    def _():
        pl.semaphore_wait(barrier, 2 + bits)

    def remote(source, target, send_sem, recv_sem, device):
        return pltpu.make_async_remote_copy(
            src_ref=source, dst_ref=target, send_sem=send_sem, recv_sem=recv_sem,
            device_id=device, device_id_type=MESH,
        )

    sent = []

    def send(copy):
        copy.start()
        sent.append(copy.wait_send)
        return copy

    g_swaps = {}

    def swap_g(at):
        g_swaps[at] = send(
            remote(gs[at], land_g[at - 1], s.swap_sent.at[at], s.swap_got.at[at], core)
        )

    def input_grad(layer, ref):
        @pl.when(p == layer)
        def _():
            pltpu.make_async_copy(ref, out.input_grads.at[0, p, 0], s.section_kept).start()

        @pl.when(p != layer)
        def _():
            remote(ref, out.input_grads.at[0, p, 0], s.section_sent, s.section_got, core).start()

    section_kept = pltpu.make_async_copy(v.do, out.input_grads.at[0, p, 0], s.section_kept)
    section_given = remote(v.do, out.input_grads.at[0, 1 - p, 0], s.section_sent, s.section_got, core)

    def first_bit(unit):
        return 0 if sides_of[unit] == 0 else bits - 1

    def second_bit(unit):
        return bits - 1 - first_bit(unit)

    def held_unit(unit):
        return unit + bit_of(second_bit(unit))

    def other_unit(unit):
        return unit + 1 - bit_of(second_bit(unit))

    rooms = s.given.shape[0]

    def first_copy(unit):
        return remote(
            s.given.at[unit % rooms], s.taken.at[unit], s.first_sent.at[unit], s.first_got.at[unit],
            across(first_bit(unit)),
        )

    def product(at, tile, cols):
        value = dot(s.factor[tile, :, 0:length], gs[at][:, cols])
        return (value + dot(s.factor[tile, :, length : 2 * length], s.g_stage[:, cols])).astype(BF)

    def room_free(unit):
        if unit >= rooms:
            first_copy(unit - rooms).wait_send()

    def make(unit):
        at = unit_weight[unit]
        base = first_units[at]
        tiles = tiles_of(at)
        if unit == base and tiles == 1:
            for copy in fetched.pop(at):
                copy.wait()
            s.factor[0] = s.x_stage[0].T
        if tiles == 1:
            room_free(unit)
            mine = bit_of(first_bit(unit))
            column = (unit - base) * width
            given = product(at, 0, pl.ds(pl.multiple_of(column + (1 - mine) * half, 128), half))
            for i in range(n):
                s.given[unit % rooms, i] = given[i * block : (i + 1) * block]
            first_copy(unit).start()
            kept = product(at, 0, pl.ds(pl.multiple_of(column + mine * half, 128), half))
            for i in range(n):
                s.kept[unit, i] = kept[i * block : (i + 1) * block]
            return
        first_copy(unit).start()

    def make_tile(at, tile):
        base, tiles = first_units[at], tiles_of(at)
        if tile == 0:
            if at == 0:
                get_cot.wait()
            for copy in fetched.pop(at):
                copy.wait()
            for i in range(tiles):
                room_free(base + i)
        s.factor[tile] = s.x_stage[tile].T
        for which in range(2):
            split_rows(base, tiles, tile, which, product(at, tile, slice(which * half, (which + 1) * half)))

    def split_rows(base, tiles, tile, which, value):
        for i in range(n):
            unit = base + (tile * n + i) % tiles
            at = (tile * n + i) // tiles
            mine = bit_of(first_bit(unit))
            rows = value[i * block : (i + 1) * block]

            @pl.when(mine == which)
            def _(unit=unit, at=at, rows=rows):
                s.kept[unit, at] = rows

            @pl.when(mine != which)
            def _(unit=unit, at=at, rows=rows):
                s.given[unit % rooms, at] = rows

    def add(target, index, source, source_index):
        target[index] += source[source_index]

    def up_copy(line, dd):
        source = line.kept.at[1:n] if dd == 0 else line.passed.at[dd + 2 : n + 1]
        return remote(source, line.passed.at[dd + 2 : n + 1], line.sems.at[0], line.sems.at[1], above)

    def down_copy(line, dd):
        source = line.kept.at[0 : n - 1] if dd == n - 1 else line.passed.at[0:dd]
        return remote(source, line.passed.at[0:dd], line.sems.at[2], line.sems.at[3], below)

    def line_start(line):
        @pl.when(d == 0)
        def _():
            up_copy(line, 0).start()

        @pl.when(d == n - 1)
        def _():
            down_copy(line, n - 1).start()

    def line_hop(line, hop):
        @pl.when(d == hop)
        def _():
            up_copy(line, hop - 1).wait_recv()
            for i in range(hop + 1, n):
                add(line.passed, i + 1, line.kept, i)
            up_copy(line, hop).start()

        @pl.when(d == n - 1 - hop)
        def _():
            down_copy(line, n - hop).wait_recv()
            for i in range(n - 1 - hop):
                add(line.passed, i, line.kept, i)
            down_copy(line, n - 1 - hop).start()

    def line_end(line):
        @pl.when(d == n - 1)
        def _():
            up_copy(line, n - 2).wait_recv()
            line.kept[n - 1] = (
                line.kept[n - 1].astype(F32) + line.passed[n].astype(F32)
            ).astype(line.kept.dtype)

        @pl.when(d == 0)
        def _():
            down_copy(line, 1).wait_recv()
            line.kept[0] = (line.kept[0].astype(F32) + line.passed[0].astype(F32)).astype(line.kept.dtype)

        for dd in range(1, n - 1):

            @pl.when(d == dd)
            def _(dd=dd):
                line.kept[dd] = (
                    line.kept[dd].astype(F32) + line.passed[dd + 1].astype(F32) + line.passed[dd].astype(F32)
                ).astype(line.kept.dtype)

    def line_sent(line):
        for dd in range(n):

            @pl.when(d == dd)
            def _(dd=dd):
                if dd < n - 1:
                    up_copy(line, dd).wait_send()
                if dd > 0:
                    down_copy(line, dd).wait_send()

    def line_unit(unit):
        return held_unit(unit) if unit in pairs else unit

    def line_of(unit):
        return SimpleNamespace(
            kept=s.kept.at[line_unit(unit)], passed=s.passed.at[unit], sems=s.line_sems.at[unit]
        )

    def rest_bits(unit):
        done = (first_bit(unit), second_bit(unit)) if unit in pairs else (first_bit(unit),)
        return [bit for bit in range(bits) if bit not in done]

    def pair_copy(unit):
        return remote(
            s.kept.at[other_unit(unit)], s.passed.at[unit + 1, 0:n], s.pair_sems.at[unit, 0],
            s.pair_sems.at[unit, 1], across(second_bit(unit)),
        )

    def pair_sum(unit):
        return s.kept.at[held_unit(unit), d] if bits == 2 else s.rest_sum.at[unit, bits - 3]

    def pair_back(unit):
        return remote(
            pair_sum(unit), s.rest_got.at[unit, bits - 2], s.rest_sems.at[unit, bits - 2, 0],
            s.rest_sems.at[unit, bits - 2, 1], across(second_bit(unit)),
        )

    def pair_last(unit, other):
        source = s.rest_got.at[unit, bits - 2] if other else pair_sum(unit)
        target = s.last_got.at[other_unit(unit) if other else held_unit(unit)]
        sems = s.last_sems.at[unit + other]
        return remote(source, target, sems.at[0], sems.at[1], across(first_bit(unit)))

    def pair_result(unit, other):
        source = s.rest_got.at[unit, bits - 2] if other else pair_sum(unit)
        chosen = other_unit(unit) if other else held_unit(unit)
        return pltpu.make_async_copy(
            source, result_at(unit, bit_of(first_bit(unit)), chosen - unit), s.result_sems.at[unit + other, 0]
        )

    def rest_copy(unit, at):
        source = s.kept.at[line_unit(unit), d] if at == 0 else s.rest_sum.at[unit, at - 1]
        return remote(
            source, s.rest_got.at[unit, at], s.rest_sems.at[unit, at, 0], s.rest_sems.at[unit, at, 1],
            across(rest_bits(unit)[at]),
        )

    def last_copy(unit):
        return remote(
            s.rest_sum.at[unit, bits - 2], s.last_got.at[unit], s.last_sems.at[unit, 0], s.last_sems.at[unit, 1],
            across(first_bit(unit)),
        )

    def result_at(unit, which, ahead=0):
        at = unit_weight[unit]
        k = unit - first_units[at] + ahead
        target = grads[at]
        if tiles_of(at) == 1:
            return target.at[:, pl.ds(pl.multiple_of(k * width + which * half, 128), half)]
        return target.at[pl.ds(pl.multiple_of(k * block, 16), block), pl.ds(pl.multiple_of(which * half, 128), half)]

    def own_result(unit):
        return pltpu.make_async_copy(
            s.rest_sum.at[unit, bits - 2], result_at(unit, bit_of(first_bit(unit))), s.result_sems.at[unit, 0]
        )

    def got_result(unit):
        return pltpu.make_async_copy(
            s.last_got.at[unit], result_at(unit, 1 - bit_of(first_bit(unit))), s.result_sems.at[unit, 1]
        )

    small_line = SimpleNamespace(kept=s.small_kept, passed=s.small_passed, sems=s.small_line)
    small_swap = remote(
        s.small.at[pl.ds((1 - p) * n, n)], s.small_core, s.small_sent.at[0], s.small_got.at[0], core
    )

    def small_copy(bit):
        return remote(
            s.small_held.at[bit], s.small_group.at[bit], s.small_sent.at[1 + bit], s.small_got.at[1 + bit], across(bit)
        )

    def small_step(at):
        if at == 0:
            small_swap.wait_recv()
            s.small_kept[...] = s.small[pl.ds(p * n, n)] + s.small_core[...]
        elif at <= bits:
            small_copy(at - 1).wait_recv()
            s.small_kept[...] += s.small_group[at - 1]
        if at < bits:
            s.small_held[at] = s.small_kept[...]
            small_copy(at).start()
        elif at == bits:
            line_start(small_line)
        elif at < bits + n - 1:
            line_hop(small_line, at - bits)
        else:
            line_end(small_line)
            total = s.small_kept[d]
            lanes = out.enc_gains.shape[1]
            for ref, row in (
                (out.enc_gains, 0), (out.enc_shifts, 2), (out.dec_gains, 4), (out.dec_shifts, 7)
            ):
                ref[...] = total[row : row + ref.shape[0], 0:lanes]
            out.table[...] = total[GAIN_ROWS:].T[0:HEADS, 0 : out.table.shape[1]]

    def gain(ref, row):
        return ref[row : row + 1, :].astype(F32)

    enc_gains, dec_gains = small_in.enc_gains, small_in.dec_gains
    head_pairs = HEADS // 2
    work = []

    def piece(time, body, *args):
        work.append((time, False, functools.partial(body, *args)))

    def make_all(at):
        count = max(tiles_of(at), gs[at].shape[1] // width)
        if tiles_of(at) > 1:
            for tile in range(tiles_of(at)):
                piece(1.1, make_tile, at, tile)
        for i in range(count):
            first_time = 1.2 if tiles_of(at) == 1 else 0.1
            later = 0.8 if tiles_of(at) == 1 else 0.1
            work.append((first_time if i == 0 else later, True, functools.partial(make, first_units[at] + i)))

    def start_feed(g_ref, slope_ref, get):
        get.wait()
        back_through_feed(g_ref, slope_ref, 0, slope_ref.shape[1] // 3)

    def end_feed(g_ref, slope_ref, at):
        back_through_feed(g_ref, slope_ref, slope_ref.shape[1] // 3, slope_ref.shape[1])
        swap_g(at)

    get_late = []

    def residual(x_ref, get, gain_row, gain_at, shift_at, low_ref):
        (get_late.pop(0) if get is None else get).wait()
        norm_backward(x_ref, gain_row, v.dn, v.stream, s.sums, gain_at, shift_at)
        low_ref[...] = v.stream[...].astype(BF)

    def residual_swap(x_ref, get, gain_row, gain_at, shift_at, low_ref, at):
        residual(x_ref, get, gain_row, gain_at, shift_at, low_ref)
        if x_ref is v.d2 and at == c_out:
            get_late.append(load(hbm.x1, v.d2))
        swap_g(at)
        back_through(low_ref, v.do)

    def begin():
        s.sums[...] = jnp.zeros_like(s.sums)
        v.stream[...] = v.cot[...].astype(F32)
        start_feed(v.cot, v.gd_up, get_gd_up)

    def cross_part(first, last):
        if first == 0:
            get_p[0].wait()
            get_gc_query.wait()
            get_gc_kv.wait()
        attend_back((first, last), v.gc_query, 0, v.gc_kv, 0, v.gc_kv, width, v.p, v.do)
        if last == head_pairs:
            get_p.append(load(hbm.p_dec, v.p))
            swap_g(c_kv)
            swap_g(c_query)

    def dec_part(first, last):
        if first == 0:
            get_p[1].wait()
            get_gd_qkv.wait()
        attend_back((first, last), v.gd_qkv, 0, v.gd_qkv, width, v.gd_qkv, 2 * width, v.p, v.do)
        if last == head_pairs:
            get_p.append(load(hbm.p_enc, v.p))
            swap_g(d_qkv)

    def enc_part(first, last):
        if first == 0:
            get_p[2].wait()
            get_ge_qkv.wait()
            s.diag[...] = jnp.zeros_like(s.diag)
            flip_shape = (length, length)
            s.flip[...] = (
                lax.broadcasted_iota(jnp.int32, flip_shape, 0) + lax.broadcasted_iota(jnp.int32, flip_shape, 1)
                == length - 1
            ).astype(BF)
        attend_back(
            (first, last), v.ge_qkv, 0, v.ge_qkv, width, v.ge_qkv, 2 * width, v.p, v.do, s.diag, s.flip
        )
        if last == head_pairs:
            swap_g(e_qkv)

    def memory_part():
        back_through(v.gc_kv, v.ge_down)
        swap_g(e_down)

    def dec_end():
        residual(v.x_dec, get_x_dec, gain(dec_gains, 0), 4, 7, v.dx_dec)
        input_grad(1, v.dx_dec)
        get_late.append(load(hbm.x_enc, v.x_dec))
        v.stream[...] = v.ge_down[...].astype(F32)

    def small_part():
        residual(v.x_dec, None, gain(enc_gains, 0), 0, 2, v.do)
        input_grad(0, v.do)
        buckets = small_in.buckets[...]
        bucket_count = out.table.shape[1] * blocks
        onehot = bucket_onehot(buckets, bucket_count).astype(BF)
        rest = s.diag[...]
        table_grad = jnp.zeros((bucket_count, rest.shape[0]), F32)
        for unused in range(3):
            part = rest.astype(BF)
            rest = rest - part.astype(F32)
            table_grad = table_grad + dot_nt(onehot, part)
        s.small[...] = jnp.zeros_like(s.small)
        lanes = width // blocks
        table_rows = bucket_count // blocks
        for at in range(blocks):
            s.small[at, 0:GAIN_ROWS, 0:lanes] = s.sums[:, at * lanes : (at + 1) * lanes]
            s.small[at, GAIN_ROWS : GAIN_ROWS + table_rows, 0 : rest.shape[0]] = table_grad[
                at * table_rows : (at + 1) * table_rows, :
            ]
        small_swap.start()

    make_all(d_down)
    piece(0.2, fetch_x, d_up)
    piece(1.2, begin)
    piece(1.8, end_feed, v.cot, v.gd_up, d_up)
    piece(1.8, back_through, v.gd_up, v.dn)
    piece(0.2, fetch_g, d_up)
    piece(1.6, residual_swap, v.d2, get_d2, gain(dec_gains, 2), 6, 9, v.gc_out, c_out)
    make_all(d_up)
    piece(0.2, fetch_x, c_out)
    piece(2.5, cross_part, 0, head_pairs // 2)
    piece(0.2, fetch_g, c_out)
    piece(2.5, cross_part, head_pairs // 2, head_pairs)
    make_all(c_out)
    piece(0.2, fetch_x, c_kv)
    piece(1.0, memory_part)
    piece(0.2, fetch_g, c_kv)
    piece(0.5, back_through, v.gc_query, v.dn)
    make_all(c_kv)
    piece(0.2, fetch_x, c_query)
    piece(0.2, fetch_g, c_query)
    piece(1.6, residual_swap, v.d1, get_d1, gain(dec_gains, 1), 5, 8, v.gd_out, d_out)
    make_all(c_query)
    piece(0.2, fetch_x, d_out)
    piece(2.5, dec_part, 0, head_pairs // 2)
    piece(0.2, fetch_g, d_out)
    piece(2.5, dec_part, head_pairs // 2, head_pairs)
    make_all(d_out)
    piece(0.2, fetch_x, d_qkv)
    piece(1.4, back_through, v.gd_qkv, v.dn)
    piece(0.2, fetch_g, d_qkv)
    piece(1.0, dec_end)
    piece(1.2, start_feed, v.ge_down, v.ge_up, get_ge_up)
    make_all(d_qkv)
    piece(0.2, fetch_x, e_down)
    piece(0.2, fetch_g, e_down)
    piece(1.8, end_feed, v.ge_down, v.ge_up, e_up)
    make_all(e_down)
    piece(0.2, fetch_x, e_up)
    piece(1.8, back_through, v.ge_up, v.dn)
    piece(0.2, fetch_g, e_up)
    piece(1.6, residual_swap, v.d2, None, gain(enc_gains, 1), 1, 3, v.ge_out, e_out)
    make_all(e_up)
    piece(0.2, fetch_x, e_out)
    piece(3.0, enc_part, 0, head_pairs // 2)
    piece(0.2, fetch_g, e_out)
    piece(3.0, enc_part, head_pairs // 2, head_pairs)
    make_all(e_out)
    piece(0.2, fetch_x, e_qkv)
    piece(1.4, back_through, v.ge_qkv, v.dn)
    piece(0.2, fetch_g, e_qkv)
    small_after = len(work)
    piece(2.0, small_part)
    make_all(e_qkv)

    def take_step(kind, unit, at):
        if kind == 0:
            work[unit][2]()
        elif kind == 1:
            first_copy(unit).wait_recv()

            def body(i, carry):
                s.kept[unit, i] += s.taken[unit, i]
                return carry

            lax.fori_loop(0, n, body, 0)
            if unit - 1 in pairs:
                pair_copy(unit - 1).start()
            elif unit not in pairs:
                line_start(line_of(unit))
        elif kind == 7:
            pair_copy(unit).wait_recv()
            held = held_unit(unit)

            def body(i, carry):
                s.kept[held, i] += s.passed[unit + 1, i]
                return carry

            lax.fori_loop(0, n, body, 0)
            line_start(line_of(unit))
        elif kind == 8:
            pair_back(unit).wait_recv()
            for other in range(2):
                pair_last(unit, other).start()
                pair_result(unit, other).start()
        elif kind == 5 and unit in pairs:
            for other in range(2):
                pair_last(unit, other).wait_recv()
            for other in range(2):
                got_result(unit + other).start()
        elif kind == 2:
            line_hop(line_of(unit), at)
        elif kind == 3:
            line_end(line_of(unit))
            if rest_bits(unit):
                rest_copy(unit, 0).start()
            else:
                pair_back(unit).start()
        elif kind == 4:
            rest_copy(unit, at).wait_recv()
            before = s.kept[line_unit(unit), d] if at == 0 else s.rest_sum[unit, at - 1]
            s.rest_sum[unit, at] = before + s.rest_got[unit, at]
            if at + 1 < len(rest_bits(unit)):
                rest_copy(unit, at + 1).start()
            elif unit in pairs:
                pair_back(unit).start()
            else:
                last_copy(unit).start()
                own_result(unit).start()
        elif kind == 5:
            last_copy(unit).wait_recv()
            got_result(unit).start()
        else:
            small_step(at)

    plan = [(time, makes) for time, makes, unused in work]
    for step in step_order(plan, small_after, sides_of, pairs, n, bits):
        take_step(*step)

    for unit in range(units):
        if unit + rooms >= units:
            first_copy(unit).wait_send()
        got_result(unit).wait()
        if unit - 1 in pairs:
            continue
        line_sent(line_of(unit))
        for at in range(len(rest_bits(unit))):
            rest_copy(unit, at).wait_send()
        if unit in pairs:
            pair_copy(unit).wait_send()
            pair_back(unit).wait_send()
            for other in range(2):
                pair_last(unit, other).wait_send()
                pair_result(unit, other).wait()
        else:
            last_copy(unit).wait_send()
            own_result(unit).wait()
    small_swap.wait_send()
    for bit in range(bits):
        small_copy(bit).wait_send()
    line_sent(small_line)
    for wait in sent:
        wait()
    section_kept.wait()
    section_given.wait()


def run_backward(n, bits, xs, hbm, small_in, weights_out, g_columns, lanes, table_shape):
    length, width = hbm["d1"].shape
    half = width // 2
    block = width // (2 * n)
    first_units, unit_weight = [], []
    for at, x in enumerate(xs):
        first_units.append(len(unit_weight))
        unit_weight += [at] * max(x.shape[1] // half, g_columns[at] // width)
    units = len(unit_weight)
    pairs = set()
    if bits > 1:
        for at in PAIRED:
            count = len([unit for unit in unit_weight if unit == at])
            pairs.update(range(first_units[at], first_units[at] + count - 1, 2))
    sides_of = pick_sides(pairs, units)
    any_spec = pl.BlockSpec(memory_space=pl.ANY)
    vmem_spec = pl.BlockSpec(memory_space=pltpu.VMEM)
    section = jax.ShapeDtypeStruct((1, hbm["cot"].shape[0], 1, length, width), BF)
    grads = [jax.ShapeDtypeStruct(shape, BF) for shape in weights_out]
    outs = dict(
        enc_gains=(2, lanes), enc_shifts=(2, lanes), dec_gains=(3, lanes), dec_shifts=(3, lanes), table=table_shape
    )
    outs = {name: jax.ShapeDtypeStruct(shape, F32) for name, shape in outs.items()}
    outs.update(input_grads=section)
    land_g = [jax.ShapeDtypeStruct((length, columns), BF) for columns in g_columns[1:]]
    most = max(x.shape[1] for x in xs) // half
    small_rows = -(-(GAIN_ROWS + table_shape[1]) // 16) * 16
    dma = pltpu.SemaphoreType.DMA
    small_all = pltpu.VMEM((n, small_rows, 128), F32)
    low = pltpu.VMEM((length, width), BF)
    wide = pltpu.VMEM((length, width), F32)
    held = dict(
        cot=low, x_dec=low, gc_query=low, gc_out=low, gd_out=low, ge_out=low, ge_down=low, do=low,
        dx_dec=low, d2=wide, d1=wide, stream=wide, dn=wide,
        gd_up=pltpu.VMEM((length, most * width), BF), ge_up=pltpu.VMEM((length, most * width), BF),
        gd_qkv=pltpu.VMEM((length, 3 * width), BF), ge_qkv=pltpu.VMEM((length, 3 * width), BF),
        gc_kv=pltpu.VMEM((length, 2 * width), BF), p=pltpu.VMEM((HEADS, length, length), BF),
    )
    scratch = dict(
        stream_w=pltpu.VMEM((3, 256, most * width), BF),
        x_stage=pltpu.VMEM((most, 2 * length, half), BF),
        g_stage=pltpu.VMEM((length, most * width), BF),
        factor=pltpu.VMEM((most, half, 2 * length), BF),
        kept=pltpu.VMEM((units, n, block, half), BF),
        given=pltpu.VMEM((10, n, block, half), BF),
        taken=pltpu.VMEM((units, n, block, half), BF),
        passed=pltpu.VMEM((units, n + 1, block, half), BF),
        rest_got=pltpu.VMEM((units, bits - 1, block, half), BF),
        rest_sum=pltpu.VMEM((units, bits - 1, block, half), BF),
        last_got=pltpu.VMEM((units, block, half), BF),
        sums=pltpu.VMEM((GAIN_ROWS, width), F32), diag=pltpu.VMEM((16, 2 * length), F32),
        flip=pltpu.VMEM((length, length), BF), small=pltpu.VMEM((2 * n, small_rows, 128), F32),
        small_kept=small_all, small_core=small_all,
        small_held=pltpu.VMEM((bits, n, small_rows, 128), F32),
        small_group=pltpu.VMEM((bits, n, small_rows, 128), F32),
        small_passed=pltpu.VMEM((n + 1, small_rows, 128), F32),
        load_sems=dma((15,)), stream_sems=dma((3, most)), stage_sems=dma((most + 1,)),
        swap_sent=dma((len(xs),)), swap_got=dma((len(xs),)),
        small_sent=dma((1 + bits,)), small_got=dma((1 + bits,)), small_line=dma((4,)),
        section_kept=dma, section_sent=dma, section_got=dma,
        first_sent=dma((units,)), first_got=dma((units,)), line_sems=dma((units, 4)), pair_sems=dma((units, 2)),
        rest_sems=dma((units, bits - 1, 2)), last_sems=dma((units, 2)), result_sems=dma((units, 2)),
    )
    groups = [
        len(xs), list(hbm), list(small_in), len(grads), list(outs), len(land_g), list(held), list(scratch)
    ]
    out_specs = [any_spec] * len(grads) + [vmem_spec] * (len(outs) - 1) + [any_spec] * (1 + len(land_g))
    results = pl.pallas_call(
        functools.partial(backward_kernel, (n, bits, first_units, unit_weight, pairs, sides_of), groups),
        out_shape=grads + list(outs.values()) + land_g,
        in_specs=[any_spec] * (len(xs) + len(hbm)) + [vmem_spec] * len(small_in),
        out_specs=out_specs,
        scratch_shapes=list(held.values()) + list(scratch.values()),
        compiler_params=pltpu.CompilerParams(
            collective_id=0, has_side_effects=True, vmem_limit_bytes=63 * 1024 * 1024
        ),
        name="backward",
    )(*xs, *hbm.values(), *small_in.values())
    return results[: len(grads)], dict(zip(outs, results[len(grads) :]))


def finish_kernel(counts, *refs):
    wides, total = counts
    sources, targets = refs[:total], refs[total : 2 * total]
    held, widened, sems = refs[2 * total : 3 * total], refs[3 * total : -1], refs[-1]
    loads = [pltpu.make_async_copy(sources[i], held[i], sems.at[0, i]) for i in range(total)]
    for copy in loads:
        copy.start()
    stores = []
    for i in range(total):
        loads[i].wait()
        if i < wides:
            rows = held[i].shape[0]
            for at in range(0, rows, 16):
                widened[i][at : at + 16, :] = held[i][at : at + 16, :].astype(F32)
        stores.append(pltpu.make_async_copy(widened[i] if i < wides else held[i], targets[i], sems.at[1, i]))
        stores[i].start()
    for copy in stores:
        copy.wait()


def run_finish(grads, plain):
    any_spec = pl.BlockSpec(memory_space=pl.ANY)
    arrays = list(grads) + list(plain)
    shapes = [jax.ShapeDtypeStruct(a.shape, F32) for a in grads]
    shapes += [jax.ShapeDtypeStruct(a.shape, a.dtype) for a in plain]
    scratch = [pltpu.VMEM(a.shape, a.dtype) for a in arrays] + [pltpu.VMEM(a.shape, F32) for a in grads]
    results = pl.pallas_call(
        functools.partial(finish_kernel, (len(grads), len(arrays))),
        out_shape=shapes,
        in_specs=[any_spec] * len(arrays),
        out_specs=[any_spec] * len(arrays),
        scratch_shapes=scratch + [pltpu.SemaphoreType.DMA((2, len(arrays)))],
        compiler_params=pltpu.CompilerParams(vmem_limit_bytes=63 * 1024 * 1024),
        name="finish",
    )(*arrays)
    return results[: len(grads)], results[len(grads) :]


def shards(
    section_inputs, cotangent, encoder_segments, decoder_segments, encoder_valid, decoder_valid,
    position_buckets, encoder_gains, encoder_shifts, encoder_qkv, encoder_out, encoder_up, encoder_down,
    position_table, decoder_gains, decoder_shifts, decoder_qkv, decoder_out, cross_query, cross_keyvalue,
    cross_out, decoder_up, decoder_down,
):
    width = section_inputs.shape[-1]
    dp = lax.axis_size("dp")
    bits = lax.axis_size("group").bit_length() - 1
    blocks = lax.axis_size("pipe") * dp
    weights = dict(
        e_qkv=encoder_qkv, e_out=encoder_out, e_up=encoder_up, e_down=encoder_down,
        d_qkv=decoder_qkv, d_out=decoder_out, c_query=cross_query, c_kv=cross_keyvalue,
        c_out=cross_out, d_up=decoder_up, d_down=decoder_down,
    )

    small_in = dict(
        enc_seg=encoder_segments, dec_seg=decoder_segments, enc_valid=encoder_valid, dec_valid=decoder_valid,
        buckets=position_buckets.reshape(1, -1), enc_gains=encoder_gains, enc_shifts=encoder_shifts,
        dec_gains=decoder_gains, dec_shifts=decoder_shifts, table=position_table.T,
    )
    r = run_forward(section_inputs, small_in, weights)
    f = SimpleNamespace(**r)
    xs = [f.xd_down, f.xd_up, f.xc_out, f.memory_cut, f.xc_query, f.xd_out, f.xd_qkv, f.xe_down, f.xe_up, f.xe_out, f.xe_qkv]
    order = [decoder_down, decoder_up, cross_out, cross_keyvalue, cross_query, decoder_out, decoder_qkv,
             encoder_down, encoder_up, encoder_out, encoder_qkv]
    cut = [(w.shape[0] // blocks, w.shape[1]) for w in order]
    kept = dict(
        gd_up=f.gd_up, d2=f.d2, p_cross=f.p_cross, gc_query=f.gc_query, gc_kv=f.gc_kv, d1=f.d1, p_dec=f.p_dec,
        gd_qkv=f.gd_qkv, ge_up=f.ge_up, x1=f.x1, p_enc=f.p_enc, ge_qkv=f.ge_qkv,
    )
    hbm = dict(kept, cot=cotangent, x_enc=f.x_enc, x_dec=f.x_dec, **weights)
    small_back = dict(buckets=small_in["buckets"], enc_gains=encoder_gains, dec_gains=decoder_gains)
    table_shape = (position_table.shape[1], position_table.shape[0] // blocks)
    columns = [w.shape[1] for w in order]
    grads, rest = run_backward(dp, bits, xs, hbm, small_back, cut, columns, width // blocks, table_shape)
    rest.update(outputs=f.outputs)
    grads, plain = run_finish(grads, list(rest.values()))
    s = SimpleNamespace(**dict(zip(rest, plain)))
    d_down, d_up, c_out, c_kv, c_query, d_out, d_qkv, e_down, e_up, e_out, e_qkv = grads
    return (
        s.outputs, s.input_grads, s.enc_gains, s.enc_shifts, e_qkv, e_out, e_up, e_down, s.table.T,
        s.dec_gains, s.dec_shifts, d_qkv, d_out, c_query, c_kv, c_out, d_up, d_down,
    )


def solution(mesh):
    section = P("pipe", None, ("dp", "group"), None, None)
    rows = P(None, ("dp", "group"), None)
    cut_rows = P(("pipe", "dp"), None)
    cut_lanes = P(None, ("pipe", "dp"))
    return jax.shard_map(
        shards,
        mesh=mesh,
        in_specs=(section, P(None, ("dp", "group"), None, None), rows, rows, rows, rows) + (P(),) * 17,
        out_specs=(section, section, cut_lanes, cut_lanes) + (cut_rows,) * 5 + (cut_lanes, cut_lanes) + (cut_rows,) * 7,
        check_vma=False,
    )
```
